32 devices in a mesh: dp: 2 (over x), sp: 4 (over z), tp: 4 (over y, core).
Axes of the slice: x: 2, y: 2, z: 4, core: 2. Of those that a mesh axis runs over, the one named last changes fastest.
Arguments:
- block_in: bfloat16 [8, 1024, 2048], P('dp', ('sp', 'tp')), may hold values from -6 to 6
- cotangent: bfloat16 [8, 1024, 2048], P('dp', ('sp', 'tp')), may hold values from -6 to 6
- qkv_weight: float32 [8, 2048, 384], P('tp', ('dp', 'sp')), may hold values from -0.125 to 0.125
- proj_weight: float32 [8, 256, 2048], P('tp', ('dp', 'sp')), may hold values from -1 to 1
- feed_weight: float32 [2, 2048, 8192], P(None, ('dp', 'sp'), 'tp'), may hold values from -0.125 to 0.125
- down_weight: float32 [32, 256, 2048], P('tp', ('dp', 'sp')), may hold values from -0.0625 to 0.0625
- norm_gains: float32 [2, 2048], P(None, ('dp', 'sp')), may hold values from 0.25 to 1.75
- qkv_first: float32 [8, 2048, 384], P('tp', ('dp', 'sp')), may hold values from -80 to 80
- proj_first: float32 [8, 256, 2048], P('tp', ('dp', 'sp')), may hold values from -6 to 6
- feed_first: float32 [2, 2048, 8192], P(None, ('dp', 'sp'), 'tp'), may hold values from -16 to 16
- down_first: float32 [32, 256, 2048], P('tp', ('dp', 'sp')), may hold values from -32 to 32
- gains_first: float32 [2, 2048], P(None, ('dp', 'sp')), may hold values from -64 to 64
- qkv_second: float32 [8, 2048, 384], P('tp', ('dp', 'sp')), may hold values from 573.44 to 7372.8
- proj_second: float32 [8, 256, 2048], P('tp', ('dp', 'sp')), may hold values from 4 to 51.2
- feed_second: float32 [2, 2048, 8192], P(None, ('dp', 'sp'), 'tp'), may hold values from 22.1184 to 294.912
- down_second: float32 [32, 256, 2048], P('tp', ('dp', 'sp')), may hold values from 90.112 to 1179.648
- gains_second: float32 [2, 2048], P(None, ('dp', 'sp')), may hold values from 352.256 to 4751.36
Outputs:
- block_out: float32 [8, 1024, 2048], P('dp', ('sp', 'tp'))
- input_grad: float32 [8, 1024, 2048], P('dp', ('sp', 'tp'))
- qkv_grad: float32 [8, 2048, 384], P('tp', ('dp', 'sp'))
- proj_grad: float32 [8, 256, 2048], P('tp', ('dp', 'sp'))
- feed_grad: float32 [2, 2048, 8192], P(None, ('dp', 'sp'), 'tp')
- down_grad: float32 [32, 256, 2048], P('tp', ('dp', 'sp'))
- gains_grad: float32 [2, 2048], P(None, ('dp', 'sp'))
- qkv_new: float32 [8, 2048, 384], P('tp', ('dp', 'sp'))
- proj_new: float32 [8, 256, 2048], P('tp', ('dp', 'sp'))
- feed_new: float32 [2, 2048, 8192], P(None, ('dp', 'sp'), 'tp')
- down_new: float32 [32, 256, 2048], P('tp', ('dp', 'sp'))
- gains_new: float32 [2, 2048], P(None, ('dp', 'sp'))
- qkv_first_new: float32 [8, 2048, 384], P('tp', ('dp', 'sp'))
- proj_first_new: float32 [8, 256, 2048], P('tp', ('dp', 'sp'))
- feed_first_new: float32 [2, 2048, 8192], P(None, ('dp', 'sp'), 'tp')
- down_first_new: float32 [32, 256, 2048], P('tp', ('dp', 'sp'))
- gains_first_new: float32 [2, 2048], P(None, ('dp', 'sp'))
- qkv_second_new: float32 [8, 2048, 384], P('tp', ('dp', 'sp'))
- proj_second_new: float32 [8, 256, 2048], P('tp', ('dp', 'sp'))
- feed_second_new: float32 [2, 2048, 8192], P(None, ('dp', 'sp'), 'tp')
- down_second_new: float32 [32, 256, 2048], P('tp', ('dp', 'sp'))
- gains_second_new: float32 [2, 2048], P(None, ('dp', 'sp'))
The draws below stay inside these ranges and needn't reach their ends.
All inputs are finite; a program needn't handle non-finite values.
Results may differ from the reference program's by a relative error of at most 0.014.
The reference program's roundings to bfloat16 on the way count: a program that leaves them out, or rounds other values in their place, can miss the bound.
Values may be sent and summed in bfloat16 or wider, within the bound.
No kernel may reach another device: no remote copies, remote signals or barrier semaphores. Data moves between devices by JAX's collectives and lax.ppermute only.
A program may use at most 256 MiB of HBM per device.

```python
import math
import jax
import jax.numpy as jnp
from jax import lax

D = 2048
KVH = 8
HD = 64
FF = 8192
QPK = 4
RB = 256
SEQ = 1024
STEP = 10
SEQS = 8
TOKENS = 8192


def levels(key, dims, split, low, largest):
    def one(dim, blocks):
        draws = jax.random.uniform(jax.random.fold_in(jax.random.fold_in(key, 6), dim), (blocks,), jnp.float32, low / len(split), largest / len(split))
        return jnp.repeat(jnp.exp(draws), dims[dim] // blocks).reshape((-1,) + (1,) * (len(dims) - dim - 1))

    factor_of = one(*split[0])
    for cut in split[1:]:
        factor_of = factor_of * one(*cut)
    return factor_of


def gaussian(key, extent, width, bound, split=(), kind=jnp.bfloat16):
    level = levels(key, extent, split, -0.22, 0.18) if split else 1.0
    array = jax.random.normal(key, extent, jnp.float32) * width * level
    return jnp.minimum(jnp.maximum(array, -bound), bound).astype(kind)


def setup_inputs(seed: int = 0) -> dict:
    splits = jax.random.split(jax.random.key(seed), 18)
    block_in = gaussian(splits[0], (SEQS, SEQ, D), 1.0, 6.0, ((0, 2), (1, 16)))
    cotangent = gaussian(splits[1], (SEQS, SEQ, D), 1.0, 6.0, ((0, 2), (1, 16)))
    qkv_weight = gaussian(splits[2], (KVH, D, (QPK + 2) * HD), D ** -0.5, 0.125, ((0, 4), (1, 8)), jnp.float32)
    proj_weight = gaussian(splits[3], (KVH, QPK * HD, D), (16 * D // SEQ) ** -0.5, 1.0, ((0, 4), (1, 8)), jnp.float32)
    feed_weight = gaussian(splits[4], (2, D, FF), D ** -0.5, 0.125, ((1, 8), (2, 4)), jnp.float32)
    down_weight = gaussian(splits[5], (FF // RB, RB, D), FF ** -0.5, 0.0625, ((0, 4), (1, 8)), jnp.float32)
    norm_gains = jnp.clip(1.0 + 0.15 * jax.random.normal(splits[6], (2, D), jnp.float32), 0.25, 1.75)
    qkv_first = gaussian(splits[7], (KVH, D, (QPK + 2) * HD), (0.16 * TOKENS ** 0.5), 80.0, ((0, 4), (1, 8)), jnp.float32)
    proj_first = gaussian(splits[8], (KVH, QPK * HD, D), (0.44 * SEQS ** 0.5), 6.0, ((0, 4), (1, 8)), jnp.float32)
    feed_first = gaussian(splits[9], (2, D, FF), (0.033 * TOKENS ** 0.5), 16.0, ((1, 8), (2, 4)), jnp.float32)
    down_first = gaussian(splits[10], (FF // RB, RB, D), (0.066 * TOKENS ** 0.5), 32.0, ((0, 4), (1, 8)), jnp.float32)
    gains_first = gaussian(splits[11], (2, D), (0.13 * TOKENS ** 0.5), 64.0, ((1, 8),), jnp.float32)
    qkv_second = jnp.clip(jnp.exp(math.log(7372.8) - 2.5538995 * jax.random.uniform(splits[12], (KVH, D, (QPK + 2) * HD), jnp.float32) ** levels(splits[12], (KVH, D, (QPK + 2) * HD), ((0, 4), (1, 8)), -0.2, 0.2)), 573.44, 7372.8)
    proj_second = jnp.clip(jnp.exp(math.log(51.2) - 2.5494452 * jax.random.uniform(splits[13], (KVH, QPK * HD, D), jnp.float32) ** levels(splits[13], (KVH, QPK * HD, D), ((0, 4), (1, 8)), -0.2, 0.2)), 4.0, 51.2)
    feed_second = jnp.clip(jnp.exp(math.log(294.912) - 2.5902671 * jax.random.uniform(splits[14], (2, D, FF), jnp.float32) ** levels(splits[14], (2, D, FF), ((1, 8), (2, 4)), -0.2, 0.2)), 22.1184, 294.912)
    down_second = jnp.clip(jnp.exp(math.log(1179.648) - 2.571918 * jax.random.uniform(splits[15], (FF // RB, RB, D), jnp.float32) ** levels(splits[15], (FF // RB, RB, D), ((0, 4), (1, 8)), -0.2, 0.2)), 90.112, 1179.648)
    gains_second = jnp.clip(jnp.exp(math.log(4751.36) - 2.6018279 * jax.random.uniform(splits[16], (2, D), jnp.float32) ** levels(splits[16], (2, D), ((1, 8),), -0.2, 0.2)), 352.256, 4751.36)
    return {"block_in": block_in, "cotangent": cotangent, "qkv_weight": qkv_weight, "proj_weight": proj_weight, "feed_weight": feed_weight, "down_weight": down_weight, "norm_gains": norm_gains, "qkv_first": qkv_first, "proj_first": proj_first, "feed_first": feed_first, "down_first": down_first, "gains_first": gains_first, "qkv_second": qkv_second, "proj_second": proj_second, "feed_second": feed_second, "down_second": down_second, "gains_second": gains_second}


NORM_EPSILON = 1e-05
ROPE_BASE = 500000.0
MASKED = -1e+30
BETA_ONE = 0.9
BETA_TWO = 0.95
ADAM_EPSILON = 1e-08
WEIGHT_DECAY = 0.1
QKV_RATE = 0.05
PROJ_RATE = 0.4
FEED_RATE = 0.05
DOWN_RATE = 0.03
GAIN_RATE = 0.5
HIGHEST = lax.Precision.HIGHEST

@jax.custom_vjp
def low(v):
    return lax.optimization_barrier(v.astype(jnp.bfloat16)).astype(jnp.float32)

@jax.custom_vjp
def low_back(v):
    return v

def low_keep(v):
    return (low(v), None)

def low_pass(kept, grad):
    return (grad,)

def back_keep(v):
    return (v, None)

def back_low(kept, grad):
    return (low(grad),)
low.defvjp(low_keep, low_pass)
low_back.defvjp(back_keep, back_low)

def rms_norm(activations, gain_row):
    mean_square = lax.optimization_barrier(jnp.mean(activations * activations, axis=-1, keepdims=True))
    return activations * lax.rsqrt(mean_square + NORM_EPSILON) * gain_row

def rope_tables(positions):
    half_width = HD // 2
    frequency = ROPE_BASE ** (-(jnp.arange(half_width, dtype=jnp.float32) * 2.0 / HD))
    angles = positions.astype(jnp.float32)[:, None] * frequency[None, :]
    return (jnp.cos(angles), jnp.sin(angles))

def rotate(values, cosine_table, sine_table):
    half_width = values.shape[-1] // 2
    table_shape = (values.shape[0],) + (1,) * (values.ndim - 2) + (half_width,)
    cosine_part = cosine_table.reshape(table_shape)
    sine_part = sine_table.reshape(table_shape)
    first_half = values[..., :half_width]
    second_half = values[..., half_width:]
    return jnp.concatenate([first_half * cosine_part - second_half * sine_part, second_half * cosine_part + first_half * sine_part], axis=-1)

def matmul(left, right):
    return jnp.dot(left, right, precision=HIGHEST, preferred_element_type=jnp.float32)

def sequence_forward(sequence_rows, qkv, proj, feed, down, gain_values, cosine_table, sine_table, allowed):
    query_width = QPK * HD
    normed_one = low(rms_norm(sequence_rows, gain_values[0]))
    projected = jnp.einsum('ld,gdc->lgc', normed_one, qkv, precision=HIGHEST)
    queries = low_back(projected[..., :query_width]).reshape(SEQ, KVH, QPK, HD)
    queries = low(rotate(queries, cosine_table, sine_table))
    key_rows = low(rotate(low_back(projected[..., query_width:query_width + HD]), cosine_table, sine_table))
    value_rows = low(low_back(projected[..., query_width + HD:]))
    scores = jnp.einsum('qgnd,kgd->gqnk', queries, key_rows, precision=HIGHEST)
    scores = low_back(scores * HD ** (-0.5))
    scores = jnp.where(allowed[None, :, None, :], scores, MASKED)
    row_peak = lax.optimization_barrier(jnp.max(scores, axis=-1, keepdims=True))
    weights = jnp.exp(scores - row_peak)
    softmax_low = low(weights / lax.optimization_barrier(jnp.sum(weights, axis=-1, keepdims=True)))
    context = jnp.einsum('gqnk,kgd->qgnd', softmax_low, value_rows, precision=HIGHEST)
    context = low(low_back(context)).reshape(SEQ, KVH * query_width)
    attention = low_back(matmul(context, proj.reshape(KVH * query_width, D)))
    hidden_one = sequence_rows + attention
    normed_two = low(rms_norm(hidden_one, gain_values[1]))
    gate_rows = low_back(matmul(normed_two, feed[0]))
    up_rows = low_back(matmul(normed_two, feed[1]))
    hidden = low(gate_rows * jax.nn.sigmoid(gate_rows) * up_rows)
    return hidden_one + matmul(hidden, down.reshape(FF, D))

def rounded_copy(master):
    return master.astype(jnp.bfloat16).astype(jnp.float32)

def adamw(param, grad, first, second, rate, decay):
    first_new = BETA_ONE * first + (1.0 - BETA_ONE) * grad
    second_new = BETA_TWO * second + (1.0 - BETA_TWO) * grad * grad
    first_hat = first_new / (1.0 - BETA_ONE ** STEP)
    second_hat = second_new / (1.0 - BETA_TWO ** STEP)
    param_new = param - rate * (first_hat / (jnp.sqrt(second_hat) + ADAM_EPSILON) + decay * param)
    return (param_new, first_new, second_new)

def reference(block_in, cotangent, qkv_weight, proj_weight, feed_weight, down_weight, norm_gains, qkv_first, proj_first, feed_first, down_first, gains_first, qkv_second, proj_second, feed_second, down_second, gains_second):
    positions = jnp.arange(SEQ)
    cosine_table, sine_table = rope_tables(positions)
    allowed = positions[None, :] <= positions[:, None]

    def forward(inputs, qkv, proj, feed, down, gain_values):

        def one_sequence(sequence_rows):
            return sequence_forward(sequence_rows, qkv, proj, feed, down, gain_values, cosine_table, sine_table, allowed)
        return lax.map(jax.checkpoint(one_sequence), inputs)
    block_out, pullback = jax.vjp(forward, block_in.astype(jnp.float32), rounded_copy(qkv_weight), rounded_copy(proj_weight), rounded_copy(feed_weight), rounded_copy(down_weight), rounded_copy(norm_gains))
    input_grad, qkv_grad, proj_grad, feed_grad, down_grad, gains_grad = pullback(cotangent.astype(jnp.float32))
    qkv_new, qkv_first_new, qkv_second_new = adamw(qkv_weight, qkv_grad, qkv_first, qkv_second, QKV_RATE, WEIGHT_DECAY)
    proj_new, proj_first_new, proj_second_new = adamw(proj_weight, proj_grad, proj_first, proj_second, PROJ_RATE, WEIGHT_DECAY)
    feed_new, feed_first_new, feed_second_new = adamw(feed_weight, feed_grad, feed_first, feed_second, FEED_RATE, WEIGHT_DECAY)
    down_new, down_first_new, down_second_new = adamw(down_weight, down_grad, down_first, down_second, DOWN_RATE, WEIGHT_DECAY)
    gains_new, gains_first_new, gains_second_new = adamw(norm_gains, gains_grad, gains_first, gains_second, GAIN_RATE, 0.0)
    return (block_out, input_grad, qkv_grad, proj_grad, feed_grad, down_grad, gains_grad, qkv_new, proj_new, feed_new, down_new, gains_new, qkv_first_new, proj_first_new, feed_first_new, down_first_new, gains_first_new, qkv_second_new, proj_second_new, feed_second_new, down_second_new, gains_second_new)
```

```python
import functools

import jax
import jax.numpy as jnp
from jax import lax
from jax.experimental import pallas as pl
from jax.experimental.pallas import tpu as pltpu
from jax.sharding import PartitionSpec as P

HD = 64
QPK = 4
STEP = 10
LANES = 128
VMEM_LIMIT = 56 * 1024 * 1024


NORM_EPSILON = 1e-05
ROPE_BASE = 500000.0
MASKED = -1e30
BETA_ONE = 0.9
BETA_TWO = 0.95
ADAM_EPSILON = 1e-08
WEIGHT_DECAY = 0.1
QKV_RATE = 0.05
PROJ_RATE = 0.4
FEED_RATE = 0.05
DOWN_RATE = 0.03
GAIN_RATE = 0.5

BF = jnp.bfloat16
F32 = jnp.float32


def after(value, *earlier):
    return lax.optimization_barrier((value,) + earlier)[0]


def swap(value, axis, mask):
    return lax.ppermute(value, axis, [(i, i ^ mask) for i in range(lax.axis_size(axis))])


def pick(value, index, axis):
    return lax.dynamic_index_in_dim(value, index, axis, keepdims=False)


def dot(left, right, dims):
    return lax.dot_general(left, right, ((dims[0], dims[1]), ((), ())), preferred_element_type=F32)


def mm(left, right):
    return dot(left, right, ((1,), (0,)))


def mm_nt(left, right):
    return dot(left, right, ((1,), (1,)))


def mm_tn(left, right):
    return dot(left, right, ((0,), (0,)))


def turn(block, cosine, sine):
    lane = lax.broadcasted_iota(jnp.int32, block.shape, 1)
    ahead = pltpu.roll(block, LANES - HD // 2, 1)
    behind = pltpu.roll(block, HD // 2, 1)
    return block * cosine + jnp.where(lane % HD < HD // 2, ahead, behind) * sine

def key_tables(cosine, sine):
    lane = lax.broadcasted_iota(jnp.int32, cosine.shape, 1)
    return jnp.where(lane < HD, cosine, 1.0), jnp.where(lane < HD, sine, 0.0)

def attend_kernel(tile, p_ref, cos_ref, sin_ref, qkv_ref, ctx_ref, log_ref, q_s, k_s, vt_s, c_s):
    length = p_ref.shape[0]
    cosine, sine = cos_ref[...], sin_ref[...]
    for b in range(QPK // 2):
        block = turn(p_ref[:, b * LANES : (b + 1) * LANES], cosine, sine).astype(BF) * BF(HD ** -0.5)
        qkv_ref[:, b * LANES : (b + 1) * LANES] = block
        q_s[2 * b] = block[:, :HD]
        q_s[2 * b + 1] = block[:, HD:]
    k_cos, k_sin = key_tables(cosine, sine)
    block = turn(p_ref[:, QPK * HD :], k_cos, k_sin)
    qkv_ref[:, QPK * HD :] = block.astype(BF)
    k_s[...] = block[:, :HD].astype(BF)
    vt_s[...] = jnp.transpose(block)[HD:].astype(BF)
    keep = lax.broadcasted_iota(jnp.int32, (tile, tile), 0) <= lax.broadcasted_iota(jnp.int32, (tile, tile), 1)

    def head(n, carry):
        for t in range(length // tile):
            before, here = t * tile, slice(t * tile, (t + 1) * tile)
            q = q_s[n, here, :]
            s_here = jnp.where(keep, mm_nt(k_s[here, :], q), MASKED)
            peak = jnp.max(s_here, axis=0, keepdims=True)
            if t:
                s_before = mm_nt(k_s[:before, :], q)
                peak = jnp.maximum(peak, jnp.max(s_before, axis=0, keepdims=True))
            e_here = jnp.exp(s_here - peak)
            total = jnp.sum(e_here, axis=0, keepdims=True)
            if t:
                e_before = jnp.exp(s_before - peak)
                total = total + jnp.sum(e_before, axis=0, keepdims=True)
            scale = 1.0 / total
            out = mm(vt_s[:, here], (e_here * scale).astype(BF))
            if t:
                out = out + mm(vt_s[:, :before], (e_before * scale).astype(BF))
            c_s[pl.ds(pl.multiple_of(n * HD, HD), HD), here] = out
            log_ref[0, pl.ds(n, 1), here] = peak + jnp.log(total)
        return carry

    lax.fori_loop(0, QPK, head, 0)
    ctx_ref[...] = jnp.transpose(c_s[...]).astype(BF)

def attend(projected, cosine, sine, groups, tile=256):
    length, columns = projected.shape[0], projected.shape[1] // groups
    qw = QPK * HD
    table = pl.BlockSpec((length, LANES), lambda g: (0, 0))
    return pl.pallas_call(
        functools.partial(attend_kernel, tile),
        grid=(groups,),
        in_specs=[pl.BlockSpec((length, columns), lambda g: (0, g)), table, table],
        out_specs=[
            pl.BlockSpec((length, columns), lambda g: (0, g)),
            pl.BlockSpec((length, qw), lambda g: (0, g)),
            pl.BlockSpec((1, QPK, length), lambda g: (g, 0, 0)),
        ],
        out_shape=[
            jax.ShapeDtypeStruct((length, groups * columns), BF),
            jax.ShapeDtypeStruct((length, groups * qw), BF),
            jax.ShapeDtypeStruct((groups, QPK, length), F32),
        ],
        scratch_shapes=[
            pltpu.VMEM((QPK, length, HD), BF),
            pltpu.VMEM((length, HD), BF),
            pltpu.VMEM((HD, length), BF),
            pltpu.VMEM((qw, length), F32),
        ],
        compiler_params=pltpu.CompilerParams(vmem_limit_bytes=VMEM_LIMIT),
        cost_estimate=pl.CostEstimate(flops=groups * QPK * length * length * 4 * HD, bytes_accessed=length * columns * groups * 8, transcendentals=0),
        name="attend",
    )(projected, cosine, sine)

def attend_back_kernel(tile, qkv_ref, grad_ref, log_ref, cos_ref, sin_ref, out_ref, q_s, k_s, v_s, kt_s, g_s, dk_s, dv_s, dq_s):
    length = qkv_ref.shape[0]
    for b in range(QPK // 2):
        lanes = slice(b * LANES, (b + 1) * LANES)
        block, grad = qkv_ref[:, lanes], grad_ref[:, lanes]
        q_s[2 * b], q_s[2 * b + 1] = block[:, :HD], block[:, HD:]
        g_s[2 * b], g_s[2 * b + 1] = grad[:, :HD], grad[:, HD:]
    block = qkv_ref[:, QPK * HD :]
    k_s[...] = block[:, :HD]
    v_s[...] = block[:, HD:]
    kt_s[...] = jnp.transpose(block.astype(F32))[:HD].astype(BF)
    dk_s[...] = jnp.zeros_like(dk_s)
    dv_s[...] = jnp.zeros_like(dv_s)
    keep = lax.broadcasted_iota(jnp.int32, (tile, tile), 0) <= lax.broadcasted_iota(jnp.int32, (tile, tile), 1)

    def head(n, carry):
        for t in range(length // tile):
            before, here = t * tile, slice(t * tile, (t + 1) * tile)
            upto = slice(0, (t + 1) * tile)
            q, g = q_s[n, here, :], g_s[n, here, :]
            log = log_ref[0, pl.ds(n, 1), here]
            a_here = jnp.exp(jnp.where(keep, mm_nt(k_s[here, :], q), MASKED) - log)
            d_here = mm_nt(v_s[here, :], g)
            inner = jnp.sum(a_here * d_here, axis=0, keepdims=True)
            if t:
                a_before = jnp.exp(mm_nt(k_s[:before, :], q) - log)
                d_before = mm_nt(v_s[:before, :], g)
                inner = inner + jnp.sum(a_before * d_before, axis=0, keepdims=True)
            s_here = (a_here * (d_here - inner)).astype(BF)
            dq = mm(kt_s[:, here], s_here)
            dk_s[here, :] += mm(s_here, q)
            dv_s[here, :] += mm(a_here.astype(BF), g)
            if t:
                s_before = (a_before * (d_before - inner)).astype(BF)
                dq = dq + mm(kt_s[:, :before], s_before)
                dk_s[:before, :] += mm(s_before, q)
                dv_s[:before, :] += mm(a_before.astype(BF), g)
            dq_s[pl.ds(pl.multiple_of(n * HD, HD), HD), here] = dq * HD ** -0.5
        return carry

    lax.fori_loop(0, QPK, head, 0)
    cosine, sine = cos_ref[...], sin_ref[...]
    grad = jnp.transpose(dq_s[...])
    for b in range(QPK // 2):
        lanes = slice(b * LANES, (b + 1) * LANES)
        out_ref[:, lanes] = turn(grad[:, lanes], cosine, -sine).astype(BF)
    k_cos, k_sin = key_tables(cosine, sine)
    block = jnp.concatenate([dk_s[...], dv_s[...]], axis=1)
    out_ref[:, QPK * HD :] = turn(block, k_cos, -k_sin).astype(BF)

def attend_back(qkv, grad, log, cosine, sine, groups, tile=256):
    length, columns = qkv.shape[0], qkv.shape[1] // groups
    qw = QPK * HD
    table = pl.BlockSpec((length, LANES), lambda g: (0, 0))
    return pl.pallas_call(
        functools.partial(attend_back_kernel, tile),
        grid=(groups,),
        in_specs=[
            pl.BlockSpec((length, columns), lambda g: (0, g)),
            pl.BlockSpec((length, qw), lambda g: (0, g)),
            pl.BlockSpec((1, QPK, length), lambda g: (g, 0, 0)),
            table, table],
        out_specs=pl.BlockSpec((length, columns), lambda g: (0, g)),
        out_shape=jax.ShapeDtypeStruct((length, groups * columns), BF),
        scratch_shapes=[
            pltpu.VMEM((QPK, length, HD), BF),
            pltpu.VMEM((length, HD), BF),
            pltpu.VMEM((length, HD), BF),
            pltpu.VMEM((HD, length), BF),
            pltpu.VMEM((QPK, length, HD), BF),
            pltpu.VMEM((length, HD), F32),
            pltpu.VMEM((length, HD), F32),
            pltpu.VMEM((qw, length), F32),
        ],
        compiler_params=pltpu.CompilerParams(vmem_limit_bytes=VMEM_LIMIT),
        cost_estimate=pl.CostEstimate(flops=groups * QPK * length * length * 10 * HD, bytes_accessed=length * columns * groups * 8, transcendentals=0),
        name="attend_back",
    )(qkv, grad, log, cosine, sine)

def tables(length):
    half = HD // 2
    freq = ROPE_BASE ** (-(jnp.arange(half, dtype=F32) * 2.0 / HD))
    ang = jnp.arange(length).astype(F32)[:, None] * freq[None, :]
    c, s = jnp.cos(ang), jnp.sin(ang)
    return jnp.concatenate([c, c, c, c], 1), jnp.concatenate([-s, s, -s, s], 1)

def gate_kernel(n_ref, g_ref, u_ref, hid_ref, a_ref, b_ref):
    rows = n_ref[...]
    gate = mm(rows, g_ref[...])
    up = mm(rows, u_ref[...])
    s = jax.nn.sigmoid(gate)
    act = gate * s
    hid_ref[...] = (act * up).astype(BF)
    a_ref[...] = act
    b_ref[...] = up * s * (1.0 + gate * (1.0 - s))

def gate_up(rows, gate_w, up_w, tm=512, tf=256):
    m, k = rows.shape; f = gate_w.shape[1]
    o = pl.BlockSpec((tm, tf), lambda i, j: (i, j))
    return pl.pallas_call(gate_kernel, grid=(m // tm, f // tf),
        in_specs=[pl.BlockSpec((tm, k), lambda i, j: (i, 0)), pl.BlockSpec((k, tf), lambda i, j: (0, j)), pl.BlockSpec((k, tf), lambda i, j: (0, j))],
        out_specs=[o, o, o],
        out_shape=[jax.ShapeDtypeStruct((m, f), BF), jax.ShapeDtypeStruct((m, f), F32), jax.ShapeDtypeStruct((m, f), F32)],
        compiler_params=pltpu.CompilerParams(vmem_limit_bytes=VMEM_LIMIT),
        cost_estimate=pl.CostEstimate(flops=4*m*k*f, bytes_accessed=2*m*k+4*k*f+10*m*f, transcendentals=0),
        name="gate_up")(rows, gate_w, up_w)

def ffn_back_kernel(tf, dy_ref, a_ref, b_ref, d_ref, g_ref, u_ref, *refs):
    dg_ref, du_ref, dn_ref = refs[-3:]
    dy = dy_ref[...]
    for j in range(d_ref.shape[0] // tf):
        c = slice(j * tf, (j + 1) * tf)
        dh = mm_nt(dy, d_ref[c, :])
        dg_ref[:, c] = (dh * b_ref[:, c]).astype(BF)
        du_ref[:, c] = (dh * a_ref[:, c]).astype(BF)
    dn_ref[...] = (mm_nt(dg_ref[...], g_ref[...]) + mm_nt(du_ref[...], u_ref[...])).astype(BF)


def ffn_back(dy, a, b, down_w, gate_w, up_w, part, earlier, tm=256, tf=256):
    m, k = dy.shape
    f = gate_w.shape[1]
    steps = m // 2 // tm
    inner = pl.BlockSpec((tm, f), lambda i: (i + part * steps, 0))
    rows = pl.BlockSpec((tm, k), lambda i: (i + part * steps, 0))

    def whole(shape):
        return pl.BlockSpec(shape, lambda i: (0, 0), pipeline_mode=pl.Buffered(1))

    held = () if earlier is None else earlier
    return pl.pallas_call(
        functools.partial(ffn_back_kernel, tf),
        grid=(steps,),
        in_specs=[rows, inner, inner, whole((f, k)), whole((k, f)), whole((k, f))]
        + [pl.BlockSpec(memory_space=pl.ANY)] * len(held),
        out_specs=[inner, inner, pl.BlockSpec((tm, k), lambda i: (i, 0))],
        out_shape=[
            jax.ShapeDtypeStruct((m, f), BF),
            jax.ShapeDtypeStruct((m, f), BF),
            jax.ShapeDtypeStruct((m // 2, k), BF),
        ],
        input_output_aliases={6 + i: i for i in range(len(held))},
        compiler_params=pltpu.CompilerParams(vmem_limit_bytes=VMEM_LIMIT),
        cost_estimate=pl.CostEstimate(
            flops=3 * m * k * f, bytes_accessed=2 * m * k + 6 * k * f + 6 * m * f, transcendentals=0
        ),
        name="ffn_back",
    )(dy, a, b, down_w, gate_w, up_w, *held)


def adamw(param, grad, first, second, rate, decay):
    first_new = BETA_ONE * first + (1.0 - BETA_ONE) * grad
    second_new = BETA_TWO * second + (1.0 - BETA_TWO) * grad * grad
    first_hat = first_new / (1.0 - BETA_ONE**STEP)
    second_hat = second_new / (1.0 - BETA_TWO**STEP)
    param_new = param - rate * (first_hat / (jnp.sqrt(second_hat) + ADAM_EPSILON) + decay * param)
    return (param_new, first_new, second_new)


def line(value, step, direction):
    n = lax.axis_size("sp")
    if direction > 0:
        pairs = [(i, i + 1) for i in range(step - 1, n - 1)]
    else:
        pairs = [(i, i - 1) for i in range(1, n - step + 1)]
    return lax.ppermute(value, "sp", pairs)


def line_gather(value, zi):
    below, above = line(value, 1, 1), line(value, 1, -1)
    below_two, above_two = line(below, 2, 1), line(above, 2, -1)
    below_three, above_three = line(below_two, 3, 1), line(above_two, 3, -1)
    near = jnp.where(zi < 2, above, below)
    mid = jnp.where(
        zi == 0, above_two, jnp.where(zi == 1, below, jnp.where(zi == 2, above, below_two))
    )
    far = jnp.where(
        zi == 0, above_three, jnp.where(zi == 1, above_two, jnp.where(zi == 2, below_two, below_three))
    )
    mid_from = jnp.where(zi == 0, 2, jnp.where(zi == 1, 0, jnp.where(zi == 2, 3, 1)))
    pieces = [
        (value, zi),
        (near, jnp.where(zi < 2, zi + 1, zi - 1)),
        (mid, mid_from),
        (far, jnp.where(zi < 2, 3, 0)),
    ]
    return pieces, (below_two, above_two)


def direct_gather(sends, zi):
    return [(v if k == 0 else swap(v, "sp", k), zi ^ k) for k, v in sends.items()]


def fill_rows(pieces, xi, gates=()):
    nx, nz = lax.axis_size("dp"), lax.axis_size("sp")
    rows, columns = pieces[0][0].shape
    out = jnp.zeros((nx * nz * rows, columns), pieces[0][0].dtype)
    for piece, source in pieces:
        for kx in range(nx):
            got = piece if kx == 0 else swap(after(piece, *gates), "dp", kx)
            out = lax.dynamic_update_slice(out, got, (((xi ^ kx) * nz + source) * rows, 0))
    return out


def fill_units(pieces, xi, gates=()):
    nx, nz = lax.axis_size("dp"), lax.axis_size("sp")
    outer, rows, columns = pieces[0][0].shape
    out = jnp.zeros((outer, nx * nz * rows, columns), pieces[0][0].dtype)
    for piece, source in pieces:
        for kx in range(nx):
            got = piece if kx == 0 else swap(after(piece, *gates), "dp", kx)
            out = lax.dynamic_update_slice(out, got, (0, ((xi ^ kx) * nz + source) * rows, 0))
    return out.reshape(outer * nx * nz * rows, columns)


def reduce_dp(parts, xi):
    total = pick(parts, xi, 0).astype(F32)
    for k in range(1, lax.axis_size("dp")):
        total = total + swap(pick(parts, xi ^ k, 0), "dp", k).astype(F32)
    return total


def reduce_line(parts, xi, zi):
    n = lax.axis_size("sp")
    summed = reduce_dp(parts, xi).astype(BF)
    up = down = None
    for step in range(1, n):
        to_up = pick(summed, jnp.clip(n - step + zi, 0, n - 1), 0)
        to_down = pick(summed, jnp.clip(zi - n + step, 0, n - 1), 0)
        if up is not None:
            to_up = (to_up.astype(F32) + up.astype(F32)).astype(BF)
            to_down = (to_down.astype(F32) + down.astype(F32)).astype(BF)
        up = lax.ppermute(to_up, "sp", [(i, i + 1) for i in range(step)])
        down = lax.ppermute(to_down, "sp", [(i, i - 1) for i in range(n - step, n)])
    return pick(summed, zi, 0).astype(F32) + up.astype(F32) + down.astype(F32)


def reduce_half(parts, xi, zi):
    summed = reduce_dp(parts, xi).astype(BF)
    moved = {k: swap(pick(summed, zi ^ k, 0), "sp", k).astype(F32) for k in (1, 2, 3)}
    return pick(summed, zi, 0).astype(F32) + moved[2], moved[1] + moved[3]


def order_tp(pieces, ti):
    rows = pieces[0]
    out = jnp.zeros((rows.shape[0], 4) + rows.shape[1:], rows.dtype)
    for k, piece in pieces.items():
        out = lax.dynamic_update_slice(out, piece[:, None], (0, ti ^ k, 0, 0))
    return out


def gather_tp(rows, ti):
    from_y = swap(rows, "tp", 2)
    return order_tp({0: rows, 1: swap(rows, "tp", 1), 2: from_y, 3: swap(from_y, "tp", 1)}, ti)


def reduce_tp(parts, ti):
    y, c = ti // 2, ti % 2
    split = parts.reshape((parts.shape[0], 2, 2) + parts.shape[2:])
    got = swap(pick(split, 1 - c, 2), "tp", 1)
    mine = (pick(split, c, 2).astype(F32) + got.astype(F32)).astype(BF)
    return pick(mine, y, 1).astype(F32) + swap(pick(mine, 1 - y, 1), "tp", 2).astype(F32)


def gather_group(rows):
    n = rows.shape[0] // 2
    a, b = rows[:n], rows[n:]
    a_y = swap(a, "tp", 2)
    b_z = swap(b, "sp", 1)
    a_z = swap(a, "sp", 1)
    b_y = swap(b, "tp", 2)
    a_yz = swap(a_y, "sp", 1)
    b_zy = swap(b_z, "tp", 2)
    mine = [a, a_z, a_y, a_yz, b, b_y, b_z, b_zy]
    other = [swap(v, "tp", 1) for v in mine]
    return jnp.concatenate(mine + other, axis=0)


def reduce_group(mine, other):
    total = (mine.astype(F32) + swap(other, "tp", 1).astype(F32)).astype(BF)
    n = mine.shape[0] // 8
    a, b = total[: 4 * n], total[4 * n :]
    a_got = swap(a[2 * n :], "tp", 2)
    b_got = swap(b[2 * n :], "sp", 1)
    a = (a[: 2 * n].astype(F32) + a_got.astype(F32)).astype(BF)
    b = (b[: 2 * n].astype(F32) + b_got.astype(F32)).astype(BF)
    a_got = swap(a[n:], "sp", 1)
    b_got = swap(b[n:], "tp", 2)
    return jnp.concatenate(
        [a[:n].astype(F32) + a_got.astype(F32), b[:n].astype(F32) + b_got.astype(F32)], axis=0
    )


def place(pieces, index):
    out = jnp.zeros((len(pieces),) + pieces[0].shape, pieces[0].dtype)
    for mask, piece in pieces.items():
        out = lax.dynamic_update_index_in_dim(out, piece, index ^ mask, 0)
    return out


def spread(rows, zi, gates=()):
    got = {0: pick(rows, zi, 0)}
    for k in (1, 2, 3):
        got[k] = swap(after(pick(rows, zi ^ k, 0), *gates), "sp", k)
    return got


def local(
    block_in,
    cotangent,
    qkv_weight,
    proj_weight,
    feed_weight,
    down_weight,
    norm_gains,
    qkv_first,
    proj_first,
    feed_first,
    down_first,
    gains_first,
    qkv_second,
    proj_second,
    feed_second,
    down_second,
    gains_second,
):
    xi, zi, ti = lax.axis_index("dp"), lax.axis_index("sp"), lax.axis_index("tp")
    nx, nz = lax.axis_size("dp"), lax.axis_size("sp")
    half = zi % 2
    width = block_in.shape[2]
    span = block_in.shape[1]
    length = span * nz * 4
    groups, row_block, columns = qkv_weight.shape
    proj_rows = proj_weight.shape[1]
    units, unit_rows = down_weight.shape[0], down_weight.shape[1]
    feed_columns = feed_weight.shape[2] // 2

    x_pieces = spread(block_in, zi)
    x_rows = place(x_pieces, zi)
    x_from_y = place({k: swap(v, "tp", 2) for k, v in x_pieces.items()}, zi)
    x_all = order_tp(
        {0: x_rows, 1: swap(x_rows, "tp", 1), 2: x_from_y, 3: swap(x_from_y, "tp", 1)}, ti
    ).reshape(length, width)

    gains_low = norm_gains.astype(BF)
    gain_values = fill_units(
        [(v[:, None], z) for v, z in direct_gather({k: gains_low for k in range(4)}, zi)], xi
    )
    gain_values = gain_values.reshape(2, width).astype(F32)

    qkv_mine = qkv_weight.transpose(1, 0, 2).reshape(row_block, groups * columns).astype(BF)
    qkv_pieces, qkv_late = line_gather(qkv_mine, zi)
    qkv_all = fill_rows(qkv_pieces, xi)
    proj_mine = after(proj_weight.astype(BF), *qkv_late)
    proj_pieces, proj_late = line_gather(proj_mine, zi)
    proj_all = fill_units(proj_pieces, xi)

    dy_pieces = spread(cotangent, zi, qkv_late)
    dy_rows = place(dy_pieces, zi)

    def halves(value, axis, gates):
        size = value.shape[axis] // 2
        same = lax.dynamic_slice_in_dim(value, half * size, size, axis).astype(BF)
        other = lax.dynamic_slice_in_dim(value, (1 - half) * size, size, axis).astype(BF)
        same, other = lax.optimization_barrier((same, other) + tuple(gates))[:2]
        return {0: same, 1: other, 2: same, 3: other}

    gate_pieces = direct_gather(halves(feed_weight[0], 1, qkv_late), zi)
    up_pieces = direct_gather(halves(feed_weight[1], 1, (gate_pieces[2][0], gate_pieces[3][0])), zi)
    down_pieces = direct_gather(halves(down_weight, 0, (up_pieces[2][0], up_pieces[3][0])), zi)

    def norm(rows, gain):
        inverse = lax.rsqrt(jnp.mean(rows * rows, axis=-1, keepdims=True) + NORM_EPSILON)
        unit = rows * inverse
        return unit, inverse, (unit * gain).astype(BF)

    _, _, normed_one = norm(x_all.astype(F32), gain_values[0])
    projected = mm(normed_one, qkv_all)
    cosine, sine = tables(length)
    qkv, context, logs = attend(projected, cosine, sine, groups)
    attn_part = mm(context, proj_all).astype(BF).reshape(nz, 4, span, width)
    attn_mine = reduce_tp(attn_part, ti).reshape(-1, width)
    inputs = x_rows.astype(F32).reshape(-1, width)
    hidden_one = inputs + attn_mine
    unit_two, inverse_two, normed_two = norm(hidden_one, gain_values[1])

    gate_all = fill_rows(gate_pieces, xi, (projected,))
    up_all = fill_rows(up_pieces, xi, (context,))
    down_all = fill_units(down_pieces, xi, (attn_part,))
    dy_all = gather_group(after(dy_rows.reshape(-1, width), projected))

    normed_all = gather_group(normed_two)
    hidden, activated, slope = gate_up(normed_all, gate_all, up_all)
    part_rows = dy_all.shape[0] // 2
    grad_gate, grad_up, grad_other = ffn_back(
        dy_all, activated, slope, down_all, gate_all, up_all, 1, None
    )
    grad_gate, grad_up, grad_mine = ffn_back(
        dy_all, activated, slope, down_all, gate_all, up_all, 0, (grad_gate, grad_up)
    )
    grad_normed_two = reduce_group(grad_mine, grad_other)

    down_part = mm_tn(hidden, dy_all).astype(BF)
    down_part = down_part.reshape(units // 2, nx, nz, unit_rows, width).transpose(1, 2, 0, 3, 4)
    down_same, down_other = reduce_half(down_part, xi, zi)
    gate_part = mm_tn(normed_all, grad_gate).astype(BF)
    gate_part = gate_part.reshape(nx, nz, row_block, feed_columns)
    gate_same, gate_other = reduce_half(gate_part, xi, zi)
    up_part = mm_tn(normed_all, grad_up).astype(BF).reshape(nx, nz, row_block, feed_columns)
    up_same, up_other = reduce_half(up_part, xi, zi)
    out_part = mm(hidden, down_all).astype(BF)
    ffn_mine = reduce_group(out_part[:part_rows], out_part[part_rows:])

    grad_unit = grad_normed_two * gain_values[1]
    row_inner = jnp.mean(grad_unit * unit_two, axis=-1, keepdims=True)
    dy_own = dy_rows.astype(F32).reshape(-1, width)
    back_two = inverse_two * (grad_unit - unit_two * row_inner)
    gain_two_part = jnp.sum(grad_normed_two * unit_two, axis=0)
    grad_hidden_one = dy_own + back_two
    grad_rows = gather_tp(grad_hidden_one.astype(BF).reshape(nz, span, width), ti)
    grad_rows = grad_rows.reshape(length, width)
    grad_context = mm_nt(grad_rows, proj_all).astype(BF)
    proj_part = mm_tn(context, grad_rows).astype(BF).reshape(groups, nx, nz, proj_rows, width)
    proj_grad = reduce_line(proj_part.transpose(1, 2, 0, 3, 4), xi, zi)
    grad_projected = attend_back(qkv, grad_context, logs, cosine, sine, groups)

    grad_normed_one = mm_nt(grad_projected, qkv_all).astype(BF).reshape(nz, 4, span, width)
    grad_normed_one = reduce_tp(grad_normed_one, ti).reshape(-1, width)
    qkv_part = mm_tn(normed_one, grad_projected).astype(BF)
    qkv_part = qkv_part.reshape(nx, nz, row_block, groups * columns)
    qkv_grad = reduce_line(qkv_part, xi, zi)
    qkv_grad = qkv_grad.reshape(row_block, groups, columns).transpose(1, 0, 2)

    inverse_one = lax.rsqrt(jnp.mean(inputs * inputs, axis=-1, keepdims=True) + NORM_EPSILON)
    unit_one = inputs * inverse_one
    grad_unit = grad_normed_one * gain_values[0]
    row_inner = jnp.mean(grad_unit * unit_one, axis=-1, keepdims=True)
    back_one = inverse_one * (grad_unit - unit_one * row_inner)
    gain_one_part = jnp.sum(grad_normed_one * unit_one, axis=0)

    block_delta = (attn_mine + ffn_mine).astype(BF).reshape(nz, span, width)
    input_delta = (back_two + back_one).astype(BF).reshape(nz, span, width)
    block_out = block_in.astype(F32) + place(spread(block_delta, zi), zi).astype(F32)
    input_grad = cotangent.astype(F32) + place(spread(input_delta, zi), zi).astype(F32)

    gains_part = jnp.stack([gain_one_part, gain_two_part])
    gains_part = gains_part + swap(gains_part, "tp", 1)
    gains_part = gains_part + swap(gains_part, "tp", 2)
    gains_part = gains_part.reshape(2, nx, nz, row_block).transpose(1, 2, 0, 3)
    gains_sum = pick(gains_part, xi, 0)
    for k in range(1, nx):
        gains_sum = gains_sum + swap(pick(gains_part, xi ^ k, 0), "dp", k)
    gains_grad = pick(gains_sum, zi, 0)
    for k in (1, 2, 3):
        gains_grad = gains_grad + swap(pick(gains_sum, zi ^ k, 0), "sp", k)

    def join(same, other, axis):
        low = jnp.where(half == 0, same, other)
        high = jnp.where(half == 0, other, same)
        return jnp.concatenate([low, high], axis=axis)

    feed_grad = jnp.stack([join(gate_same, gate_other, 1), join(up_same, up_other, 1)])
    down_grad = join(down_same, down_other, 0)

    qkv_new, qkv_first_new, qkv_second_new = adamw(
        qkv_weight, qkv_grad, qkv_first, qkv_second, QKV_RATE, WEIGHT_DECAY
    )
    proj_new, proj_first_new, proj_second_new = adamw(
        proj_weight, proj_grad, proj_first, proj_second, PROJ_RATE, WEIGHT_DECAY
    )
    feed_new, feed_first_new, feed_second_new = adamw(
        feed_weight, feed_grad, feed_first, feed_second, FEED_RATE, WEIGHT_DECAY
    )
    down_new, down_first_new, down_second_new = adamw(
        down_weight, down_grad, down_first, down_second, DOWN_RATE, WEIGHT_DECAY
    )
    gains_new, gains_first_new, gains_second_new = adamw(
        norm_gains, gains_grad, gains_first, gains_second, GAIN_RATE, 0.0
    )
    return (
        block_out,
        input_grad,
        qkv_grad,
        proj_grad,
        feed_grad,
        down_grad,
        gains_grad,
        qkv_new,
        proj_new,
        feed_new,
        down_new,
        gains_new,
        qkv_first_new,
        proj_first_new,
        feed_first_new,
        down_first_new,
        gains_first_new,
        qkv_second_new,
        proj_second_new,
        feed_second_new,
        down_second_new,
        gains_second_new,
    )


def solution(mesh):
    rows = P("dp", ("sp", "tp"), None)
    heads = P("tp", ("dp", "sp"), None)
    feed = P(None, ("dp", "sp"), "tp")
    gains = P(None, ("dp", "sp"))
    params = (heads, heads, feed, heads, gains)
    return jax.shard_map(
        local,
        mesh=mesh,
        in_specs=(rows, rows) + params * 3,
        out_specs=(rows, rows) + params * 4,
        check_vma=False,
    )
```

```python
import functools

import jax
import jax.numpy as jnp
from jax import lax
from jax.experimental import pallas as pl
from jax.experimental.pallas import tpu as pltpu
from jax.sharding import Mesh, PartitionSpec as P

HD = 64
QPK = 4
STEP = 10
LANES = 128
VMEM_LIMIT = 56 * 1024 * 1024
SP = ("sp_pair", "sp_in_pair")


NORM_EPSILON = 1e-05
ROPE_BASE = 500000.0
MASKED = -1e30
BETA_ONE = 0.9
BETA_TWO = 0.95
ADAM_EPSILON = 1e-08
WEIGHT_DECAY = 0.1
QKV_RATE = 0.05
PROJ_RATE = 0.4
FEED_RATE = 0.05
DOWN_RATE = 0.03
GAIN_RATE = 0.5

BF = jnp.bfloat16
F32 = jnp.float32
HEAVY = pl.CostEstimate(flops=1 << 36, bytes_accessed=1 << 20, transcendentals=0)
LIGHT = pl.CostEstimate(flops=1 << 32, bytes_accessed=1 << 20, transcendentals=0)


def after(value, *earlier):
    return lax.optimization_barrier((value,) + earlier)[0]


def swap(value, axis, mask):
    return lax.ppermute(value, axis, [(i, i ^ mask) for i in range(lax.axis_size(axis))])


def pick(value, index, axis):
    return lax.dynamic_index_in_dim(value, index, axis, keepdims=False)


def dot(left, right, dims):
    return lax.dot_general(left, right, ((dims[0], dims[1]), ((), ())), preferred_element_type=F32)


def mm(left, right):
    return dot(left, right, ((1,), (0,)))


def mm_nt(left, right):
    return dot(left, right, ((1,), (1,)))


def mm_tn(left, right):
    return dot(left, right, ((0,), (0,)))


def turn(block, cosine, sine):
    lane = lax.broadcasted_iota(jnp.int32, block.shape, 1)
    ahead = pltpu.roll(block, LANES - HD // 2, 1)
    behind = pltpu.roll(block, HD // 2, 1)
    return block * cosine + jnp.where(lane % HD < HD // 2, ahead, behind) * sine

def key_tables(cosine, sine):
    lane = lax.broadcasted_iota(jnp.int32, cosine.shape, 1)
    return jnp.where(lane < HD, cosine, 1.0), jnp.where(lane < HD, sine, 0.0)

def attend_kernel(tile, p_ref, cos_ref, sin_ref, qkv_ref, ctx_ref, log_ref, q_s, k_s, vt_s, c_s):
    length = p_ref.shape[0]
    cosine, sine = cos_ref[...], sin_ref[...]
    for b in range(QPK // 2):
        block = turn(p_ref[:, b * LANES : (b + 1) * LANES], cosine, sine).astype(BF) * BF(HD ** -0.5)
        qkv_ref[:, b * LANES : (b + 1) * LANES] = block
        q_s[2 * b] = block[:, :HD]
        q_s[2 * b + 1] = block[:, HD:]
    k_cos, k_sin = key_tables(cosine, sine)
    block = turn(p_ref[:, QPK * HD :], k_cos, k_sin)
    qkv_ref[:, QPK * HD :] = block.astype(BF)
    k_s[...] = block[:, :HD].astype(BF)
    vt_s[...] = jnp.transpose(block)[HD:].astype(BF)
    keep = lax.broadcasted_iota(jnp.int32, (tile, tile), 0) <= lax.broadcasted_iota(jnp.int32, (tile, tile), 1)

    def head(n, carry):
        for t in range(length // tile):
            before, here = t * tile, slice(t * tile, (t + 1) * tile)
            q = q_s[n, here, :]
            s_here = jnp.where(keep, mm_nt(k_s[here, :], q), MASKED)
            peak = jnp.max(s_here, axis=0, keepdims=True)
            if t:
                s_before = mm_nt(k_s[:before, :], q)
                peak = jnp.maximum(peak, jnp.max(s_before, axis=0, keepdims=True))
            e_here = jnp.exp(s_here - peak)
            total = jnp.sum(e_here, axis=0, keepdims=True)
            if t:
                e_before = jnp.exp(s_before - peak)
                total = total + jnp.sum(e_before, axis=0, keepdims=True)
            scale = 1.0 / total
            out = mm(vt_s[:, here], (e_here * scale).astype(BF))
            if t:
                out = out + mm(vt_s[:, :before], (e_before * scale).astype(BF))
            c_s[pl.ds(pl.multiple_of(n * HD, HD), HD), here] = out
            log_ref[0, pl.ds(n, 1), here] = peak + jnp.log(total)
        return carry

    lax.fori_loop(0, QPK, head, 0)
    ctx_ref[...] = jnp.transpose(c_s[...]).astype(BF)

def attend(projected, cosine, sine, groups, tile=256):
    length, columns = projected.shape[0], projected.shape[1] // groups
    qw = QPK * HD
    table = pl.BlockSpec((length, LANES), lambda g: (0, 0))
    return pl.pallas_call(
        functools.partial(attend_kernel, tile),
        grid=(groups,),
        in_specs=[pl.BlockSpec((length, columns), lambda g: (0, g)), table, table],
        out_specs=[
            pl.BlockSpec((length, columns), lambda g: (0, g)),
            pl.BlockSpec((length, qw), lambda g: (0, g)),
            pl.BlockSpec((1, QPK, length), lambda g: (g, 0, 0)),
        ],
        out_shape=[
            jax.ShapeDtypeStruct((length, groups * columns), BF),
            jax.ShapeDtypeStruct((length, groups * qw), BF),
            jax.ShapeDtypeStruct((groups, QPK, length), F32),
        ],
        scratch_shapes=[
            pltpu.VMEM((QPK, length, HD), BF),
            pltpu.VMEM((length, HD), BF),
            pltpu.VMEM((HD, length), BF),
            pltpu.VMEM((qw, length), F32),
        ],
        compiler_params=pltpu.CompilerParams(vmem_limit_bytes=VMEM_LIMIT),
        cost_estimate=HEAVY,
        name="attend",
    )(projected, cosine, sine)

def attend_back_kernel(tile, qkv_ref, grad_ref, log_ref, cos_ref, sin_ref, out_ref, q_s, k_s, v_s, kt_s, g_s, dk_s, dv_s, dq_s):
    length = qkv_ref.shape[0]
    for b in range(QPK // 2):
        lanes = slice(b * LANES, (b + 1) * LANES)
        block, grad = qkv_ref[:, lanes], grad_ref[:, lanes]
        q_s[2 * b], q_s[2 * b + 1] = block[:, :HD], block[:, HD:]
        g_s[2 * b], g_s[2 * b + 1] = grad[:, :HD], grad[:, HD:]
    block = qkv_ref[:, QPK * HD :]
    k_s[...] = block[:, :HD]
    v_s[...] = block[:, HD:]
    kt_s[...] = jnp.transpose(block.astype(F32))[:HD].astype(BF)
    dk_s[...] = jnp.zeros_like(dk_s)
    dv_s[...] = jnp.zeros_like(dv_s)
    keep = lax.broadcasted_iota(jnp.int32, (tile, tile), 0) <= lax.broadcasted_iota(jnp.int32, (tile, tile), 1)

    def head(n, carry):
        for t in range(length // tile):
            before, here = t * tile, slice(t * tile, (t + 1) * tile)
            upto = slice(0, (t + 1) * tile)
            q, g = q_s[n, here, :], g_s[n, here, :]
            log = log_ref[0, pl.ds(n, 1), here]
            a_here = jnp.exp(jnp.where(keep, mm_nt(k_s[here, :], q), MASKED) - log)
            d_here = mm_nt(v_s[here, :], g)
            inner = jnp.sum(a_here * d_here, axis=0, keepdims=True)
            if t:
                a_before = jnp.exp(mm_nt(k_s[:before, :], q) - log)
                d_before = mm_nt(v_s[:before, :], g)
                inner = inner + jnp.sum(a_before * d_before, axis=0, keepdims=True)
            s_here = (a_here * (d_here - inner)).astype(BF)
            dq = mm(kt_s[:, here], s_here)
            dk_s[here, :] += mm(s_here, q)
            dv_s[here, :] += mm(a_here.astype(BF), g)
            if t:
                s_before = (a_before * (d_before - inner)).astype(BF)
                dq = dq + mm(kt_s[:, :before], s_before)
                dk_s[:before, :] += mm(s_before, q)
                dv_s[:before, :] += mm(a_before.astype(BF), g)
            dq_s[pl.ds(pl.multiple_of(n * HD, HD), HD), here] = dq * HD ** -0.5
        return carry

    lax.fori_loop(0, QPK, head, 0)
    cosine, sine = cos_ref[...], sin_ref[...]
    grad = jnp.transpose(dq_s[...])
    for b in range(QPK // 2):
        lanes = slice(b * LANES, (b + 1) * LANES)
        out_ref[:, lanes] = turn(grad[:, lanes], cosine, -sine).astype(BF)
    k_cos, k_sin = key_tables(cosine, sine)
    block = jnp.concatenate([dk_s[...], dv_s[...]], axis=1)
    out_ref[:, QPK * HD :] = turn(block, k_cos, -k_sin).astype(BF)

def attend_back(qkv, grad, log, cosine, sine, groups, tile=256):
    length, columns = qkv.shape[0], qkv.shape[1] // groups
    qw = QPK * HD
    table = pl.BlockSpec((length, LANES), lambda g: (0, 0))
    return pl.pallas_call(
        functools.partial(attend_back_kernel, tile),
        grid=(groups,),
        in_specs=[
            pl.BlockSpec((length, columns), lambda g: (0, g)),
            pl.BlockSpec((length, qw), lambda g: (0, g)),
            pl.BlockSpec((1, QPK, length), lambda g: (g, 0, 0)),
            table, table],
        out_specs=pl.BlockSpec((length, columns), lambda g: (0, g)),
        out_shape=jax.ShapeDtypeStruct((length, groups * columns), BF),
        scratch_shapes=[
            pltpu.VMEM((QPK, length, HD), BF),
            pltpu.VMEM((length, HD), BF),
            pltpu.VMEM((length, HD), BF),
            pltpu.VMEM((HD, length), BF),
            pltpu.VMEM((QPK, length, HD), BF),
            pltpu.VMEM((length, HD), F32),
            pltpu.VMEM((length, HD), F32),
            pltpu.VMEM((qw, length), F32),
        ],
        compiler_params=pltpu.CompilerParams(vmem_limit_bytes=VMEM_LIMIT),
        cost_estimate=HEAVY,
        name="attend_back",
    )(qkv, grad, log, cosine, sine)

def tables(length):
    half = HD // 2
    freq = ROPE_BASE ** (-(jnp.arange(half, dtype=F32) * 2.0 / HD))
    ang = jnp.arange(length).astype(F32)[:, None] * freq[None, :]
    c, s = jnp.cos(ang), jnp.sin(ang)
    return jnp.concatenate([c, c, c, c], 1), jnp.concatenate([-s, s, -s, s], 1)

def by_parts(at_ref, rows_ref, weights):
    depth = weights[0].shape[0]
    total = None
    for k, weight in enumerate(weights):
        rows = rows_ref[:, pl.ds(pl.multiple_of(at_ref[k] * depth, depth), depth)]
        part = mm(rows, weight[...])
        total = part if total is None else total + part
    return total


def gate_kernel(blocks, at_ref, *refs):
    rows_refs, weights, (gate_ref, rows_ref) = refs[:blocks], refs[blocks:-2], refs[-2:]

    @pl.when(pl.program_id(1) == 0)
    def _():
        for t in range(blocks):

            @pl.when(pl.program_id(0) == t)
            def _():
                rows_ref[...] = rows_refs[t][...]

    gate_ref[...] = by_parts(at_ref, rows_ref, weights)


def gate_rows(at, rows, gates, tf=512):
    tm, k = rows[0].shape
    f = gates[0].shape[1]
    parts, blocks = len(gates), len(rows)
    return pl.pallas_call(
        functools.partial(gate_kernel, blocks),
        grid=(blocks, f // tf),
        in_specs=[pl.BlockSpec(memory_space=pltpu.SMEM)]
        + [pl.BlockSpec((tm, k), lambda i, j: (0, 0), pipeline_mode=pl.Buffered(1))] * blocks
        + [pl.BlockSpec((k // parts, tf), lambda i, j: (0, j))] * parts,
        out_specs=[
            pl.BlockSpec((tm, tf), lambda i, j: (i, j)),
            pl.BlockSpec((tm, k), lambda i, j: (i, 0)),
        ],
        out_shape=[
            jax.ShapeDtypeStruct((tm * blocks, f), F32),
            jax.ShapeDtypeStruct((tm * blocks, k), BF),
        ],
        compiler_params=pltpu.CompilerParams(vmem_limit_bytes=VMEM_LIMIT),
        cost_estimate=HEAVY,
        name="gate_rows",
    )(at, *rows, *gates)


def up_kernel(at_ref, rows_ref, gate_ref, *refs):
    weights, (hid_ref, a_ref, b_ref) = refs[:-3], refs[-3:]
    up = by_parts(at_ref, rows_ref, weights)
    gate = gate_ref[...]
    s = jax.nn.sigmoid(gate)
    act = gate * s
    hid_ref[...] = (act * up).astype(BF)
    a_ref[...] = act
    b_ref[...] = up * s * (1.0 + gate * (1.0 - s))


def up_rows(at, rows, gate, ups, tm=512, tf=512):
    m, k = rows.shape
    f = gate.shape[1]
    parts = len(ups)
    o = pl.BlockSpec((tm, tf), lambda i, j: (i, j))
    return pl.pallas_call(
        up_kernel,
        grid=(m // tm, f // tf),
        in_specs=[
            pl.BlockSpec(memory_space=pltpu.SMEM),
            pl.BlockSpec((tm, k), lambda i, j: (i, 0)),
            o,
        ]
        + [pl.BlockSpec((k // parts, tf), lambda i, j: (0, j))] * parts,
        out_specs=[o, o, o],
        out_shape=[
            jax.ShapeDtypeStruct((m, f), BF),
            jax.ShapeDtypeStruct((m, f), F32),
            jax.ShapeDtypeStruct((m, f), F32),
        ],
        compiler_params=pltpu.CompilerParams(vmem_limit_bytes=VMEM_LIMIT),
        cost_estimate=HEAVY,
        name="up_rows",
    )(at, rows, gate, *ups)


def ffn_back_kernel(tf, parts, at_ref, dy_ref, a_ref, b_ref, d_ref, *refs):
    weights, (dg_ref, du_ref, dn_ref) = refs[: 2 * parts], refs[-3:]
    dy = dy_ref[...]
    for j in range(d_ref.shape[0] // tf):
        c = slice(j * tf, (j + 1) * tf)
        dh = mm_nt(dy, d_ref[c, :])
        dg_ref[:, c] = (dh * b_ref[:, c]).astype(BF)
        du_ref[:, c] = (dh * a_ref[:, c]).astype(BF)
    depth = weights[0].shape[0]
    for k in range(parts):
        part = mm_nt(dg_ref[...], weights[k][...]) + mm_nt(du_ref[...], weights[parts + k][...])
        dn_ref[:, pl.ds(pl.multiple_of(at_ref[k] * depth, depth), depth)] = part.astype(BF)


def ffn_back(at, dy, a, b, down_w, gates, ups, part, earlier, tm=256, tf=256):
    m, k = dy.shape
    f = gates[0].shape[1]
    parts = len(gates)
    steps = m // 2 // tm
    inner = pl.BlockSpec((tm, f), lambda i: (i + part * steps, 0))
    rows = pl.BlockSpec((tm, k), lambda i: (i + part * steps, 0))

    def whole(shape):
        return pl.BlockSpec(shape, lambda i: (0, 0), pipeline_mode=pl.Buffered(1))

    held = () if earlier is None else earlier
    return pl.pallas_call(
        functools.partial(ffn_back_kernel, tf, parts),
        grid=(steps,),
        in_specs=[pl.BlockSpec(memory_space=pltpu.SMEM), rows, inner, inner, whole((f, k))]
        + [whole((k // parts, f))] * (2 * parts)
        + [pl.BlockSpec(memory_space=pl.ANY)] * len(held),
        out_specs=[inner, inner, pl.BlockSpec((tm, k), lambda i: (i, 0))],
        out_shape=[
            jax.ShapeDtypeStruct((m, f), BF),
            jax.ShapeDtypeStruct((m, f), BF),
            jax.ShapeDtypeStruct((m // 2, k), BF),
        ],
        input_output_aliases={5 + 2 * parts + i: i for i in range(len(held))},
        compiler_params=pltpu.CompilerParams(vmem_limit_bytes=VMEM_LIMIT),
        cost_estimate=HEAVY,
        name="ffn_back",
    )(at, dy, a, b, down_w, *gates, *ups, *held)


def project_kernel(pieces, at_ref, *refs):
    piece_refs, (gain_ref, w_ref, n_ref, p_ref, x_s) = refs[:pieces], refs[pieces:]
    rows = piece_refs[0].shape[1]
    for k in range(pieces):
        x_s[pl.ds(pl.multiple_of(at_ref[k] * rows, rows), rows), :] = piece_refs[k][0]
    x = x_s[...].astype(F32)
    inverse = lax.rsqrt(jnp.mean(x * x, axis=-1, keepdims=True) + NORM_EPSILON)
    n_ref[...] = (x * inverse * gain_ref[...]).astype(BF)
    p_ref[...] = mm(n_ref[...], w_ref[...])


def project(at, pieces, gain, weights):
    b, r, d = pieces[0].shape
    c = weights.shape[1]
    rows = r * len(pieces)
    return pl.pallas_call(
        functools.partial(project_kernel, len(pieces)),
        grid=(b,),
        in_specs=[pl.BlockSpec(memory_space=pltpu.SMEM)]
        + [pl.BlockSpec((1, r, d), lambda i: (i, 0, 0))] * len(pieces)
        + [
            pl.BlockSpec((1, d), lambda i: (0, 0)),
            pl.BlockSpec((d, c), lambda i: (0, 0), pipeline_mode=pl.Buffered(1)),
        ],
        out_specs=[pl.BlockSpec((rows, d), lambda i: (i, 0)), pl.BlockSpec((rows, c), lambda i: (i, 0))],
        out_shape=[jax.ShapeDtypeStruct((b * rows, d), BF), jax.ShapeDtypeStruct((b * rows, c), F32)],
        scratch_shapes=[pltpu.VMEM((rows, d), BF)],
        compiler_params=pltpu.CompilerParams(vmem_limit_bytes=VMEM_LIMIT),
        cost_estimate=LIGHT,
        name="project",
    )(at, *pieces, gain, weights)


def context_kernel(pieces, at_ref, *refs):
    piece_refs, (w_ref, rows_ref, c_ref) = refs[:pieces], refs[pieces:]
    rows = piece_refs[0].shape[1]
    for k in range(pieces):
        rows_ref[pl.ds(pl.multiple_of(at_ref[k] * rows, rows), rows), :] = piece_refs[k][0]
    c_ref[...] = mm_nt(rows_ref[...], w_ref[...]).astype(BF)


def context_grad(at, pieces, weights):
    b, r, d = pieces[0].shape
    c = weights.shape[0]
    rows = r * len(pieces)
    return pl.pallas_call(
        functools.partial(context_kernel, len(pieces)),
        grid=(b,),
        in_specs=[pl.BlockSpec(memory_space=pltpu.SMEM)]
        + [pl.BlockSpec((1, r, d), lambda i: (i, 0, 0))] * len(pieces)
        + [pl.BlockSpec((c, d), lambda i: (0, 0), pipeline_mode=pl.Buffered(1))],
        out_specs=[pl.BlockSpec((rows, d), lambda i: (i, 0)), pl.BlockSpec((rows, c), lambda i: (i, 0))],
        out_shape=[jax.ShapeDtypeStruct((b * rows, d), BF), jax.ShapeDtypeStruct((b * rows, c), BF)],
        compiler_params=pltpu.CompilerParams(vmem_limit_bytes=VMEM_LIMIT),
        cost_estimate=LIGHT,
        name="context_grad",
    )(at, *pieces, weights)


def collect_kernel(put, parts, at_ref, *refs):
    for k in range(parts):
        put(refs[k], refs[parts], at_ref[k])


def collect(at, pieces, shape, put):
    return pl.pallas_call(
        functools.partial(collect_kernel, put, len(pieces)),
        in_specs=[pl.BlockSpec(memory_space=pltpu.SMEM)]
        + [pl.BlockSpec(memory_space=pltpu.VMEM)] * len(pieces),
        out_specs=pl.BlockSpec(memory_space=pltpu.VMEM),
        out_shape=jax.ShapeDtypeStruct(shape, pieces[0].dtype),
        compiler_params=pltpu.CompilerParams(vmem_limit_bytes=VMEM_LIMIT),
        name="collect",
    )(at, *pieces)


def fence_kernel(x_ref, o_ref):
    o_ref[...] = x_ref[...]


def fence_call(value):
    return pl.pallas_call(
        fence_kernel,
        out_shape=jax.ShapeDtypeStruct(value.shape, value.dtype),
        cost_estimate=HEAVY,
        name="fence",
    )(value)


def adamw(param, grad, first, second, rate, decay):
    first_new = BETA_ONE * first + (1.0 - BETA_ONE) * grad
    second_new = BETA_TWO * second + (1.0 - BETA_TWO) * grad * grad
    first_hat = first_new / (1.0 - BETA_ONE**STEP)
    second_hat = second_new / (1.0 - BETA_TWO**STEP)
    param_new = param - rate * (first_hat / (jnp.sqrt(second_hat) + ADAM_EPSILON) + decay * param)
    return (param_new, first_new, second_new)


class Chain:
    def __init__(self):
        self.token = None
        self.begun = []

    def now(self, value):
        return value if self.token is None else after(value, self.token)

    def take(self, value):
        value = self.now(value)
        self.begun.append(value)
        return value

    def start(self, value, axis, mask, name):
        value = self.take(value)
        with jax.named_scope(name):
            return swap(value, axis, mask)

    def start_dp(self, value, name):
        return [self.start(value, "dp", k, name) for k in range(1, lax.axis_size("dp"))]

    def start_all(self, blocks, name):
        blocks = self.take(blocks)
        with jax.named_scope(name):
            return lax.all_to_all(blocks, SP, 0, 0, tiled=True)

    def fence(self, *values):
        seed = self.token
        if seed is None or seed.shape != (8, LANES):
            seed = jnp.zeros((8, LANES), F32) if seed is None else after(jnp.zeros((8, LANES), F32), seed)
        self.passed(fence_call(after(seed, *self.begun, *values)))

    def passed(self, token):
        self.token = token
        self.begun = []

    def gate(self, value):
        return after(value, *self.begun) if self.begun else value


def order_units(pieces, at, sp):
    _, outer, rows, width = pieces[0].shape
    if rows % 16:
        out = jnp.zeros((outer, len(pieces), sp * rows, width), BF)
        for k, piece in enumerate(pieces):
            piece = piece.transpose(1, 0, 2, 3).reshape(outer, 1, sp * rows, width)
            out = lax.dynamic_update_slice(out, piece, (0, at[k], 0, 0))
        return out.reshape(-1, width)

    def put(piece, out, x):
        for z in range(sp):
            out[:, x, z * rows : (z + 1) * rows] = piece[z]

    return collect(at, pieces, (outer, len(pieces), sp * rows, width), put).reshape(-1, width)


def place(pieces, index):
    out = jnp.zeros((len(pieces),) + pieces[0].shape, pieces[0].dtype)
    for mask, piece in pieces.items():
        out = lax.dynamic_update_index_in_dim(out, piece, index ^ mask, 0)
    return out


class Gather:
    def __init__(self, chain, rows, name):
        self.chain = chain
        self.name = name
        n = rows.shape[0] // 2
        self.a, self.b, self.n = rows[:n], rows[n:], n
        self.a_y = chain.start(self.a, "tp", 2, name)
        self.b_z = chain.start(self.b, SP, 1, name)

    def second(self):
        now, n = self.chain.now, self.n
        self.near = jnp.concatenate([self.a, now(self.a_y), self.b, now(self.b_z)], axis=0)
        self.far_z = self.chain.start(self.near[: 2 * n], SP, 1, self.name)
        self.far_y = self.chain.start(self.near[2 * n :], "tp", 2, self.name)

    def near_core(self):
        self.near_other = self.chain.start(self.near, "tp", 1, self.name)

    def far_core(self):
        now = self.chain.now
        self.far = jnp.concatenate([now(self.far_z), now(self.far_y)], axis=0)
        self.far_other = self.chain.start(self.far, "tp", 1, self.name)

    def result(self):
        now = self.chain.now
        return [self.near, self.far, now(self.near_other), now(self.far_other)]


class Reduce:
    def __init__(self, chain, other, name):
        self.chain = chain
        self.name = name
        self.got = chain.start(other, "tp", 1, name)

    def first(self, mine):
        total = (mine.astype(F32) + self.chain.now(self.got).astype(F32)).astype(BF)
        total = total.reshape(2, 2, 2, -1, total.shape[-1])
        self.a, self.b = (total[0, 0, 0], total[1, 0, 0]), (total[0, 1, 0], total[1, 1, 0])
        self.a_y = self.chain.start(total[:, 0, 1], "tp", 2, self.name)
        self.b_z = self.chain.start(total[:, 1, 1], SP, 1, self.name)

    def second(self):
        a_y, b_z = self.chain.now(self.a_y).astype(F32), self.chain.now(self.b_z).astype(F32)
        self.a_sum = self.a[0].astype(F32) + a_y[0]
        self.b_sum = self.b[0].astype(F32) + b_z[0]
        self.a_z = self.chain.start((self.a[1].astype(F32) + a_y[1]).astype(BF), SP, 1, self.name)
        self.b_y = self.chain.start((self.b[1].astype(F32) + b_z[1]).astype(BF), "tp", 2, self.name)

    def result(self):
        a = self.a_sum + self.chain.now(self.a_z).astype(F32)
        b = self.b_sum + self.chain.now(self.b_y).astype(F32)
        return jnp.concatenate([a, b], axis=0)


def local(
    block_in,
    cotangent,
    qkv_weight,
    proj_weight,
    feed_weight,
    down_weight,
    norm_gains,
    qkv_first,
    proj_first,
    feed_first,
    down_first,
    gains_first,
    qkv_second,
    proj_second,
    feed_second,
    down_second,
    gains_second,
):
    xi, zi, ti = lax.axis_index("dp"), lax.axis_index(SP), lax.axis_index("tp")
    nx, nz = lax.axis_size("dp"), lax.axis_size(SP)
    width = block_in.shape[2]
    span = block_in.shape[1]
    length = span * nz * 4
    groups, row_block, columns = qkv_weight.shape
    proj_rows = proj_weight.shape[1]
    units, unit_rows = down_weight.shape[0], down_weight.shape[1]
    feed_columns = feed_weight.shape[2] // 2

    y, c = ti // 2, ti % 2
    chain = Chain()
    now, start, fence = chain.now, chain.start, chain.fence

    at = jnp.stack([xi ^ k for k in range(nx)])

    at_tp = jnp.stack([ti ^ k for k in range(4)])

    x_rows = chain.start_all(block_in, "x_sp")
    qkv_mine = qkv_weight.transpose(1, 0, 2).reshape(row_block, groups * columns).astype(BF)
    qkv_all = lax.all_gather(qkv_mine, ("dp",) + SP, tiled=True)
    fence(qkv_mine)

    gains_low = now(norm_gains).astype(BF)
    gains_sent = {k: start(gains_low, SP, k, "gains_sp") for k in (1, 2, 3)}
    proj_blocks = now(proj_weight).astype(BF)
    proj_blocks = jnp.tile(proj_blocks[None], (nz, 1, 1, 1))
    fence(proj_blocks)

    gate_blocks = now(feed_weight[0]).astype(BF).reshape(row_block, 2, feed_columns)
    gate_blocks = jnp.tile(gate_blocks.transpose(1, 0, 2), (nz // 2, 1, 1))
    up_blocks = now(feed_weight[1]).astype(BF).reshape(row_block, 2, feed_columns)
    up_blocks = jnp.tile(up_blocks.transpose(1, 0, 2), (nz // 2, 1, 1))
    down_blocks = now(down_weight).astype(BF).reshape(2, units // 2, unit_rows, width)
    down_blocks = jnp.tile(down_blocks, (nz // 2, 1, 1, 1))

    x_rows = now(x_rows)
    x_y, x_c = start(x_rows, "tp", 2, "x_y"), start(x_rows, "tp", 1, "x_c")
    gains_sp = place({0: gains_low, **{k: now(v) for k, v in gains_sent.items()}}, zi)
    gains_dp = chain.start_dp(gains_sp, "gains_dp")
    fence()
    proj_own = chain.start_all(proj_blocks, "proj_sp")
    fence()
    x_y = now(x_y)
    x_yc = start(x_y, "tp", 1, "x_yc")
    fence(gate_blocks, up_blocks, down_blocks)

    gains_all = place({0: gains_sp, **{k + 1: now(v) for k, v in enumerate(gains_dp)}}, xi)
    gain_values = gains_all.transpose(2, 0, 1, 3).reshape(2, width).astype(F32)
    x_yc = now(x_yc)
    proj_own = now(proj_own)
    proj_got = chain.start_dp(proj_own, "proj_dp")
    gate_own = chain.start_all(after(gate_blocks, proj_own), "gate_sp")
    fence(x_yc, gain_values)

    def norm(rows, gain):
        inverse = lax.rsqrt(jnp.mean(rows * rows, axis=-1, keepdims=True) + NORM_EPSILON)
        unit = rows * inverse
        return unit, inverse, (unit * gain).astype(BF)

    normed_one, projected = project(at_tp, [x_rows, now(x_c), x_y, x_yc], gain_values[:1], qkv_all)
    cosine, sine = tables(length)
    qkv, context, logs = attend(chain.gate(projected), cosine, sine, groups)
    chain.passed(context)

    proj_all = order_units([proj_own] + [now(v) for v in proj_got], at, nz)
    attn_part = mm(context, proj_all).astype(BF).reshape(nz, 2, 2, span, width)
    attn_core = start(pick(attn_part, 1 - c, 2), "tp", 1, "attn_c")
    fence()
    attn_sum = (pick(attn_part, c, 2).astype(F32) + now(attn_core).astype(F32)).astype(BF)
    attn_y = start(pick(attn_sum, 1 - y, 1), "tp", 2, "attn_y")
    fence()
    gate_own = now(gate_own)
    gate_got = chain.start_dp(gate_own, "gate_dp")
    up_own = chain.start_all(after(up_blocks, gate_own), "up_sp")
    fence()

    attn_mine = (pick(attn_sum, y, 1).astype(F32) + now(attn_y).astype(F32)).reshape(-1, width)
    inputs = x_rows.astype(F32).reshape(-1, width)
    hidden_one = inputs + attn_mine
    unit_two, inverse_two, normed_two = norm(hidden_one, gain_values[1])
    gather = Gather(chain, normed_two, "normed")
    fence()
    gather.second()
    gather.near_core()
    fence()
    up_own = now(up_own)
    up_got = chain.start_dp(up_own, "up_dp")
    dy_rows = chain.start_all(after(cotangent, up_own), "dy_sp")
    fence()
    gather.far_core()
    gate_got = [chain.take(v) for v in gate_got]
    fence()

    def flat(arrays):
        return [v.reshape(-1, v.shape[-1]) for v in arrays]

    dy_rows = now(dy_rows)
    dy_gather = Gather(chain, dy_rows.reshape(-1, width), "dy")
    down_own = chain.start_all(after(down_blocks, dy_rows), "down_sp")
    gates = flat([gate_own] + gate_got)
    first, *others = gather.result()
    gate, normed_all = gate_rows(at, [chain.gate(first)] + others, gates)
    chain.passed(gate)

    dy_gather.second()
    ups = flat([up_own] + [chain.take(v) for v in up_got])
    hidden, activated, slope = up_rows(at, chain.gate(normed_all), gate, ups)
    chain.passed(hidden)

    dy_gather.near_core()
    dy_gather.far_core()
    fence()
    down_own = now(down_own)
    down_got = chain.start_dp(down_own, "down_dp")
    fence()
    dy_all = jnp.concatenate(dy_gather.result(), axis=0)
    down_part = mm_tn(hidden, dy_all).astype(BF)
    down_part = down_part.reshape(units // 2, nx, nz, unit_rows, width).transpose(1, 2, 0, 3, 4)

    def to_dp(parts, name):
        return [start(pick(parts, xi ^ k, 0), "dp", k, name) for k in range(1, nx)]

    def sum_dp(parts, got):
        total = pick(parts, xi, 0).astype(F32)
        for block in got:
            total = total + now(block).astype(F32)
        return total.astype(BF)

    down_dp = to_dp(down_part, "down_grad_dp")
    fence()

    down_all = order_units([down_own] + [now(v) for v in down_got], at, nz)
    grad_gate, grad_up, grad_other = ffn_back(
        at, dy_all, activated, slope, down_all, gates, ups, 1, None
    )
    chain.passed(grad_other)
    reduce = Reduce(chain, grad_other, "normed_grad")
    grad_gate, grad_up, grad_mine = ffn_back(
        at, chain.gate(dy_all), activated, slope, down_all, gates, ups, 0, (grad_gate, grad_up)
    )
    chain.passed(grad_mine)

    reduce.first(grad_mine)
    fence()

    gate_part = mm_tn(now(normed_all), grad_gate).astype(BF)
    gate_part = gate_part.reshape(nx, nz, row_block, feed_columns)
    gate_dp = to_dp(gate_part, "gate_grad_dp")
    fence()

    reduce.second()
    fence()
    down_moved = chain.start_all(sum_dp(down_part, down_dp), "down_grad_sp")
    fence()
    up_part = mm_tn(now(normed_all), grad_up).astype(BF).reshape(nx, nz, row_block, feed_columns)
    up_dp = to_dp(up_part, "up_grad_dp")
    fence()

    grad_normed_two = reduce.result()
    grad_unit = grad_normed_two * gain_values[1]
    row_inner = jnp.mean(grad_unit * unit_two, axis=-1, keepdims=True)
    dy_own = dy_rows.astype(F32).reshape(-1, width)
    back_two = inverse_two * (grad_unit - unit_two * row_inner)
    gain_two_part = jnp.sum(grad_normed_two * unit_two, axis=0)
    grad_hidden_one = dy_own + back_two
    rows_mine = grad_hidden_one.astype(BF).reshape(nz, span, width)
    rows_y, rows_c = start(rows_mine, "tp", 2, "rows_y"), start(rows_mine, "tp", 1, "rows_c")
    fence()
    down_moved = chain.take(down_moved)
    gate_sum = sum_dp(gate_part, gate_dp)
    gate_moved = chain.start_all(after(gate_sum, down_moved), "gate_grad_sp")
    fence()
    out_part = mm(now(hidden), down_all).astype(BF)
    out_rows = out_part.shape[0] // 2
    out_reduce = Reduce(chain, out_part[out_rows:], "out")
    fence()
    rows_y = now(rows_y)
    rows_yc = start(rows_y, "tp", 1, "rows_yc")
    fence()

    grad_rows, grad_context = context_grad(
        at_tp, [rows_mine, now(rows_c), rows_y, now(rows_yc)], proj_all
    )
    out_reduce.first(out_part[:out_rows])
    grad_projected = attend_back(qkv, chain.gate(grad_context), logs, cosine, sine, groups)
    chain.passed(grad_projected)

    gate_moved = chain.take(gate_moved)
    up_sum = sum_dp(up_part, up_dp)
    up_moved = chain.start_all(after(up_sum, gate_moved), "up_grad_sp")
    dn_part = mm_nt(grad_projected, qkv_all).astype(BF).reshape(nz, 2, 2, span, width)
    dn_core = start(pick(dn_part, 1 - c, 2), "tp", 1, "dn_c")
    fence()
    dn_sum = (pick(dn_part, c, 2).astype(F32) + now(dn_core).astype(F32)).astype(BF)
    dn_y = start(pick(dn_sum, 1 - y, 1), "tp", 2, "dn_y")
    fence()
    qkv_part = mm_tn(now(normed_one), grad_projected).astype(BF)
    qkv_grad = lax.psum_scatter(qkv_part, ("dp",) + SP, tiled=True)
    out_reduce.second()
    fence(qkv_part)
    proj_part = mm_tn(context, now(grad_rows)).astype(BF)
    proj_part = proj_part.reshape(groups, nx, nz, proj_rows, width).transpose(1, 2, 0, 3, 4)
    proj_dp = to_dp(proj_part, "proj_grad_dp")
    fence()

    grad_normed_one = (pick(dn_sum, y, 1).astype(F32) + now(dn_y).astype(F32)).reshape(-1, width)
    inverse_one = lax.rsqrt(jnp.mean(inputs * inputs, axis=-1, keepdims=True) + NORM_EPSILON)
    unit_one = inputs * inverse_one
    grad_unit = grad_normed_one * gain_values[0]
    row_inner = jnp.mean(grad_unit * unit_one, axis=-1, keepdims=True)
    back_one = inverse_one * (grad_unit - unit_one * row_inner)
    gain_one_part = jnp.sum(grad_normed_one * unit_one, axis=0)
    input_delta = (back_two + back_one).astype(BF).reshape(nz, span, width)
    gains_part = jnp.stack([gain_one_part, gain_two_part])
    gains_c = start(gains_part, "tp", 1, "gains_c")
    up_moved = chain.take(up_moved)
    input_moved = chain.start_all(after(input_delta, up_moved), "input_sp")
    fence()

    def halves(blocks, axis):
        blocks = [blocks[i].astype(F32) for i in range(nz)]
        parity = [sum(blocks[i] for i in range(p, nz, 2)) for p in range(2)]
        return jnp.concatenate(parity, axis=axis)

    gains_part = gains_part + now(gains_c)
    gains_y = start(gains_part, "tp", 2, "gains_y")
    block_delta = (attn_mine + out_reduce.result()).astype(BF).reshape(nz, span, width)
    down_grad = halves(now(down_moved), 0)
    down_new, down_first_new, down_second_new = adamw(
        down_weight, down_grad, down_first, down_second, DOWN_RATE, WEIGHT_DECAY
    )
    proj_sum = sum_dp(proj_part, proj_dp)
    fence(block_delta, down_new, proj_sum)

    gains_part = (gains_part + now(gains_y)).reshape(2, nx, nz, row_block).transpose(1, 2, 0, 3)
    gains_dp = to_dp(gains_part, "gains_dp")
    feed_grad = jnp.stack([halves(gate_moved, 1), halves(up_moved, 1)])
    feed_new, feed_first_new, feed_second_new = adamw(
        now(feed_weight), feed_grad, feed_first, feed_second, FEED_RATE, WEIGHT_DECAY
    )
    input_moved = chain.take(input_moved)
    proj_moved = chain.start_all(after(proj_sum, input_moved), "proj_grad_sp")
    fence(feed_new)

    gains_sum = pick(gains_part, xi, 0)
    for block in gains_dp:
        gains_sum = gains_sum + now(block)
    gains_moved = {k: start(pick(gains_sum, zi ^ k, 0), SP, k, "gains_sp") for k in (1, 2, 3)}
    input_grad = cotangent.astype(F32) + input_moved.astype(F32)
    proj_moved = chain.take(proj_moved).astype(F32)
    proj_grad = proj_moved[0] + proj_moved[1] + proj_moved[2] + proj_moved[3]
    block_moved = chain.start_all(after(block_delta, proj_moved), "block_sp")
    fence(input_grad)
    qkv_grad = now(qkv_grad).reshape(row_block, groups, columns).transpose(1, 0, 2)
    qkv_grad = after(qkv_grad).astype(F32)
    gains_grad = pick(gains_sum, zi, 0)
    for block in gains_moved.values():
        gains_grad = gains_grad + now(block)
    block_out = block_in.astype(F32) + now(block_moved).astype(F32)

    qkv_new, qkv_first_new, qkv_second_new = adamw(
        qkv_weight, qkv_grad, qkv_first, qkv_second, QKV_RATE, WEIGHT_DECAY
    )
    proj_new, proj_first_new, proj_second_new = adamw(
        proj_weight, proj_grad, proj_first, proj_second, PROJ_RATE, WEIGHT_DECAY
    )
    gains_new, gains_first_new, gains_second_new = adamw(
        norm_gains, gains_grad, gains_first, gains_second, GAIN_RATE, 0.0
    )
    return (
        block_out,
        input_grad,
        qkv_grad,
        proj_grad,
        feed_grad,
        down_grad,
        gains_grad,
        qkv_new,
        proj_new,
        feed_new,
        down_new,
        gains_new,
        qkv_first_new,
        proj_first_new,
        feed_first_new,
        down_first_new,
        gains_first_new,
        qkv_second_new,
        proj_second_new,
        feed_second_new,
        down_second_new,
        gains_second_new,
    )


def solution(mesh):
    sizes = mesh.shape
    mesh = Mesh(
        mesh.devices.reshape(sizes["dp"], sizes["sp"] // 2, 2, sizes["tp"]), ("dp",) + SP + ("tp",)
    )
    rows = P("dp", SP + ("tp",), None)
    heads = P("tp", ("dp",) + SP, None)
    feed = P(None, ("dp",) + SP, "tp")
    gains = P(None, ("dp",) + SP)
    params = (heads, heads, feed, heads, gains)
    return jax.shard_map(
        local,
        mesh=mesh,
        in_specs=(rows, rows) + params * 3,
        out_specs=(rows, rows) + params * 4,
        check_vma=False,
    )
```

```python
import functools

import jax
import jax.numpy as jnp
from jax import lax
from jax.experimental import pallas as pl
from jax.experimental.pallas import tpu as pltpu
from jax.sharding import Mesh, PartitionSpec as P

HD = 64
QPK = 4
STEP = 10
LANES = 128
VMEM_LIMIT = 56 * 1024 * 1024
SP = ("sp_pair", "sp_in_pair")


NORM_EPSILON = 1e-05
ROPE_BASE = 500000.0
MASKED = -1e30
BETA_ONE = 0.9
BETA_TWO = 0.95
ADAM_EPSILON = 1e-08
WEIGHT_DECAY = 0.1
QKV_RATE = 0.05
PROJ_RATE = 0.4
FEED_RATE = 0.05
DOWN_RATE = 0.03
GAIN_RATE = 0.5

BF = jnp.bfloat16
F32 = jnp.float32
HEAVY = pl.CostEstimate(flops=1 << 36, bytes_accessed=1 << 20, transcendentals=0)
LIGHT = pl.CostEstimate(flops=1 << 32, bytes_accessed=1 << 20, transcendentals=0)


def after(value, *earlier):
    return lax.optimization_barrier((value,) + earlier)[0]


def swap(value, axis, mask):
    return lax.ppermute(value, axis, [(i, i ^ mask) for i in range(lax.axis_size(axis))])


def pick(value, index, axis):
    return lax.dynamic_index_in_dim(value, index, axis, keepdims=False)


def dot(left, right, dims):
    return lax.dot_general(left, right, ((dims[0], dims[1]), ((), ())), preferred_element_type=F32)


def mm(left, right):
    return dot(left, right, ((1,), (0,)))


def mm_nt(left, right):
    return dot(left, right, ((1,), (1,)))


def mm_tn(left, right):
    return dot(left, right, ((0,), (0,)))


def turn(block, cosine, sine):
    lane = lax.broadcasted_iota(jnp.int32, block.shape, 1)
    ahead = pltpu.roll(block, LANES - HD // 2, 1)
    behind = pltpu.roll(block, HD // 2, 1)
    return block * cosine + jnp.where(lane % HD < HD // 2, ahead, behind) * sine

def key_tables(cosine, sine):
    lane = lax.broadcasted_iota(jnp.int32, cosine.shape, 1)
    return jnp.where(lane < HD, cosine, 1.0), jnp.where(lane < HD, sine, 0.0)

def attend_kernel(tile, p_ref, cos_ref, sin_ref, qkv_ref, ctx_ref, log_ref, q_s, k_s, vt_s, c_s):
    length = p_ref.shape[0]
    cosine, sine = cos_ref[...], sin_ref[...]
    for b in range(QPK // 2):
        block = turn(p_ref[:, b * LANES : (b + 1) * LANES], cosine, sine).astype(BF) * BF(HD ** -0.5)
        qkv_ref[:, b * LANES : (b + 1) * LANES] = block
        q_s[2 * b] = block[:, :HD]
        q_s[2 * b + 1] = block[:, HD:]
    k_cos, k_sin = key_tables(cosine, sine)
    block = turn(p_ref[:, QPK * HD :], k_cos, k_sin)
    qkv_ref[:, QPK * HD :] = block.astype(BF)
    k_s[...] = block[:, :HD].astype(BF)
    vt_s[...] = jnp.transpose(block)[HD:].astype(BF)
    keep = lax.broadcasted_iota(jnp.int32, (tile, tile), 0) <= lax.broadcasted_iota(jnp.int32, (tile, tile), 1)

    def head(n, carry):
        for t in range(length // tile):
            before, here = t * tile, slice(t * tile, (t + 1) * tile)
            q = q_s[n, here, :]
            s_here = jnp.where(keep, mm_nt(k_s[here, :], q), MASKED)
            peak = jnp.max(s_here, axis=0, keepdims=True)
            if t:
                s_before = mm_nt(k_s[:before, :], q)
                peak = jnp.maximum(peak, jnp.max(s_before, axis=0, keepdims=True))
            e_here = jnp.exp(s_here - peak)
            total = jnp.sum(e_here, axis=0, keepdims=True)
            if t:
                e_before = jnp.exp(s_before - peak)
                total = total + jnp.sum(e_before, axis=0, keepdims=True)
            scale = 1.0 / total
            out = mm(vt_s[:, here], (e_here * scale).astype(BF))
            if t:
                out = out + mm(vt_s[:, :before], (e_before * scale).astype(BF))
            c_s[pl.ds(pl.multiple_of(n * HD, HD), HD), here] = out
            log_ref[0, pl.ds(n, 1), here] = peak + jnp.log(total)
        return carry

    lax.fori_loop(0, QPK, head, 0)
    ctx_ref[...] = jnp.transpose(c_s[...]).astype(BF)

def attend(projected, cosine, sine, groups, tile=256):
    length, columns = projected.shape[0], projected.shape[1] // groups
    qw = QPK * HD
    table = pl.BlockSpec((length, LANES), lambda g: (0, 0))
    return pl.pallas_call(
        functools.partial(attend_kernel, tile),
        grid=(groups,),
        in_specs=[pl.BlockSpec((length, columns), lambda g: (0, g)), table, table],
        out_specs=[
            pl.BlockSpec((length, columns), lambda g: (0, g)),
            pl.BlockSpec((length, qw), lambda g: (0, g)),
            pl.BlockSpec((1, QPK, length), lambda g: (g, 0, 0)),
        ],
        out_shape=[
            jax.ShapeDtypeStruct((length, groups * columns), BF),
            jax.ShapeDtypeStruct((length, groups * qw), BF),
            jax.ShapeDtypeStruct((groups, QPK, length), F32),
        ],
        scratch_shapes=[
            pltpu.VMEM((QPK, length, HD), BF),
            pltpu.VMEM((length, HD), BF),
            pltpu.VMEM((HD, length), BF),
            pltpu.VMEM((qw, length), F32),
        ],
        compiler_params=pltpu.CompilerParams(vmem_limit_bytes=VMEM_LIMIT),
        cost_estimate=HEAVY,
        name="attend",
    )(projected, cosine, sine)

def attend_back_kernel(tile, qkv_ref, grad_ref, log_ref, cos_ref, sin_ref, *refs):
    out_ref, q_s, k_s, v_s, kt_s, g_s, dk_s, dv_s, dq_s = refs[-9:]
    length = qkv_ref.shape[0]
    for b in range(QPK // 2):
        lanes = slice(b * LANES, (b + 1) * LANES)
        block, grad = qkv_ref[:, lanes], grad_ref[:, lanes]
        q_s[2 * b], q_s[2 * b + 1] = block[:, :HD], block[:, HD:]
        g_s[2 * b], g_s[2 * b + 1] = grad[:, :HD], grad[:, HD:]
    block = qkv_ref[:, QPK * HD :]
    k_s[...] = block[:, :HD]
    v_s[...] = block[:, HD:]
    kt_s[...] = jnp.transpose(block.astype(F32))[:HD].astype(BF)
    dk_s[...] = jnp.zeros_like(dk_s)
    dv_s[...] = jnp.zeros_like(dv_s)
    keep = lax.broadcasted_iota(jnp.int32, (tile, tile), 0) <= lax.broadcasted_iota(jnp.int32, (tile, tile), 1)

    def head(n, carry):
        for t in range(length // tile):
            before, here = t * tile, slice(t * tile, (t + 1) * tile)
            upto = slice(0, (t + 1) * tile)
            q, g = q_s[n, here, :], g_s[n, here, :]
            log = log_ref[0, pl.ds(n, 1), here]
            a_here = jnp.exp(jnp.where(keep, mm_nt(k_s[here, :], q), MASKED) - log)
            d_here = mm_nt(v_s[here, :], g)
            inner = jnp.sum(a_here * d_here, axis=0, keepdims=True)
            if t:
                a_before = jnp.exp(mm_nt(k_s[:before, :], q) - log)
                d_before = mm_nt(v_s[:before, :], g)
                inner = inner + jnp.sum(a_before * d_before, axis=0, keepdims=True)
            s_here = (a_here * (d_here - inner)).astype(BF)
            dq = mm(kt_s[:, here], s_here)
            dk_s[here, :] += mm(s_here, q)
            dv_s[here, :] += mm(a_here.astype(BF), g)
            if t:
                s_before = (a_before * (d_before - inner)).astype(BF)
                dq = dq + mm(kt_s[:, :before], s_before)
                dk_s[:before, :] += mm(s_before, q)
                dv_s[:before, :] += mm(a_before.astype(BF), g)
            dq_s[pl.ds(pl.multiple_of(n * HD, HD), HD), here] = dq * HD ** -0.5
        return carry

    lax.fori_loop(0, QPK, head, 0)
    cosine, sine = cos_ref[...], sin_ref[...]
    grad = jnp.transpose(dq_s[...])
    for b in range(QPK // 2):
        lanes = slice(b * LANES, (b + 1) * LANES)
        out_ref[:, lanes] = turn(grad[:, lanes], cosine, -sine).astype(BF)
    k_cos, k_sin = key_tables(cosine, sine)
    block = jnp.concatenate([dk_s[...], dv_s[...]], axis=1)
    out_ref[:, QPK * HD :] = turn(block, k_cos, -k_sin).astype(BF)

def attend_back(qkv, grad, log, cosine, sine, groups, group, earlier, tile=256):
    length, columns = qkv.shape[0], qkv.shape[1] // groups
    qw = QPK * HD
    table = pl.BlockSpec((length, LANES), lambda g: (0, 0))
    held = () if earlier is None else (earlier,)
    return pl.pallas_call(
        functools.partial(attend_back_kernel, tile),
        grid=(1,),
        in_specs=[
            pl.BlockSpec((length, columns), lambda g: (0, group)),
            pl.BlockSpec((length, qw), lambda g: (0, group)),
            pl.BlockSpec((1, QPK, length), lambda g: (group, 0, 0)),
            table,
            table,
        ]
        + [pl.BlockSpec(memory_space=pl.ANY)] * len(held),
        out_specs=pl.BlockSpec((length, columns), lambda g: (0, group)),
        out_shape=jax.ShapeDtypeStruct((length, groups * columns), BF),
        scratch_shapes=[
            pltpu.VMEM((QPK, length, HD), BF),
            pltpu.VMEM((length, HD), BF),
            pltpu.VMEM((length, HD), BF),
            pltpu.VMEM((HD, length), BF),
            pltpu.VMEM((QPK, length, HD), BF),
            pltpu.VMEM((length, HD), F32),
            pltpu.VMEM((length, HD), F32),
            pltpu.VMEM((qw, length), F32),
        ],
        input_output_aliases={5: 0} if held else {},
        compiler_params=pltpu.CompilerParams(vmem_limit_bytes=VMEM_LIMIT),
        cost_estimate=HEAVY,
        name="attend_back",
    )(qkv, grad, log, cosine, sine, *held)


def tables(length):
    half = HD // 2
    freq = ROPE_BASE ** (-(jnp.arange(half, dtype=F32) * 2.0 / HD))
    ang = jnp.arange(length).astype(F32)[:, None] * freq[None, :]
    c, s = jnp.cos(ang), jnp.sin(ang)
    return jnp.concatenate([c, c, c, c], 1), jnp.concatenate([-s, s, -s, s], 1)

def by_parts(at_ref, rows_ref, weights):
    depth = weights[0].shape[0]
    total = None
    for k, weight in enumerate(weights):
        rows = rows_ref[:, pl.ds(pl.multiple_of(at_ref[k] * depth, depth), depth)]
        part = mm(rows, weight[...])
        total = part if total is None else total + part
    return total


def gate_kernel(blocks, at_ref, *refs):
    rows_refs, weights, (gate_ref, rows_ref) = refs[:blocks], refs[blocks:-2], refs[-2:]

    @pl.when(pl.program_id(1) == 0)
    def _():
        for t in range(blocks):

            @pl.when(pl.program_id(0) == t)
            def _():
                rows_ref[...] = rows_refs[t][...]

    gate_ref[...] = by_parts(at_ref, rows_ref, weights)


def gate_rows(at, rows, gates, tf=512):
    tm, k = rows[0].shape
    f = gates[0].shape[1]
    parts, blocks = len(gates), len(rows)
    return pl.pallas_call(
        functools.partial(gate_kernel, blocks),
        grid=(blocks, f // tf),
        in_specs=[pl.BlockSpec(memory_space=pltpu.SMEM)]
        + [pl.BlockSpec((tm, k), lambda i, j: (0, 0), pipeline_mode=pl.Buffered(1))] * blocks
        + [pl.BlockSpec((k // parts, tf), lambda i, j: (0, j))] * parts,
        out_specs=[
            pl.BlockSpec((tm, tf), lambda i, j: (i, j)),
            pl.BlockSpec((tm, k), lambda i, j: (i, 0)),
        ],
        out_shape=[
            jax.ShapeDtypeStruct((tm * blocks, f), F32),
            jax.ShapeDtypeStruct((tm * blocks, k), BF),
        ],
        compiler_params=pltpu.CompilerParams(vmem_limit_bytes=VMEM_LIMIT),
        cost_estimate=HEAVY,
        name="gate_rows",
    )(at, *rows, *gates)


def up_kernel(at_ref, rows_ref, gate_ref, *refs):
    weights, (hid_ref, a_ref, b_ref) = refs[:-3], refs[-3:]
    up = by_parts(at_ref, rows_ref, weights)
    gate = gate_ref[...]
    s = jax.nn.sigmoid(gate)
    act = gate * s
    hid_ref[...] = (act * up).astype(BF)
    a_ref[...] = act
    b_ref[...] = up * s * (1.0 + gate * (1.0 - s))


def up_rows(at, rows, gate, ups, tm=512, tf=512):
    m, k = rows.shape
    f = gate.shape[1]
    parts = len(ups)
    o = pl.BlockSpec((tm, tf), lambda i, j: (i, j))
    return pl.pallas_call(
        up_kernel,
        grid=(m // tm, f // tf),
        in_specs=[
            pl.BlockSpec(memory_space=pltpu.SMEM),
            pl.BlockSpec((tm, k), lambda i, j: (i, 0)),
            o,
        ]
        + [pl.BlockSpec((k // parts, tf), lambda i, j: (0, j))] * parts,
        out_specs=[o, o, o],
        out_shape=[
            jax.ShapeDtypeStruct((m, f), BF),
            jax.ShapeDtypeStruct((m, f), F32),
            jax.ShapeDtypeStruct((m, f), F32),
        ],
        compiler_params=pltpu.CompilerParams(vmem_limit_bytes=VMEM_LIMIT),
        cost_estimate=HEAVY,
        name="up_rows",
    )(at, rows, gate, *ups)


def ffn_back_kernel(tf, downs, parts, at_ref, dy_ref, a_ref, b_ref, *refs):
    d_refs, weights, (dg_ref, du_ref, dn_ref) = refs[:downs], refs[downs : downs + 2 * parts], refs[-3:]
    dy = dy_ref[...]
    each = d_refs[0].shape[0]
    for j in range(downs * each // tf):
        c = slice(j * tf, (j + 1) * tf)
        row = j * tf % each
        dh = mm_nt(dy, d_refs[j * tf // each][row : row + tf, :])
        dg_ref[:, c] = (dh * b_ref[:, c]).astype(BF)
        du_ref[:, c] = (dh * a_ref[:, c]).astype(BF)
    depth = weights[0].shape[0]
    for k in range(parts):
        part = mm_nt(dg_ref[...], weights[k][...]) + mm_nt(du_ref[...], weights[parts + k][...])
        dn_ref[:, pl.ds(pl.multiple_of(at_ref[k] * depth, depth), depth)] = part.astype(BF)


def ffn_back(at, dy, a, b, downs, gates, ups, part, earlier, tm=256, tf=256):
    m, k = dy.shape
    f = gates[0].shape[1]
    parts = len(gates)
    steps = m // 2 // tm
    inner = pl.BlockSpec((tm, f), lambda i: (i + part * steps, 0))
    rows = pl.BlockSpec((tm, k), lambda i: (i + part * steps, 0))

    def whole(shape):
        return pl.BlockSpec(shape, lambda i: (0, 0), pipeline_mode=pl.Buffered(1))

    held = () if earlier is None else earlier
    return pl.pallas_call(
        functools.partial(ffn_back_kernel, tf, len(downs), parts),
        grid=(steps,),
        in_specs=[pl.BlockSpec(memory_space=pltpu.SMEM), rows, inner, inner]
        + [whole((f // len(downs), k))] * len(downs)
        + [whole((k // parts, f))] * (2 * parts)
        + [pl.BlockSpec(memory_space=pl.ANY)] * len(held),
        out_specs=[inner, inner, pl.BlockSpec((tm, k), lambda i: (i, 0))],
        out_shape=[
            jax.ShapeDtypeStruct((m, f), BF),
            jax.ShapeDtypeStruct((m, f), BF),
            jax.ShapeDtypeStruct((m // 2, k), BF),
        ],
        input_output_aliases={4 + len(downs) + 2 * parts + i: i for i in range(len(held))},
        compiler_params=pltpu.CompilerParams(vmem_limit_bytes=VMEM_LIMIT),
        cost_estimate=HEAVY,
        name="ffn_back",
    )(at, dy, a, b, *downs, *gates, *ups, *held)


def project_kernel(pieces, at_ref, *refs):
    piece_refs, (gain_ref, w_ref, n_ref, p_ref, x_s) = refs[:pieces], refs[pieces:]
    rows = piece_refs[0].shape[1]
    for k in range(pieces):
        x_s[pl.ds(pl.multiple_of(at_ref[k] * rows, rows), rows), :] = piece_refs[k][0]
    x = x_s[...].astype(F32)
    inverse = lax.rsqrt(jnp.mean(x * x, axis=-1, keepdims=True) + NORM_EPSILON)
    n_ref[...] = (x * inverse * gain_ref[...]).astype(BF)
    p_ref[...] = mm(n_ref[...], w_ref[...])


def project(at, pieces, gain, weights):
    b, r, d = pieces[0].shape
    c = weights.shape[1]
    rows = r * len(pieces)
    return pl.pallas_call(
        functools.partial(project_kernel, len(pieces)),
        grid=(b,),
        in_specs=[pl.BlockSpec(memory_space=pltpu.SMEM)]
        + [pl.BlockSpec((1, r, d), lambda i: (i, 0, 0))] * len(pieces)
        + [
            pl.BlockSpec((1, d), lambda i: (0, 0)),
            pl.BlockSpec((d, c), lambda i: (0, 0), pipeline_mode=pl.Buffered(1)),
        ],
        out_specs=[pl.BlockSpec((rows, d), lambda i: (i, 0)), pl.BlockSpec((rows, c), lambda i: (i, 0))],
        out_shape=[jax.ShapeDtypeStruct((b * rows, d), BF), jax.ShapeDtypeStruct((b * rows, c), F32)],
        scratch_shapes=[pltpu.VMEM((rows, d), BF)],
        compiler_params=pltpu.CompilerParams(vmem_limit_bytes=VMEM_LIMIT),
        cost_estimate=LIGHT,
        name="project",
    )(at, *pieces, gain, weights)


def context_kernel(pieces, at_ref, *refs):
    piece_refs, (w_ref, rows_ref, c_ref) = refs[:pieces], refs[pieces:]
    rows = piece_refs[0].shape[1]
    for k in range(pieces):
        rows_ref[pl.ds(pl.multiple_of(at_ref[k] * rows, rows), rows), :] = piece_refs[k][0]
    c_ref[...] = mm_nt(rows_ref[...], w_ref[...]).astype(BF)


def context_grad(at, pieces, weights):
    b, r, d = pieces[0].shape
    c = weights.shape[0]
    rows = r * len(pieces)
    return pl.pallas_call(
        functools.partial(context_kernel, len(pieces)),
        grid=(b,),
        in_specs=[pl.BlockSpec(memory_space=pltpu.SMEM)]
        + [pl.BlockSpec((1, r, d), lambda i: (i, 0, 0))] * len(pieces)
        + [pl.BlockSpec((c, d), lambda i: (0, 0), pipeline_mode=pl.Buffered(1))],
        out_specs=[pl.BlockSpec((rows, d), lambda i: (i, 0)), pl.BlockSpec((rows, c), lambda i: (i, 0))],
        out_shape=[jax.ShapeDtypeStruct((b * rows, d), BF), jax.ShapeDtypeStruct((b * rows, c), BF)],
        compiler_params=pltpu.CompilerParams(vmem_limit_bytes=VMEM_LIMIT),
        cost_estimate=LIGHT,
        name="context_grad",
    )(at, *pieces, weights)


def out_kernel(hid_ref, *refs):
    weights, out_ref = refs[:-1], refs[-1]
    each = weights[0].shape[0]
    total = None
    for k, weight in enumerate(weights):
        part = mm(hid_ref[:, k * each : (k + 1) * each], weight[...])
        total = part if total is None else total + part
    out_ref[...] = total.astype(BF)


def out_rows(hidden, weights, tm=256):
    m, f = hidden.shape
    each, d = weights[0].shape
    return pl.pallas_call(
        out_kernel,
        grid=(m // tm,),
        in_specs=[pl.BlockSpec((tm, f), lambda i: (i, 0))]
        + [pl.BlockSpec((each, d), lambda i: (0, 0), pipeline_mode=pl.Buffered(1))] * len(weights),
        out_specs=pl.BlockSpec((tm, d), lambda i: (i, 0)),
        out_shape=jax.ShapeDtypeStruct((m, d), BF),
        compiler_params=pltpu.CompilerParams(vmem_limit_bytes=VMEM_LIMIT),
        cost_estimate=LIGHT,
        name="out_rows",
    )(hidden, *weights)


def join_kernel(count, *refs):
    rows = refs[0].shape[0]
    for k in range(count):
        refs[count][k * rows : (k + 1) * rows] = refs[k][...]


def join(pieces):
    rows, width = pieces[0].shape
    count = len(pieces)
    tile = width // 4
    return pl.pallas_call(
        functools.partial(join_kernel, count),
        grid=(width // tile,),
        in_specs=[pl.BlockSpec((rows, tile), lambda i: (0, i))] * count,
        out_specs=pl.BlockSpec((rows * count, tile), lambda i: (0, i)),
        out_shape=jax.ShapeDtypeStruct((rows * count, width), pieces[0].dtype),
        compiler_params=pltpu.CompilerParams(vmem_limit_bytes=VMEM_LIMIT),
        name="join",
    )(*pieces)


def collect_kernel(put, parts, at_ref, *refs):
    for k in range(parts):
        put(refs[k], refs[parts], at_ref[k])


def collect(at, pieces, shape, put):
    return pl.pallas_call(
        functools.partial(collect_kernel, put, len(pieces)),
        in_specs=[pl.BlockSpec(memory_space=pltpu.SMEM)]
        + [pl.BlockSpec(memory_space=pltpu.VMEM)] * len(pieces),
        out_specs=pl.BlockSpec(memory_space=pltpu.VMEM),
        out_shape=jax.ShapeDtypeStruct(shape, pieces[0].dtype),
        compiler_params=pltpu.CompilerParams(vmem_limit_bytes=VMEM_LIMIT),
        name="collect",
    )(at, *pieces)


def fence_kernel(x_ref, o_ref):
    o_ref[...] = x_ref[...]


def fence_call(value):
    return pl.pallas_call(
        fence_kernel,
        out_shape=jax.ShapeDtypeStruct(value.shape, value.dtype),
        cost_estimate=HEAVY,
        name="fence",
    )(value)


def adamw(param, grad, first, second, rate, decay):
    first_new = BETA_ONE * first + (1.0 - BETA_ONE) * grad
    second_new = BETA_TWO * second + (1.0 - BETA_TWO) * grad * grad
    first_hat = first_new / (1.0 - BETA_ONE**STEP)
    second_hat = second_new / (1.0 - BETA_TWO**STEP)
    param_new = param - rate * (first_hat / (jnp.sqrt(second_hat) + ADAM_EPSILON) + decay * param)
    return (param_new, first_new, second_new)


class Chain:
    def __init__(self):
        self.token = None
        self.fences = []
        self.begun = []

    def now(self, value):
        return value if self.token is None else after(value, self.token)

    def take(self, value):
        value = self.now(value)
        self.begun.append(value)
        return value

    def start(self, value, axis, mask, name):
        value = self.take(value)
        with jax.named_scope(name):
            return swap(value, axis, mask)

    def start_dp(self, value, name):
        return [self.start(value, "dp", k, name) for k in range(1, lax.axis_size("dp"))]

    def start_all(self, blocks, name):
        blocks = self.take(blocks)
        with jax.named_scope(name):
            return lax.all_to_all(blocks, SP, 0, 0, tiled=True)

    def fence(self, *values):
        self.passed(fence_call(after(jnp.zeros((8, LANES), F32), self.token, *self.fences, *self.begun, *values)
            if self.token is not None else after(jnp.zeros((8, LANES), F32), *self.begun, *values)))
        self.fences = [self.token]

    def passed(self, token):
        self.token = token
        self.begun = []

    def gate(self, value):
        return after(value, self.token, *self.begun)


def order_units(pieces, at, sp):
    _, outer, rows, width = pieces[0].shape
    if rows % 16:
        out = jnp.zeros((outer, len(pieces), sp * rows, width), BF)
        for k, piece in enumerate(pieces):
            piece = piece.transpose(1, 0, 2, 3).reshape(outer, 1, sp * rows, width)
            out = lax.dynamic_update_slice(out, piece, (0, at[k], 0, 0))
        return out.reshape(-1, width)

    def put(piece, out, x):
        for z in range(sp):
            out[:, x, z * rows : (z + 1) * rows] = piece[z]

    return collect(at, pieces, (outer, len(pieces), sp * rows, width), put).reshape(-1, width)


def place(pieces, index):
    out = jnp.zeros((len(pieces),) + pieces[0].shape, pieces[0].dtype)
    for mask, piece in pieces.items():
        out = lax.dynamic_update_index_in_dim(out, piece, index ^ mask, 0)
    return out


class Gather:
    def __init__(self, chain, rows, name):
        self.chain = chain
        self.name = name
        n = rows.shape[0] // 2
        self.a, self.b, self.n = rows[:n], rows[n:], n
        self.a_y = chain.start(self.a, "tp", 2, name)
        self.b_z = chain.start(self.b, SP, 1, name)

    def second(self):
        now, n = self.chain.now, self.n
        self.near = jnp.concatenate([self.a, now(self.a_y), self.b, now(self.b_z)], axis=0)
        self.far_z = self.chain.start(self.near[: 2 * n], SP, 1, self.name)
        self.far_y = self.chain.start(self.near[2 * n :], "tp", 2, self.name)

    def near_core(self):
        self.near_other = self.chain.start(self.near, "tp", 1, self.name)

    def far_core(self):
        now = self.chain.now
        self.far = jnp.concatenate([now(self.far_z), now(self.far_y)], axis=0)
        self.far_other = self.chain.start(self.far, "tp", 1, self.name)

    def result(self):
        now = self.chain.now
        return [self.near, self.far, now(self.near_other), now(self.far_other)]


class Reduce:
    def __init__(self, chain, other, name):
        self.chain = chain
        self.name = name
        self.got = chain.start(other, "tp", 1, name)

    def first(self, mine):
        total = (mine.astype(F32) + self.chain.now(self.got).astype(F32)).astype(BF)
        total = total.reshape(2, 2, 2, -1, total.shape[-1])
        self.a, self.b = (total[0, 0, 0], total[1, 0, 0]), (total[0, 1, 0], total[1, 1, 0])
        self.a_y = self.chain.start(total[:, 0, 1], "tp", 2, self.name)
        self.b_z = self.chain.start(total[:, 1, 1], SP, 1, self.name)

    def second(self):
        a_y, b_z = self.chain.now(self.a_y).astype(F32), self.chain.now(self.b_z).astype(F32)
        self.a_sum = self.a[0].astype(F32) + a_y[0]
        self.b_sum = self.b[0].astype(F32) + b_z[0]
        self.a_z = self.chain.start((self.a[1].astype(F32) + a_y[1]).astype(BF), SP, 1, self.name)
        self.b_y = self.chain.start((self.b[1].astype(F32) + b_z[1]).astype(BF), "tp", 2, self.name)

    def result(self):
        a = self.a_sum + self.chain.now(self.a_z).astype(F32)
        b = self.b_sum + self.chain.now(self.b_y).astype(F32)
        return jnp.concatenate([a, b], axis=0)


def local(
    block_in,
    cotangent,
    qkv_weight,
    proj_weight,
    feed_weight,
    down_weight,
    norm_gains,
    qkv_first,
    proj_first,
    feed_first,
    down_first,
    gains_first,
    qkv_second,
    proj_second,
    feed_second,
    down_second,
    gains_second,
):
    xi, zi, ti = lax.axis_index("dp"), lax.axis_index(SP), lax.axis_index("tp")
    nx, nz = lax.axis_size("dp"), lax.axis_size(SP)
    width = block_in.shape[2]
    span = block_in.shape[1]
    length = span * nz * 4
    groups, row_block, columns = qkv_weight.shape
    proj_rows = proj_weight.shape[1]
    units, unit_rows = down_weight.shape[0], down_weight.shape[1]
    feed_columns = feed_weight.shape[2] // 2

    y, c = ti // 2, ti % 2
    chain = Chain()
    now, start, fence = chain.now, chain.start, chain.fence

    at = jnp.stack([xi ^ k for k in range(nx)])

    at_tp = jnp.stack([ti ^ k for k in range(4)])

    x_rows = chain.start_all(block_in, "x_sp")
    qkv_mine = qkv_weight.transpose(1, 0, 2).reshape(row_block, groups * columns).astype(BF)
    qkv_all = lax.all_gather(qkv_mine, ("dp",) + SP, tiled=True)
    fence(qkv_mine)

    gains_low = now(norm_gains).astype(BF)
    gains_sent = {k: start(gains_low, SP, k, "gains_sp") for k in (1, 2, 3)}
    proj_blocks = now(proj_weight).astype(BF)
    proj_blocks = jnp.tile(proj_blocks[None], (nz, 1, 1, 1))
    fence(proj_blocks)

    gate_blocks = now(feed_weight[0]).astype(BF).reshape(row_block, 2, feed_columns)
    gate_blocks = jnp.tile(gate_blocks.transpose(1, 0, 2), (nz // 2, 1, 1))
    up_blocks = now(feed_weight[1]).astype(BF).reshape(row_block, 2, feed_columns)
    up_blocks = jnp.tile(up_blocks.transpose(1, 0, 2), (nz // 2, 1, 1))
    down_blocks = now(down_weight).astype(BF).reshape(2, units // 2, unit_rows, width)
    down_blocks = jnp.tile(down_blocks, (nz // 2, 1, 1, 1))

    x_rows = now(x_rows)
    x_y, x_c = start(x_rows, "tp", 2, "x_y"), start(x_rows, "tp", 1, "x_c")
    gains_sp = place({0: gains_low, **{k: now(v) for k, v in gains_sent.items()}}, zi)
    gains_dp = chain.start_dp(gains_sp, "gains_dp")
    fence()
    proj_own = chain.start_all(proj_blocks, "proj_sp")
    fence()
    x_y = now(x_y)
    x_yc = start(x_y, "tp", 1, "x_yc")
    fence(gate_blocks, up_blocks, down_blocks)

    gains_all = place({0: gains_sp, **{k + 1: now(v) for k, v in enumerate(gains_dp)}}, xi)
    gain_values = gains_all.transpose(2, 0, 1, 3).reshape(2, width).astype(F32)
    x_yc = now(x_yc)
    proj_own = now(proj_own)
    proj_got = chain.start_dp(proj_own, "proj_dp")
    gate_own = chain.start_all(after(gate_blocks, proj_own), "gate_sp")
    fence(x_yc, gain_values)

    def norm(rows, gain):
        inverse = lax.rsqrt(jnp.mean(rows * rows, axis=-1, keepdims=True) + NORM_EPSILON)
        unit = rows * inverse
        return unit, inverse, (unit * gain).astype(BF)

    normed_one, projected = project(at_tp, [x_rows, now(x_c), x_y, x_yc], gain_values[:1], qkv_all)
    cosine, sine = tables(length)
    qkv, context, logs = attend(chain.gate(projected), cosine, sine, groups)
    chain.passed(context)

    proj_all = order_units([proj_own] + [now(v) for v in proj_got], at, nz)
    attn_part = mm(context, proj_all).astype(BF).reshape(nz, 2, 2, span, width)
    attn_core = start(pick(attn_part, 1 - c, 2), "tp", 1, "attn_c")
    fence()
    attn_sum = (pick(attn_part, c, 2).astype(F32) + now(attn_core).astype(F32)).astype(BF)
    attn_y = start(pick(attn_sum, 1 - y, 1), "tp", 2, "attn_y")
    fence()
    gate_own = now(gate_own)
    gate_got = chain.start_dp(gate_own, "gate_dp")
    up_own = chain.start_all(after(up_blocks, gate_own), "up_sp")
    fence()

    attn_mine = (pick(attn_sum, y, 1).astype(F32) + now(attn_y).astype(F32)).reshape(-1, width)
    inputs = x_rows.astype(F32).reshape(-1, width)
    hidden_one = inputs + attn_mine
    unit_two, inverse_two, normed_two = norm(hidden_one, gain_values[1])
    gather = Gather(chain, normed_two, "normed")
    fence()
    gather.second()
    gather.near_core()
    fence()
    up_own = now(up_own)
    up_got = chain.start_dp(up_own, "up_dp")
    dy_rows = chain.start_all(after(cotangent, up_own), "dy_sp")
    fence()
    gather.far_core()
    gate_got = [chain.take(v) for v in gate_got]
    fence()

    def flat(arrays):
        return [v.reshape(-1, v.shape[-1]) for v in arrays]

    dy_rows = now(dy_rows)
    dy_gather = Gather(chain, dy_rows.reshape(-1, width), "dy")
    fence()
    cut = units // 4
    down_own = [chain.start_all(after(down_blocks[:, :cut], dy_rows), "down_sp")]
    gates = flat([gate_own] + gate_got)
    first, *others = gather.result()
    gate, normed_all = gate_rows(at, [chain.gate(first)] + others, gates)
    chain.passed(gate)

    ups = flat([up_own] + [chain.take(v) for v in up_got])
    down_own[0] = now(down_own[0])
    down_got = [chain.start_dp(down_own[0], "down_dp")]
    down_own.append(chain.start_all(after(down_blocks[:, cut:], down_own[0]), "down_sp"))
    dy_gather.second()
    dy_gather.near_core()
    hidden, activated, slope = up_rows(at, chain.gate(normed_all), gate, ups)
    chain.passed(hidden)

    down_own[1] = now(down_own[1])
    down_got.append(chain.start_dp(down_own[1], "down_dp"))
    dy_gather.far_core()
    fence()
    dy_all = join(dy_gather.result())
    down_part = mm_tn(hidden, dy_all).astype(BF)
    down_part = down_part.reshape(units // 2, nx, nz, unit_rows, width).transpose(1, 2, 0, 3, 4)

    def to_dp(parts, name):
        return [start(pick(parts, xi ^ k, 0), "dp", k, name) for k in range(1, nx)]

    def sum_dp(parts, got):
        total = pick(parts, xi, 0).astype(F32)
        for block in got:
            total = total + now(block).astype(F32)
        return total.astype(BF)

    down_dp = to_dp(down_part, "down_grad_dp")
    fence()
    downs = [
        order_units([own] + [now(v) for v in got], at, nz) for own, got in zip(down_own, down_got)
    ]

    grad_gate, grad_up, grad_other = ffn_back(
        at, chain.gate(dy_all), activated, slope, downs, gates, ups, 1, None
    )
    chain.passed(grad_other)
    reduce = Reduce(chain, grad_other, "normed_grad")
    grad_gate, grad_up, grad_mine = ffn_back(
        at, chain.gate(dy_all), activated, slope, downs, gates, ups, 0, (grad_gate, grad_up)
    )
    chain.passed(grad_mine)

    reduce.first(grad_mine)
    fence()
    gate_part = mm_tn(now(normed_all), grad_gate).astype(BF)
    gate_part = gate_part.reshape(nx, nz, row_block, feed_columns)
    gate_dp = to_dp(gate_part, "gate_grad_dp")
    fence()
    reduce.second()
    fence()
    down_moved = chain.start_all(sum_dp(down_part, down_dp), "down_grad_sp")
    fence()
    up_part = mm_tn(now(normed_all), grad_up).astype(BF).reshape(nx, nz, row_block, feed_columns)
    up_dp = to_dp(up_part, "up_grad_dp")
    fence()

    grad_normed_two = reduce.result()
    grad_unit = grad_normed_two * gain_values[1]
    row_inner = jnp.mean(grad_unit * unit_two, axis=-1, keepdims=True)
    dy_own = dy_rows.astype(F32).reshape(-1, width)
    back_two = inverse_two * (grad_unit - unit_two * row_inner)
    gain_two_part = jnp.sum(grad_normed_two * unit_two, axis=0)
    grad_hidden_one = dy_own + back_two
    rows_mine = grad_hidden_one.astype(BF).reshape(nz, span, width)
    rows_y, rows_c = start(rows_mine, "tp", 2, "rows_y"), start(rows_mine, "tp", 1, "rows_c")
    fence()
    down_moved = chain.take(down_moved)
    gate_sum = sum_dp(gate_part, gate_dp)
    gate_moved = chain.start_all(after(gate_sum, down_moved), "gate_grad_sp")
    fence()
    out_part = out_rows(now(hidden), downs)
    fence(out_part)
    rows_y = now(rows_y)
    rows_yc = start(rows_y, "tp", 1, "rows_yc")
    fence()

    grad_rows, grad_context = context_grad(
        at_tp, [rows_mine, now(rows_c), rows_y, now(rows_yc)], proj_all
    )
    rows_half = out_part.shape[0] // 2
    out_reduce = Reduce(chain, out_part[rows_half:], "out")
    fence(grad_context)
    out_reduce.first(out_part[:rows_half])
    grad_projected = None
    for group in range(groups):
        grad_projected = attend_back(
            qkv, chain.gate(grad_context), logs, cosine, sine, groups, group, grad_projected
        )
        chain.passed(grad_projected)
        if group == 0:
            gate_moved = chain.take(gate_moved)
            up_sum = sum_dp(up_part, up_dp)
            up_moved = chain.start_all(after(up_sum, gate_moved), "up_grad_sp")

    qkv_part = mm_tn(normed_one, now(grad_projected)).astype(BF)
    qkv_grad = lax.psum_scatter(qkv_part, ("dp",) + SP, tiled=True)
    out_reduce.second()
    fence(qkv_part)
    dn_part = mm_nt(now(grad_projected), qkv_all).astype(BF).reshape(nz, 2, 2, span, width)
    dn_core = start(pick(dn_part, 1 - c, 2), "tp", 1, "dn_c")
    fence()
    dn_sum = (pick(dn_part, c, 2).astype(F32) + now(dn_core).astype(F32)).astype(BF)
    dn_y = start(pick(dn_sum, 1 - y, 1), "tp", 2, "dn_y")
    fence()
    proj_part = mm_tn(context, now(grad_rows)).astype(BF)
    proj_part = proj_part.reshape(groups, nx, nz, proj_rows, width).transpose(1, 2, 0, 3, 4)
    proj_dp = to_dp(proj_part, "proj_grad_dp")
    fence()

    grad_normed_one = (pick(dn_sum, y, 1).astype(F32) + now(dn_y).astype(F32)).reshape(-1, width)
    inverse_one = lax.rsqrt(jnp.mean(inputs * inputs, axis=-1, keepdims=True) + NORM_EPSILON)
    unit_one = inputs * inverse_one
    grad_unit = grad_normed_one * gain_values[0]
    row_inner = jnp.mean(grad_unit * unit_one, axis=-1, keepdims=True)
    back_one = inverse_one * (grad_unit - unit_one * row_inner)
    gain_one_part = jnp.sum(grad_normed_one * unit_one, axis=0)
    input_delta = (back_two + back_one).astype(BF).reshape(nz, span, width)
    gains_part = jnp.stack([gain_one_part, gain_two_part])
    gains_c = start(gains_part, "tp", 1, "gains_c")
    fence(input_delta)
    up_moved = chain.take(up_moved)
    input_moved = chain.start_all(after(input_delta, up_moved), "input_sp")
    fence()

    def halves(blocks, axis):
        blocks = [blocks[i].astype(F32) for i in range(nz)]
        parity = [sum(blocks[i] for i in range(p, nz, 2)) for p in range(2)]
        return jnp.concatenate(parity, axis=axis)

    block_delta = (attn_mine + out_reduce.result()).astype(BF).reshape(nz, span, width)
    proj_sum = sum_dp(proj_part, proj_dp)
    gains_part = gains_part + now(gains_c)
    gains_y = start(gains_part, "tp", 2, "gains_y")
    down_grad = halves(now(down_moved), 0)
    down_new, down_first_new, down_second_new = adamw(
        now(down_weight), down_grad, down_first, down_second, DOWN_RATE, WEIGHT_DECAY
    )
    fence(proj_sum, down_new, block_delta)

    input_moved = chain.take(input_moved)
    proj_moved = chain.start_all(after(proj_sum, input_moved), "proj_grad_sp")
    fence()

    gains_part = (gains_part + now(gains_y)).reshape(2, nx, nz, row_block).transpose(1, 2, 0, 3)
    gains_dp = to_dp(gains_part, "gains_dp")
    feed_grad = jnp.stack([halves(now(gate_moved), 1), halves(now(up_moved), 1)])
    feed_new, feed_first_new, feed_second_new = adamw(
        now(feed_weight), feed_grad, feed_first, feed_second, FEED_RATE, WEIGHT_DECAY
    )
    input_grad = now(cotangent).astype(F32) + input_moved.astype(F32)
    fence(feed_new, input_grad)

    proj_moved = chain.take(proj_moved)
    block_moved = chain.start_all(after(block_delta, proj_moved), "block_sp")
    gains_sum = pick(gains_part, xi, 0)
    for block in gains_dp:
        gains_sum = gains_sum + now(block)
    gains_moved = {k: start(pick(gains_sum, zi ^ k, 0), SP, k, "gains_sp") for k in (1, 2, 3)}
    fence()

    proj_grad = sum(now(proj_moved)[i].astype(F32) for i in range(nz))
    qkv_grad = now(qkv_grad).reshape(row_block, groups, columns).transpose(1, 0, 2)
    qkv_grad = after(qkv_grad).astype(F32)
    gains_grad = pick(gains_sum, zi, 0)
    for block in gains_moved.values():
        gains_grad = gains_grad + now(block)
    block_out = block_in.astype(F32) + now(block_moved).astype(F32)

    qkv_new, qkv_first_new, qkv_second_new = adamw(
        qkv_weight, qkv_grad, qkv_first, qkv_second, QKV_RATE, WEIGHT_DECAY
    )
    proj_new, proj_first_new, proj_second_new = adamw(
        proj_weight, proj_grad, proj_first, proj_second, PROJ_RATE, WEIGHT_DECAY
    )
    gains_new, gains_first_new, gains_second_new = adamw(
        norm_gains, gains_grad, gains_first, gains_second, GAIN_RATE, 0.0
    )
    return (
        block_out,
        input_grad,
        qkv_grad,
        proj_grad,
        feed_grad,
        down_grad,
        gains_grad,
        qkv_new,
        proj_new,
        feed_new,
        down_new,
        gains_new,
        qkv_first_new,
        proj_first_new,
        feed_first_new,
        down_first_new,
        gains_first_new,
        qkv_second_new,
        proj_second_new,
        feed_second_new,
        down_second_new,
        gains_second_new,
    )


def solution(mesh):
    sizes = mesh.shape
    mesh = Mesh(
        mesh.devices.reshape(sizes["dp"], sizes["sp"] // 2, 2, sizes["tp"]), ("dp",) + SP + ("tp",)
    )
    rows = P("dp", SP + ("tp",), None)
    heads = P("tp", ("dp",) + SP, None)
    feed = P(None, ("dp",) + SP, "tp")
    gains = P(None, ("dp",) + SP)
    params = (heads, heads, feed, heads, gains)
    return jax.shard_map(
        local,
        mesh=mesh,
        in_specs=(rows, rows) + params * 3,
        out_specs=(rows, rows) + params * 4,
        check_vma=False,
    )
```

```python
import functools

import jax
import jax.numpy as jnp
from jax import lax
from jax.experimental import pallas as pl
from jax.experimental.pallas import tpu as pltpu
from jax.sharding import Mesh, PartitionSpec as P

HD = 64
QPK = 4
STEP = 10
LANES = 128
VMEM_LIMIT = 56 * 1024 * 1024
SP = ("sp_pair", "sp_in_pair")


NORM_EPSILON = 1e-05
ROPE_BASE = 500000.0
MASKED = -1e30
BETA_ONE = 0.9
BETA_TWO = 0.95
ADAM_EPSILON = 1e-08
WEIGHT_DECAY = 0.1
QKV_RATE = 0.05
PROJ_RATE = 0.4
FEED_RATE = 0.05
DOWN_RATE = 0.03
GAIN_RATE = 0.5

BF = jnp.bfloat16
F32 = jnp.float32
HEAVY = pl.CostEstimate(flops=1 << 36, bytes_accessed=1 << 20, transcendentals=0)
LIGHT = pl.CostEstimate(flops=1 << 32, bytes_accessed=1 << 20, transcendentals=0)


def after(value, *earlier):
    return lax.optimization_barrier((value,) + earlier)[0]


def swap(value, axis, mask):
    return lax.ppermute(value, axis, [(i, i ^ mask) for i in range(lax.axis_size(axis))])


def pick(value, index, axis):
    return lax.dynamic_index_in_dim(value, index, axis, keepdims=False)


def dot(left, right, dims):
    return lax.dot_general(left, right, ((dims[0], dims[1]), ((), ())), preferred_element_type=F32)


def mm(left, right):
    return dot(left, right, ((1,), (0,)))


def mm_nt(left, right):
    return dot(left, right, ((1,), (1,)))


def mm_tn(left, right):
    return dot(left, right, ((0,), (0,)))


def turn(block, cosine, sine):
    lane = lax.broadcasted_iota(jnp.int32, block.shape, 1)
    ahead = pltpu.roll(block, LANES - HD // 2, 1)
    behind = pltpu.roll(block, HD // 2, 1)
    return block * cosine + jnp.where(lane % HD < HD // 2, ahead, behind) * sine

def key_tables(cosine, sine):
    lane = lax.broadcasted_iota(jnp.int32, cosine.shape, 1)
    return jnp.where(lane < HD, cosine, 1.0), jnp.where(lane < HD, sine, 0.0)

def attend_kernel(tile, p_ref, cos_ref, sin_ref, qkv_ref, ctx_ref, log_ref, q_s, k_s, vt_s, c_s):
    length = p_ref.shape[0]
    cosine, sine = cos_ref[...], sin_ref[...]
    for b in range(QPK // 2):
        block = turn(p_ref[:, b * LANES : (b + 1) * LANES], cosine, sine).astype(BF) * BF(HD ** -0.5)
        qkv_ref[:, b * LANES : (b + 1) * LANES] = block
        q_s[2 * b] = block[:, :HD]
        q_s[2 * b + 1] = block[:, HD:]
    k_cos, k_sin = key_tables(cosine, sine)
    block = turn(p_ref[:, QPK * HD :], k_cos, k_sin)
    qkv_ref[:, QPK * HD :] = block.astype(BF)
    k_s[...] = block[:, :HD].astype(BF)
    vt_s[...] = jnp.transpose(block)[HD:].astype(BF)
    keep = lax.broadcasted_iota(jnp.int32, (tile, tile), 0) <= lax.broadcasted_iota(jnp.int32, (tile, tile), 1)

    def head(n, carry):
        for t in range(length // tile):
            before, here = t * tile, slice(t * tile, (t + 1) * tile)
            q = q_s[n, here, :]
            s_here = jnp.where(keep, mm_nt(k_s[here, :], q), MASKED)
            peak = jnp.max(s_here, axis=0, keepdims=True)
            if t:
                s_before = mm_nt(k_s[:before, :], q)
                peak = jnp.maximum(peak, jnp.max(s_before, axis=0, keepdims=True))
            e_here = jnp.exp(s_here - peak)
            total = jnp.sum(e_here, axis=0, keepdims=True)
            if t:
                e_before = jnp.exp(s_before - peak)
                total = total + jnp.sum(e_before, axis=0, keepdims=True)
            scale = 1.0 / total
            out = mm(vt_s[:, here], (e_here * scale).astype(BF))
            if t:
                out = out + mm(vt_s[:, :before], (e_before * scale).astype(BF))
            c_s[pl.ds(pl.multiple_of(n * HD, HD), HD), here] = out
            log_ref[0, pl.ds(n, 1), here] = peak + jnp.log(total)
        return carry

    lax.fori_loop(0, QPK, head, 0)
    ctx_ref[...] = jnp.transpose(c_s[...]).astype(BF)

def attend(projected, cosine, sine, groups, tile=512):
    length, columns = projected.shape[0], projected.shape[1] // groups
    qw = QPK * HD
    table = pl.BlockSpec((length, LANES), lambda g: (0, 0))
    return pl.pallas_call(
        functools.partial(attend_kernel, tile),
        grid=(groups,),
        in_specs=[pl.BlockSpec((length, columns), lambda g: (0, g)), table, table],
        out_specs=[
            pl.BlockSpec((length, columns), lambda g: (0, g)),
            pl.BlockSpec((length, qw), lambda g: (0, g)),
            pl.BlockSpec((1, QPK, length), lambda g: (g, 0, 0)),
        ],
        out_shape=[
            jax.ShapeDtypeStruct((length, groups * columns), BF),
            jax.ShapeDtypeStruct((length, groups * qw), BF),
            jax.ShapeDtypeStruct((groups, QPK, length), F32),
        ],
        scratch_shapes=[
            pltpu.VMEM((QPK, length, HD), BF),
            pltpu.VMEM((length, HD), BF),
            pltpu.VMEM((HD, length), BF),
            pltpu.VMEM((qw, length), F32),
        ],
        compiler_params=pltpu.CompilerParams(vmem_limit_bytes=VMEM_LIMIT),
        cost_estimate=HEAVY,
        name="attend",
    )(projected, cosine, sine)

def attend_back_kernel(tile, qkv_ref, grad_ref, log_ref, cos_ref, sin_ref, *refs):
    out_ref, q_s, k_s, v_s, kt_s, g_s, dk_s, dv_s, dq_s = refs[-9:]
    length = qkv_ref.shape[0]
    for b in range(QPK // 2):
        lanes = slice(b * LANES, (b + 1) * LANES)
        block, grad = qkv_ref[:, lanes], grad_ref[:, lanes]
        q_s[2 * b], q_s[2 * b + 1] = block[:, :HD], block[:, HD:]
        g_s[2 * b], g_s[2 * b + 1] = grad[:, :HD], grad[:, HD:]
    block = qkv_ref[:, QPK * HD :]
    k_s[...] = block[:, :HD]
    v_s[...] = block[:, HD:]
    kt_s[...] = jnp.transpose(block.astype(F32))[:HD].astype(BF)
    dk_s[...] = jnp.zeros_like(dk_s)
    dv_s[...] = jnp.zeros_like(dv_s)
    keep = lax.broadcasted_iota(jnp.int32, (tile, tile), 0) <= lax.broadcasted_iota(jnp.int32, (tile, tile), 1)

    def head(n, carry):
        for t in range(length // tile):
            before, here = t * tile, slice(t * tile, (t + 1) * tile)
            upto = slice(0, (t + 1) * tile)
            q, g = q_s[n, here, :], g_s[n, here, :]
            log = log_ref[0, pl.ds(n, 1), here]
            a_here = jnp.exp(jnp.where(keep, mm_nt(k_s[here, :], q), MASKED) - log)
            d_here = mm_nt(v_s[here, :], g)
            inner = jnp.sum(a_here * d_here, axis=0, keepdims=True)
            if t:
                a_before = jnp.exp(mm_nt(k_s[:before, :], q) - log)
                d_before = mm_nt(v_s[:before, :], g)
                inner = inner + jnp.sum(a_before * d_before, axis=0, keepdims=True)
            s_here = (a_here * (d_here - inner)).astype(BF)
            dq = mm(kt_s[:, here], s_here)
            dk_s[here, :] += mm(s_here, q)
            dv_s[here, :] += mm(a_here.astype(BF), g)
            if t:
                s_before = (a_before * (d_before - inner)).astype(BF)
                dq = dq + mm(kt_s[:, :before], s_before)
                dk_s[:before, :] += mm(s_before, q)
                dv_s[:before, :] += mm(a_before.astype(BF), g)
            dq_s[pl.ds(pl.multiple_of(n * HD, HD), HD), here] = dq * HD ** -0.5
        return carry

    lax.fori_loop(0, QPK, head, 0)
    cosine, sine = cos_ref[...], sin_ref[...]
    grad = jnp.transpose(dq_s[...])
    for b in range(QPK // 2):
        lanes = slice(b * LANES, (b + 1) * LANES)
        out_ref[:, lanes] = turn(grad[:, lanes], cosine, -sine).astype(BF)
    k_cos, k_sin = key_tables(cosine, sine)
    block = jnp.concatenate([dk_s[...], dv_s[...]], axis=1)
    out_ref[:, QPK * HD :] = turn(block, k_cos, -k_sin).astype(BF)

def attend_back(qkv, grad, log, cosine, sine, groups, group, earlier, tile=512):
    length, columns = qkv.shape[0], qkv.shape[1] // groups
    qw = QPK * HD
    table = pl.BlockSpec((length, LANES), lambda g: (0, 0))
    held = () if earlier is None else (earlier,)
    return pl.pallas_call(
        functools.partial(attend_back_kernel, tile),
        grid=(1,),
        in_specs=[
            pl.BlockSpec((length, columns), lambda g: (0, group)),
            pl.BlockSpec((length, qw), lambda g: (0, group)),
            pl.BlockSpec((1, QPK, length), lambda g: (group, 0, 0)),
            table,
            table,
        ]
        + [pl.BlockSpec(memory_space=pl.ANY)] * len(held),
        out_specs=pl.BlockSpec((length, columns), lambda g: (0, group)),
        out_shape=jax.ShapeDtypeStruct((length, groups * columns), BF),
        scratch_shapes=[
            pltpu.VMEM((QPK, length, HD), BF),
            pltpu.VMEM((length, HD), BF),
            pltpu.VMEM((length, HD), BF),
            pltpu.VMEM((HD, length), BF),
            pltpu.VMEM((QPK, length, HD), BF),
            pltpu.VMEM((length, HD), F32),
            pltpu.VMEM((length, HD), F32),
            pltpu.VMEM((qw, length), F32),
        ],
        input_output_aliases={5: 0} if held else {},
        compiler_params=pltpu.CompilerParams(vmem_limit_bytes=VMEM_LIMIT),
        cost_estimate=HEAVY,
        name="attend_back",
    )(qkv, grad, log, cosine, sine, *held)


def tables(length):
    half = HD // 2
    freq = ROPE_BASE ** (-(jnp.arange(half, dtype=F32) * 2.0 / HD))
    ang = jnp.arange(length).astype(F32)[:, None] * freq[None, :]
    c, s = jnp.cos(ang), jnp.sin(ang)
    return jnp.concatenate([c, c, c, c], 1), jnp.concatenate([-s, s, -s, s], 1)

def by_parts(at_ref, rows_ref, weights):
    depth = weights[0].shape[0]
    total = None
    for k, weight in enumerate(weights):
        rows = rows_ref[:, pl.ds(pl.multiple_of(at_ref[k] * depth, depth), depth)]
        part = mm(rows, weight[...])
        total = part if total is None else total + part
    return total


def gate_kernel(blocks, at_ref, *refs):
    rows_refs, weights, (gate_ref, rows_ref) = refs[:blocks], refs[blocks:-2], refs[-2:]

    @pl.when(pl.program_id(1) == 0)
    def _():
        for t in range(blocks):

            @pl.when(pl.program_id(0) == t)
            def _():
                rows_ref[...] = rows_refs[t][...]

    gate_ref[...] = by_parts(at_ref, rows_ref, weights)


def gate_rows(at, rows, gates, tf=1024):
    tm, k = rows[0].shape
    f = gates[0].shape[1]
    parts, blocks = len(gates), len(rows)
    return pl.pallas_call(
        functools.partial(gate_kernel, blocks),
        grid=(blocks, f // tf),
        in_specs=[pl.BlockSpec(memory_space=pltpu.SMEM)]
        + [pl.BlockSpec((tm, k), lambda i, j: (0, 0), pipeline_mode=pl.Buffered(1))] * blocks
        + [pl.BlockSpec((k // parts, tf), lambda i, j: (0, j))] * parts,
        out_specs=[
            pl.BlockSpec((tm, tf), lambda i, j: (i, j)),
            pl.BlockSpec((tm, k), lambda i, j: (i, 0)),
        ],
        out_shape=[
            jax.ShapeDtypeStruct((tm * blocks, f), F32),
            jax.ShapeDtypeStruct((tm * blocks, k), BF),
        ],
        compiler_params=pltpu.CompilerParams(vmem_limit_bytes=VMEM_LIMIT),
        cost_estimate=HEAVY,
        name="gate_rows",
    )(at, *rows, *gates)


def up_kernel(at_ref, rows_ref, gate_ref, *refs):
    weights, (hid_ref, a_ref, b_ref) = refs[:-3], refs[-3:]
    up = by_parts(at_ref, rows_ref, weights)
    gate = gate_ref[...]
    s = jax.nn.sigmoid(gate)
    act = gate * s
    hid_ref[...] = (act * up).astype(BF)
    a_ref[...] = act
    b_ref[...] = up * s * (1.0 + gate * (1.0 - s))


def up_rows(at, rows, gate, ups, tm=512, tf=1024):
    m, k = rows.shape
    f = gate.shape[1]
    parts = len(ups)
    o = pl.BlockSpec((tm, tf), lambda i, j: (i, j))
    return pl.pallas_call(
        up_kernel,
        grid=(m // tm, f // tf),
        in_specs=[
            pl.BlockSpec(memory_space=pltpu.SMEM),
            pl.BlockSpec((tm, k), lambda i, j: (i, 0)),
            o,
        ]
        + [pl.BlockSpec((k // parts, tf), lambda i, j: (0, j))] * parts,
        out_specs=[o, o, o],
        out_shape=[
            jax.ShapeDtypeStruct((m, f), BF),
            jax.ShapeDtypeStruct((m, f), F32),
            jax.ShapeDtypeStruct((m, f), F32),
        ],
        compiler_params=pltpu.CompilerParams(vmem_limit_bytes=VMEM_LIMIT),
        cost_estimate=HEAVY,
        name="up_rows",
    )(at, rows, gate, *ups)


def ffn_back_kernel(tf, downs, parts, at_ref, dy_ref, a_ref, b_ref, *refs):
    d_refs, weights, (dg_ref, du_ref, dn_ref) = refs[:downs], refs[downs : downs + 2 * parts], refs[-3:]
    dy = dy_ref[...]
    each = d_refs[0].shape[0]
    for j in range(downs * each // tf):
        c = slice(j * tf, (j + 1) * tf)
        row = j * tf % each
        dh = mm_nt(dy, d_refs[j * tf // each][row : row + tf, :])
        dg_ref[:, c] = (dh * b_ref[:, c]).astype(BF)
        du_ref[:, c] = (dh * a_ref[:, c]).astype(BF)
    depth = weights[0].shape[0]
    for k in range(parts):
        part = mm_nt(dg_ref[...], weights[k][...]) + mm_nt(du_ref[...], weights[parts + k][...])
        dn_ref[:, pl.ds(pl.multiple_of(at_ref[k] * depth, depth), depth)] = part.astype(BF)


def ffn_back(at, dy, a, b, downs, gates, ups, part, earlier, tm=256, tf=256):
    m, k = dy.shape
    f = gates[0].shape[1]
    parts = len(gates)
    steps = m // 2 // tm
    inner = pl.BlockSpec((tm, f), lambda i: (i + part * steps, 0))
    rows = pl.BlockSpec((tm, k), lambda i: (i + part * steps, 0))

    def whole(shape):
        return pl.BlockSpec(shape, lambda i: (0, 0), pipeline_mode=pl.Buffered(1))

    held = () if earlier is None else earlier
    return pl.pallas_call(
        functools.partial(ffn_back_kernel, tf, len(downs), parts),
        grid=(steps,),
        in_specs=[pl.BlockSpec(memory_space=pltpu.SMEM), rows, inner, inner]
        + [whole((f // len(downs), k))] * len(downs)
        + [whole((k // parts, f))] * (2 * parts)
        + [pl.BlockSpec(memory_space=pl.ANY)] * len(held),
        out_specs=[inner, inner, pl.BlockSpec((tm, k), lambda i: (i, 0))],
        out_shape=[
            jax.ShapeDtypeStruct((m, f), BF),
            jax.ShapeDtypeStruct((m, f), BF),
            jax.ShapeDtypeStruct((m // 2, k), BF),
        ],
        input_output_aliases={4 + len(downs) + 2 * parts + i: i for i in range(len(held))},
        compiler_params=pltpu.CompilerParams(vmem_limit_bytes=VMEM_LIMIT),
        cost_estimate=HEAVY,
        name="ffn_back",
    )(at, dy, a, b, *downs, *gates, *ups, *held)


def project_kernel(pieces, at_ref, *refs):
    piece_refs, (gain_ref, w_ref, n_ref, p_ref, x_s) = refs[:pieces], refs[pieces:]
    rows = piece_refs[0].shape[1]
    for k in range(pieces):
        x_s[pl.ds(pl.multiple_of(at_ref[k] * rows, rows), rows), :] = piece_refs[k][0]
    x = x_s[...].astype(F32)
    inverse = lax.rsqrt(jnp.mean(x * x, axis=-1, keepdims=True) + NORM_EPSILON)
    n_ref[...] = (x * inverse * gain_ref[...]).astype(BF)
    p_ref[...] = mm(n_ref[...], w_ref[...])


def project(at, pieces, gain, weights):
    b, r, d = pieces[0].shape
    c = weights.shape[1]
    rows = r * len(pieces)
    return pl.pallas_call(
        functools.partial(project_kernel, len(pieces)),
        grid=(b,),
        in_specs=[pl.BlockSpec(memory_space=pltpu.SMEM)]
        + [pl.BlockSpec((1, r, d), lambda i: (i, 0, 0))] * len(pieces)
        + [
            pl.BlockSpec((1, d), lambda i: (0, 0)),
            pl.BlockSpec((d, c), lambda i: (0, 0), pipeline_mode=pl.Buffered(1)),
        ],
        out_specs=[pl.BlockSpec((rows, d), lambda i: (i, 0)), pl.BlockSpec((rows, c), lambda i: (i, 0))],
        out_shape=[jax.ShapeDtypeStruct((b * rows, d), BF), jax.ShapeDtypeStruct((b * rows, c), F32)],
        scratch_shapes=[pltpu.VMEM((rows, d), BF)],
        compiler_params=pltpu.CompilerParams(vmem_limit_bytes=VMEM_LIMIT),
        cost_estimate=LIGHT,
        name="project",
    )(at, *pieces, gain, weights)


def context_kernel(pieces, at_ref, *refs):
    piece_refs, (w_ref, rows_ref, c_ref) = refs[:pieces], refs[pieces:]
    rows = piece_refs[0].shape[1]
    for k in range(pieces):
        rows_ref[pl.ds(pl.multiple_of(at_ref[k] * rows, rows), rows), :] = piece_refs[k][0]
    c_ref[...] = mm_nt(rows_ref[...], w_ref[...]).astype(BF)


def context_grad(at, pieces, weights):
    b, r, d = pieces[0].shape
    c = weights.shape[0]
    rows = r * len(pieces)
    return pl.pallas_call(
        functools.partial(context_kernel, len(pieces)),
        grid=(b,),
        in_specs=[pl.BlockSpec(memory_space=pltpu.SMEM)]
        + [pl.BlockSpec((1, r, d), lambda i: (i, 0, 0))] * len(pieces)
        + [pl.BlockSpec((c, d), lambda i: (0, 0), pipeline_mode=pl.Buffered(1))],
        out_specs=[pl.BlockSpec((rows, d), lambda i: (i, 0)), pl.BlockSpec((rows, c), lambda i: (i, 0))],
        out_shape=[jax.ShapeDtypeStruct((b * rows, d), BF), jax.ShapeDtypeStruct((b * rows, c), BF)],
        compiler_params=pltpu.CompilerParams(vmem_limit_bytes=VMEM_LIMIT),
        cost_estimate=LIGHT,
        name="context_grad",
    )(at, *pieces, weights)


def out_kernel(hid_ref, *refs):
    weights, out_ref = refs[:-1], refs[-1]
    each = weights[0].shape[0]
    total = None
    for k, weight in enumerate(weights):
        part = mm(hid_ref[:, k * each : (k + 1) * each], weight[...])
        total = part if total is None else total + part
    out_ref[...] = total.astype(BF)


def out_rows(hidden, weights, part, tm=256):
    m, f = hidden.shape
    steps = m // 2 // tm
    each, d = weights[0].shape
    return pl.pallas_call(
        out_kernel,
        grid=(steps,),
        in_specs=[pl.BlockSpec((tm, f), lambda i: (i + part * steps, 0))]
        + [pl.BlockSpec((each, d), lambda i: (0, 0), pipeline_mode=pl.Buffered(1))] * len(weights),
        out_specs=pl.BlockSpec((tm, d), lambda i: (i, 0)),
        out_shape=jax.ShapeDtypeStruct((m // 2, d), BF),
        compiler_params=pltpu.CompilerParams(vmem_limit_bytes=VMEM_LIMIT),
        cost_estimate=LIGHT,
        name="out_rows",
    )(hidden, *weights)


def join_kernel(count, *refs):
    rows = refs[0].shape[0]
    for k in range(count):
        refs[count][k * rows : (k + 1) * rows] = refs[k][...]


def join(pieces):
    rows, width = pieces[0].shape
    count = len(pieces)
    tile = width // 4
    return pl.pallas_call(
        functools.partial(join_kernel, count),
        grid=(width // tile,),
        in_specs=[pl.BlockSpec((rows, tile), lambda i: (0, i))] * count,
        out_specs=pl.BlockSpec((rows * count, tile), lambda i: (0, i)),
        out_shape=jax.ShapeDtypeStruct((rows * count, width), pieces[0].dtype),
        compiler_params=pltpu.CompilerParams(vmem_limit_bytes=VMEM_LIMIT),
        name="join",
    )(*pieces)


def collect_kernel(put, parts, at_ref, *refs):
    for k in range(parts):
        put(refs[k], refs[parts], at_ref[k])


def collect(at, pieces, shape, put):
    return pl.pallas_call(
        functools.partial(collect_kernel, put, len(pieces)),
        in_specs=[pl.BlockSpec(memory_space=pltpu.SMEM)]
        + [pl.BlockSpec(memory_space=pltpu.VMEM)] * len(pieces),
        out_specs=pl.BlockSpec(memory_space=pltpu.VMEM),
        out_shape=jax.ShapeDtypeStruct(shape, pieces[0].dtype),
        compiler_params=pltpu.CompilerParams(vmem_limit_bytes=VMEM_LIMIT),
        name="collect",
    )(at, *pieces)


def fence_kernel(x_ref, o_ref):
    o_ref[...] = x_ref[...]


def fence_call(value):
    return pl.pallas_call(
        fence_kernel,
        out_shape=jax.ShapeDtypeStruct(value.shape, value.dtype),
        cost_estimate=HEAVY,
        name="fence",
    )(value)


def adamw(param, grad, first, second, rate, decay):
    first_new = BETA_ONE * first + (1.0 - BETA_ONE) * grad
    second_new = BETA_TWO * second + (1.0 - BETA_TWO) * grad * grad
    first_hat = first_new / (1.0 - BETA_ONE**STEP)
    second_hat = second_new / (1.0 - BETA_TWO**STEP)
    param_new = param - rate * (first_hat / (jnp.sqrt(second_hat) + ADAM_EPSILON) + decay * param)
    return (param_new, first_new, second_new)


class Chain:
    def __init__(self):
        self.token = None
        self.fences = []
        self.begun = []

    def now(self, value):
        return value if self.token is None else after(value, self.token)

    def take(self, value):
        value = self.now(value)
        self.begun.append(value)
        return value

    def start(self, value, axis, mask, name):
        value = self.take(value)
        with jax.named_scope(name):
            return swap(value, axis, mask)

    def start_dp(self, value, name):
        return [self.start(value, "dp", k, name) for k in range(1, lax.axis_size("dp"))]

    def start_all(self, blocks, name):
        blocks = self.take(blocks)
        with jax.named_scope(name):
            return lax.all_to_all(blocks, SP, 0, 0, tiled=True)

    def fence(self, *values):
        self.passed(fence_call(after(jnp.zeros((8, LANES), F32), self.token, *self.fences, *self.begun, *values)
            if self.token is not None else after(jnp.zeros((8, LANES), F32), *self.begun, *values)))
        self.fences = [self.token]

    def passed(self, token):
        self.token = token
        self.begun = []

    def gate(self, value):
        return after(value, self.token, *self.begun)


def order_units(pieces, at, sp):
    _, outer, rows, width = pieces[0].shape
    if rows % 16:
        out = jnp.zeros((outer, len(pieces), sp * rows, width), BF)
        for k, piece in enumerate(pieces):
            piece = piece.transpose(1, 0, 2, 3).reshape(outer, 1, sp * rows, width)
            out = lax.dynamic_update_slice(out, piece, (0, at[k], 0, 0))
        return out.reshape(-1, width)

    def put(piece, out, x):
        for z in range(sp):
            out[:, x, z * rows : (z + 1) * rows] = piece[z]

    return collect(at, pieces, (outer, len(pieces), sp * rows, width), put).reshape(-1, width)


def place(pieces, index):
    out = jnp.zeros((len(pieces),) + pieces[0].shape, pieces[0].dtype)
    for mask, piece in pieces.items():
        out = lax.dynamic_update_index_in_dim(out, piece, index ^ mask, 0)
    return out


class Gather:
    def __init__(self, chain, rows, name):
        self.chain = chain
        self.name = name
        n = rows.shape[0] // 2
        self.a, self.b, self.n = rows[:n], rows[n:], n
        self.a_y = chain.start(self.a, "tp", 2, name)
        self.b_z = chain.start(self.b, SP, 1, name)

    def second(self):
        now, n = self.chain.now, self.n
        self.near = jnp.concatenate([self.a, now(self.a_y), self.b, now(self.b_z)], axis=0)
        self.far_z = self.chain.start(self.near[: 2 * n], SP, 1, self.name)
        self.far_y = self.chain.start(self.near[2 * n :], "tp", 2, self.name)

    def near_core(self):
        self.near_other = self.chain.start(self.near, "tp", 1, self.name)

    def far_core(self):
        now = self.chain.now
        self.far = jnp.concatenate([now(self.far_z), now(self.far_y)], axis=0)
        self.far_other = self.chain.start(self.far, "tp", 1, self.name)

    def result(self):
        now = self.chain.now
        return [self.near, self.far, now(self.near_other), now(self.far_other)]


class Reduce:
    def __init__(self, chain, other, name):
        self.chain = chain
        self.name = name
        self.got = chain.start(other, "tp", 1, name)

    def first(self, mine):
        total = (mine.astype(F32) + self.chain.now(self.got).astype(F32)).astype(BF)
        total = total.reshape(2, 2, 2, -1, total.shape[-1])
        self.a, self.b = (total[0, 0, 0], total[1, 0, 0]), (total[0, 1, 0], total[1, 1, 0])
        self.a_y = self.chain.start(total[:, 0, 1], "tp", 2, self.name)
        self.b_z = self.chain.start(total[:, 1, 1], SP, 1, self.name)

    def second(self):
        a_y, b_z = self.chain.now(self.a_y).astype(F32), self.chain.now(self.b_z).astype(F32)
        self.a_sum = self.a[0].astype(F32) + a_y[0]
        self.b_sum = self.b[0].astype(F32) + b_z[0]
        self.a_z = self.chain.start((self.a[1].astype(F32) + a_y[1]).astype(BF), SP, 1, self.name)
        self.b_y = self.chain.start((self.b[1].astype(F32) + b_z[1]).astype(BF), "tp", 2, self.name)

    def result(self):
        a = self.a_sum + self.chain.now(self.a_z).astype(F32)
        b = self.b_sum + self.chain.now(self.b_y).astype(F32)
        return jnp.concatenate([a, b], axis=0)


def local(
    block_in,
    cotangent,
    qkv_weight,
    proj_weight,
    feed_weight,
    down_weight,
    norm_gains,
    qkv_first,
    proj_first,
    feed_first,
    down_first,
    gains_first,
    qkv_second,
    proj_second,
    feed_second,
    down_second,
    gains_second,
):
    xi, zi, ti = lax.axis_index("dp"), lax.axis_index(SP), lax.axis_index("tp")
    nx, nz = lax.axis_size("dp"), lax.axis_size(SP)
    width = block_in.shape[2]
    span = block_in.shape[1]
    length = span * nz * 4
    groups, row_block, columns = qkv_weight.shape
    proj_rows = proj_weight.shape[1]
    units, unit_rows = down_weight.shape[0], down_weight.shape[1]
    feed_columns = feed_weight.shape[2] // 2

    y, c = ti // 2, ti % 2
    chain = Chain()
    now, start, fence = chain.now, chain.start, chain.fence

    at = jnp.stack([xi ^ k for k in range(nx)])

    at_tp = jnp.stack([ti ^ k for k in range(4)])

    x_rows = chain.start_all(block_in, "x_sp")
    qkv_mine = qkv_weight.transpose(1, 0, 2).reshape(row_block, groups * columns).astype(BF)
    qkv_all = lax.all_gather(qkv_mine, ("dp",) + SP, tiled=True)
    fence(qkv_mine)

    gains_low = now(norm_gains).astype(BF)
    gains_sent = {k: start(gains_low, SP, k, "gains_sp") for k in (1, 2, 3)}
    proj_blocks = now(proj_weight).astype(BF)
    proj_blocks = jnp.tile(proj_blocks[None], (nz, 1, 1, 1))
    fence(proj_blocks)

    gate_blocks = now(feed_weight[0]).astype(BF).reshape(row_block, 2, feed_columns)
    gate_blocks = jnp.tile(gate_blocks.transpose(1, 0, 2), (nz // 2, 1, 1))
    up_blocks = now(feed_weight[1]).astype(BF).reshape(row_block, 2, feed_columns)
    up_blocks = jnp.tile(up_blocks.transpose(1, 0, 2), (nz // 2, 1, 1))
    down_blocks = now(down_weight).astype(BF).reshape(2, units // 2, unit_rows, width)
    down_blocks = jnp.tile(down_blocks, (nz // 2, 1, 1, 1))

    x_rows = now(x_rows)
    x_y, x_c = start(x_rows, "tp", 2, "x_y"), start(x_rows, "tp", 1, "x_c")
    gains_sp = place({0: gains_low, **{k: now(v) for k, v in gains_sent.items()}}, zi)
    gains_dp = chain.start_dp(gains_sp, "gains_dp")
    fence()
    proj_own = chain.start_all(proj_blocks, "proj_sp")
    fence()
    x_y = now(x_y)
    x_yc = start(x_y, "tp", 1, "x_yc")
    fence(gate_blocks, up_blocks, down_blocks)

    gains_all = place({0: gains_sp, **{k + 1: now(v) for k, v in enumerate(gains_dp)}}, xi)
    gain_values = gains_all.transpose(2, 0, 1, 3).reshape(2, width).astype(F32)
    x_yc = now(x_yc)
    proj_own = now(proj_own)
    proj_got = chain.start_dp(proj_own, "proj_dp")
    gate_own = chain.start_all(after(gate_blocks, proj_own), "gate_sp")
    fence(x_yc, gain_values)

    def norm(rows, gain):
        inverse = lax.rsqrt(jnp.mean(rows * rows, axis=-1, keepdims=True) + NORM_EPSILON)
        unit = rows * inverse
        return unit, inverse, (unit * gain).astype(BF)

    normed_one, projected = project(at_tp, [x_rows, now(x_c), x_y, x_yc], gain_values[:1], qkv_all)
    cosine, sine = tables(length)
    qkv, context, logs = attend(chain.gate(projected), cosine, sine, groups)
    chain.passed(context)

    proj_all = order_units([proj_own] + [now(v) for v in proj_got], at, nz)
    attn_part = mm(context, proj_all).astype(BF).reshape(nz, 2, 2, span, width)
    attn_core = start(pick(attn_part, 1 - c, 2), "tp", 1, "attn_c")
    fence()
    attn_sum = (pick(attn_part, c, 2).astype(F32) + now(attn_core).astype(F32)).astype(BF)
    attn_y = start(pick(attn_sum, 1 - y, 1), "tp", 2, "attn_y")
    fence()
    gate_own = now(gate_own)
    gate_got = chain.start_dp(gate_own, "gate_dp")
    up_own = chain.start_all(after(up_blocks, gate_own), "up_sp")
    fence()

    attn_mine = (pick(attn_sum, y, 1).astype(F32) + now(attn_y).astype(F32)).reshape(-1, width)
    inputs = x_rows.astype(F32).reshape(-1, width)
    hidden_one = inputs + attn_mine
    unit_two, inverse_two, normed_two = norm(hidden_one, gain_values[1])
    gather = Gather(chain, normed_two, "normed")
    fence()
    gather.second()
    gather.near_core()
    fence()
    up_own = now(up_own)
    up_got = chain.start_dp(up_own, "up_dp")
    dy_rows = chain.start_all(after(cotangent, up_own), "dy_sp")
    fence()
    gather.far_core()
    gate_got = [chain.take(v) for v in gate_got]
    fence()

    def flat(arrays):
        return [v.reshape(-1, v.shape[-1]) for v in arrays]

    dy_rows = now(dy_rows)
    dy_gather = Gather(chain, dy_rows.reshape(-1, width), "dy")
    fence()
    cut = units // 4
    down_own = [chain.start_all(after(down_blocks[:, :cut], dy_rows), "down_sp")]
    gates = flat([gate_own] + gate_got)
    first, *others = gather.result()
    gate, normed_all = gate_rows(at, [chain.gate(first)] + others, gates)
    chain.passed(gate)

    ups = flat([up_own] + [chain.take(v) for v in up_got])
    down_own[0] = now(down_own[0])
    down_got = [chain.start_dp(down_own[0], "down_dp")]
    down_own.append(chain.start_all(after(down_blocks[:, cut:], down_own[0]), "down_sp"))
    dy_gather.second()
    dy_gather.near_core()
    hidden, activated, slope = up_rows(at, chain.gate(normed_all), gate, ups)
    chain.passed(hidden)

    down_own[1] = now(down_own[1])
    down_got.append(chain.start_dp(down_own[1], "down_dp"))
    dy_gather.far_core()
    fence()
    dy_all = join(dy_gather.result())
    down_part = mm_tn(hidden, dy_all).astype(BF)
    down_part = down_part.reshape(units // 2, nx, nz, unit_rows, width).transpose(1, 2, 0, 3, 4)

    def to_dp(parts, name):
        return [start(pick(parts, xi ^ k, 0), "dp", k, name) for k in range(1, nx)]

    def sum_dp(parts, got):
        total = pick(parts, xi, 0).astype(F32)
        for block in got:
            total = total + now(block).astype(F32)
        return total.astype(BF)

    down_dp = to_dp(down_part, "down_grad_dp")
    fence()
    downs = [
        order_units([own] + [now(v) for v in got], at, nz) for own, got in zip(down_own, down_got)
    ]

    grad_gate, grad_up, grad_other = ffn_back(
        at, chain.gate(dy_all), activated, slope, downs, gates, ups, 1, None
    )
    chain.passed(grad_other)
    reduce = Reduce(chain, grad_other, "normed_grad")
    grad_gate, grad_up, grad_mine = ffn_back(
        at, chain.gate(dy_all), activated, slope, downs, gates, ups, 0, (grad_gate, grad_up)
    )
    chain.passed(grad_mine)

    reduce.first(grad_mine)
    fence()
    down_moved = chain.start_all(sum_dp(down_part, down_dp), "down_grad_sp")
    gate_part = mm_tn(now(normed_all), grad_gate).astype(BF)
    gate_part = gate_part.reshape(nx, nz, row_block, feed_columns)
    gate_dp = to_dp(gate_part, "gate_grad_dp")
    fence()
    reduce.second()
    fence()
    up_part = mm_tn(now(normed_all), grad_up).astype(BF).reshape(nx, nz, row_block, feed_columns)
    up_dp = to_dp(up_part, "up_grad_dp")
    fence()

    grad_normed_two = reduce.result()
    grad_unit = grad_normed_two * gain_values[1]
    row_inner = jnp.mean(grad_unit * unit_two, axis=-1, keepdims=True)
    dy_own = dy_rows.astype(F32).reshape(-1, width)
    back_two = inverse_two * (grad_unit - unit_two * row_inner)
    gain_two_part = jnp.sum(grad_normed_two * unit_two, axis=0)
    grad_hidden_one = dy_own + back_two
    rows_mine = grad_hidden_one.astype(BF).reshape(nz, span, width)
    rows_y, rows_c = start(rows_mine, "tp", 2, "rows_y"), start(rows_mine, "tp", 1, "rows_c")
    fence()
    down_moved = chain.take(down_moved)
    gate_sum = sum_dp(gate_part, gate_dp)
    gate_moved = chain.start_all(after(gate_sum, down_moved), "gate_grad_sp")
    fence()
    out_other = out_rows(now(hidden), downs, 1)
    out_mine = out_rows(now(hidden), downs, 0)
    fence(out_other, out_mine)
    rows_y = now(rows_y)
    rows_yc = start(rows_y, "tp", 1, "rows_yc")
    fence()

    grad_rows, grad_context = context_grad(
        at_tp, [rows_mine, now(rows_c), rows_y, now(rows_yc)], proj_all
    )
    out_reduce = Reduce(chain, out_other, "out")
    fence(grad_context)
    out_reduce.first(out_mine)
    grad_projected = None
    for group in range(groups):
        grad_projected = attend_back(
            qkv, chain.gate(grad_context), logs, cosine, sine, groups, group, grad_projected
        )
        chain.passed(grad_projected)
        if group == 0:
            gate_moved = chain.take(gate_moved)
            up_sum = sum_dp(up_part, up_dp)
            up_moved = chain.start_all(after(up_sum, gate_moved), "up_grad_sp")

    dn_part = mm_nt(now(grad_projected), qkv_all).astype(BF).reshape(nz, 2, 2, span, width)
    dn_core = start(pick(dn_part, 1 - c, 2), "tp", 1, "dn_c")
    fence()
    dn_sum = (pick(dn_part, c, 2).astype(F32) + now(dn_core).astype(F32)).astype(BF)
    dn_y = start(pick(dn_sum, 1 - y, 1), "tp", 2, "dn_y")
    qkv_part = mm_tn(normed_one, now(grad_projected)).astype(BF)
    qkv_grad = lax.psum_scatter(qkv_part, ("dp",) + SP, tiled=True)
    out_reduce.second()
    proj_part = mm_tn(context, now(grad_rows)).astype(BF)
    proj_part = proj_part.reshape(groups, nx, nz, proj_rows, width).transpose(1, 2, 0, 3, 4)
    proj_dp = to_dp(proj_part, "proj_grad_dp")

    grad_normed_one = (pick(dn_sum, y, 1).astype(F32) + now(dn_y).astype(F32)).reshape(-1, width)
    inverse_one = lax.rsqrt(jnp.mean(inputs * inputs, axis=-1, keepdims=True) + NORM_EPSILON)
    unit_one = inputs * inverse_one
    grad_unit = grad_normed_one * gain_values[0]
    row_inner = jnp.mean(grad_unit * unit_one, axis=-1, keepdims=True)
    back_one = inverse_one * (grad_unit - unit_one * row_inner)
    gain_one_part = jnp.sum(grad_normed_one * unit_one, axis=0)
    input_delta = (back_two + back_one).astype(BF).reshape(nz, span, width)
    gains_part = jnp.stack([gain_one_part, gain_two_part])
    gains_c = start(gains_part, "tp", 1, "gains_c")
    fence(input_delta, qkv_part)
    up_moved = chain.take(up_moved)
    input_moved = chain.start_all(after(input_delta, up_moved), "input_sp")
    fence()

    def halves(blocks, axis):
        blocks = [blocks[i].astype(F32) for i in range(nz)]
        parity = [sum(blocks[i] for i in range(p, nz, 2)) for p in range(2)]
        return jnp.concatenate(parity, axis=axis)

    block_delta = (attn_mine + out_reduce.result()).astype(BF).reshape(nz, span, width)
    proj_sum = sum_dp(proj_part, proj_dp)
    gains_part = gains_part + now(gains_c)
    gains_y = start(gains_part, "tp", 2, "gains_y")
    down_grad = halves(now(down_moved), 0)
    down_new, down_first_new, down_second_new = adamw(
        now(down_weight), down_grad, down_first, down_second, DOWN_RATE, WEIGHT_DECAY
    )
    fence(proj_sum, down_new, block_delta)

    input_moved = chain.take(input_moved)
    proj_moved = chain.start_all(after(proj_sum, input_moved), "proj_grad_sp")
    fence()

    gains_part = (gains_part + now(gains_y)).reshape(2, nx, nz, row_block).transpose(1, 2, 0, 3)
    gains_dp = to_dp(gains_part, "gains_dp")
    feed_grad = jnp.stack([halves(now(gate_moved), 1), halves(now(up_moved), 1)])
    feed_new, feed_first_new, feed_second_new = adamw(
        now(feed_weight), feed_grad, feed_first, feed_second, FEED_RATE, WEIGHT_DECAY
    )
    input_grad = now(cotangent).astype(F32) + input_moved.astype(F32)
    fence(feed_new, input_grad)

    proj_moved = chain.take(proj_moved)
    block_moved = chain.start_all(after(block_delta, proj_moved), "block_sp")
    gains_sum = pick(gains_part, xi, 0)
    for block in gains_dp:
        gains_sum = gains_sum + now(block)
    gains_moved = {k: start(pick(gains_sum, zi ^ k, 0), SP, k, "gains_sp") for k in (1, 2, 3)}
    fence()

    proj_grad = sum(now(proj_moved)[i].astype(F32) for i in range(nz))
    qkv_grad = now(qkv_grad).reshape(row_block, groups, columns).transpose(1, 0, 2)
    qkv_grad = after(qkv_grad).astype(F32)
    gains_grad = pick(gains_sum, zi, 0)
    for block in gains_moved.values():
        gains_grad = gains_grad + now(block)
    block_out = block_in.astype(F32) + now(block_moved).astype(F32)

    qkv_new, qkv_first_new, qkv_second_new = adamw(
        qkv_weight, qkv_grad, qkv_first, qkv_second, QKV_RATE, WEIGHT_DECAY
    )
    proj_new, proj_first_new, proj_second_new = adamw(
        proj_weight, proj_grad, proj_first, proj_second, PROJ_RATE, WEIGHT_DECAY
    )
    gains_new, gains_first_new, gains_second_new = adamw(
        norm_gains, gains_grad, gains_first, gains_second, GAIN_RATE, 0.0
    )
    return (
        block_out,
        input_grad,
        qkv_grad,
        proj_grad,
        feed_grad,
        down_grad,
        gains_grad,
        qkv_new,
        proj_new,
        feed_new,
        down_new,
        gains_new,
        qkv_first_new,
        proj_first_new,
        feed_first_new,
        down_first_new,
        gains_first_new,
        qkv_second_new,
        proj_second_new,
        feed_second_new,
        down_second_new,
        gains_second_new,
    )


def solution(mesh):
    sizes = mesh.shape
    mesh = Mesh(
        mesh.devices.reshape(sizes["dp"], sizes["sp"] // 2, 2, sizes["tp"]), ("dp",) + SP + ("tp",)
    )
    rows = P("dp", SP + ("tp",), None)
    heads = P("tp", ("dp",) + SP, None)
    feed = P(None, ("dp",) + SP, "tp")
    gains = P(None, ("dp",) + SP)
    params = (heads, heads, feed, heads, gains)
    return jax.shard_map(
        local,
        mesh=mesh,
        in_specs=(rows, rows) + params * 3,
        out_specs=(rows, rows) + params * 4,
        check_vma=False,
    )
```

```python
import functools

import jax
import jax.numpy as jnp
from jax import lax
from jax.experimental import pallas as pl
from jax.experimental.pallas import tpu as pltpu
from jax.sharding import Mesh, PartitionSpec as P

HD = 64
QPK = 4
STEP = 10
LANES = 128
VMEM_LIMIT = 56 * 1024 * 1024
SP = ("sp_pair", "sp_in_pair")


NORM_EPSILON = 1e-05
ROPE_BASE = 500000.0
MASKED = -1e30
BETA_ONE = 0.9
BETA_TWO = 0.95
ADAM_EPSILON = 1e-08
WEIGHT_DECAY = 0.1
QKV_RATE = 0.05
PROJ_RATE = 0.4
FEED_RATE = 0.05
DOWN_RATE = 0.03
GAIN_RATE = 0.5

BF = jnp.bfloat16
F32 = jnp.float32
HEAVY = pl.CostEstimate(flops=1 << 36, bytes_accessed=1 << 20, transcendentals=0)
LIGHT = pl.CostEstimate(flops=1 << 32, bytes_accessed=1 << 20, transcendentals=0)


def after(value, *earlier):
    return lax.optimization_barrier((value,) + earlier)[0]


def swap(value, axis, mask):
    return lax.ppermute(value, axis, [(i, i ^ mask) for i in range(lax.axis_size(axis))])


def pick(value, index, axis):
    return lax.dynamic_index_in_dim(value, index, axis, keepdims=False)


def dot(left, right, dims):
    return lax.dot_general(left, right, ((dims[0], dims[1]), ((), ())), preferred_element_type=F32)


def mm(left, right):
    return dot(left, right, ((1,), (0,)))


def mm_nt(left, right):
    return dot(left, right, ((1,), (1,)))


def mm_tn(left, right):
    return dot(left, right, ((0,), (0,)))


def turn(block, cosine, sine):
    lane = lax.broadcasted_iota(jnp.int32, block.shape, 1)
    ahead = pltpu.roll(block, LANES - HD // 2, 1)
    behind = pltpu.roll(block, HD // 2, 1)
    return block * cosine + jnp.where(lane % HD < HD // 2, ahead, behind) * sine

def key_tables(cosine, sine):
    lane = lax.broadcasted_iota(jnp.int32, cosine.shape, 1)
    return jnp.where(lane < HD, cosine, 1.0), jnp.where(lane < HD, sine, 0.0)

def attend_kernel(tile, p_ref, cos_ref, sin_ref, qkv_ref, ctx_ref, log_ref, q_s, k_s, vt_s, c_s):
    length = p_ref.shape[0]
    cosine, sine = cos_ref[...], sin_ref[...]
    for b in range(QPK // 2):
        block = turn(p_ref[:, b * LANES : (b + 1) * LANES], cosine, sine).astype(BF) * BF(HD ** -0.5)
        qkv_ref[:, b * LANES : (b + 1) * LANES] = block
        q_s[2 * b] = block[:, :HD]
        q_s[2 * b + 1] = block[:, HD:]
    k_cos, k_sin = key_tables(cosine, sine)
    block = turn(p_ref[:, QPK * HD :], k_cos, k_sin)
    qkv_ref[:, QPK * HD :] = block.astype(BF)
    k_s[...] = block[:, :HD].astype(BF)
    vt_s[...] = jnp.transpose(block)[HD:].astype(BF)
    keep = lax.broadcasted_iota(jnp.int32, (tile, tile), 0) <= lax.broadcasted_iota(jnp.int32, (tile, tile), 1)

    def head(n, carry):
        for t in range(length // tile):
            before, here = t * tile, slice(t * tile, (t + 1) * tile)
            q = q_s[n, here, :]
            s_here = jnp.where(keep, mm_nt(k_s[here, :], q), MASKED)
            peak = jnp.max(s_here, axis=0, keepdims=True)
            if t:
                s_before = mm_nt(k_s[:before, :], q)
                peak = jnp.maximum(peak, jnp.max(s_before, axis=0, keepdims=True))
            e_here = jnp.exp(s_here - peak)
            total = jnp.sum(e_here, axis=0, keepdims=True)
            if t:
                e_before = jnp.exp(s_before - peak)
                total = total + jnp.sum(e_before, axis=0, keepdims=True)
            scale = 1.0 / total
            out = mm(vt_s[:, here], (e_here * scale).astype(BF))
            if t:
                out = out + mm(vt_s[:, :before], (e_before * scale).astype(BF))
            c_s[pl.ds(pl.multiple_of(n * HD, HD), HD), here] = out
            log_ref[0, pl.ds(n, 1), here] = peak + jnp.log(total)
        return carry

    lax.fori_loop(0, QPK, head, 0)
    ctx_ref[...] = jnp.transpose(c_s[...]).astype(BF)

def attend(projected, cosine, sine, groups, tile=512):
    length, columns = projected.shape[0], projected.shape[1] // groups
    qw = QPK * HD
    table = pl.BlockSpec((length, LANES), lambda g: (0, 0))
    return pl.pallas_call(
        functools.partial(attend_kernel, tile),
        grid=(groups,),
        in_specs=[pl.BlockSpec((length, columns), lambda g: (0, g)), table, table],
        out_specs=[
            pl.BlockSpec((length, columns), lambda g: (0, g)),
            pl.BlockSpec((length, qw), lambda g: (0, g)),
            pl.BlockSpec((1, QPK, length), lambda g: (g, 0, 0)),
        ],
        out_shape=[
            jax.ShapeDtypeStruct((length, groups * columns), BF),
            jax.ShapeDtypeStruct((length, groups * qw), BF),
            jax.ShapeDtypeStruct((groups, QPK, length), F32),
        ],
        scratch_shapes=[
            pltpu.VMEM((QPK, length, HD), BF),
            pltpu.VMEM((length, HD), BF),
            pltpu.VMEM((HD, length), BF),
            pltpu.VMEM((qw, length), F32),
        ],
        compiler_params=pltpu.CompilerParams(vmem_limit_bytes=VMEM_LIMIT),
        cost_estimate=HEAVY,
        name="attend",
    )(projected, cosine, sine)

def attend_back_kernel(tile, qkv_ref, grad_ref, log_ref, cos_ref, sin_ref, *refs):
    out_ref, q_s, k_s, v_s, kt_s, g_s, dk_s, dv_s, dq_s = refs[-9:]
    length = qkv_ref.shape[0]
    for b in range(QPK // 2):
        lanes = slice(b * LANES, (b + 1) * LANES)
        block, grad = qkv_ref[:, lanes], grad_ref[:, lanes]
        q_s[2 * b], q_s[2 * b + 1] = block[:, :HD], block[:, HD:]
        g_s[2 * b], g_s[2 * b + 1] = grad[:, :HD], grad[:, HD:]
    block = qkv_ref[:, QPK * HD :]
    k_s[...] = block[:, :HD]
    v_s[...] = block[:, HD:]
    kt_s[...] = jnp.transpose(block.astype(F32))[:HD].astype(BF)
    dk_s[...] = jnp.zeros_like(dk_s)
    dv_s[...] = jnp.zeros_like(dv_s)
    keep = lax.broadcasted_iota(jnp.int32, (tile, tile), 0) <= lax.broadcasted_iota(jnp.int32, (tile, tile), 1)

    def head(n, carry):
        for t in range(length // tile):
            before, here = t * tile, slice(t * tile, (t + 1) * tile)
            upto = slice(0, (t + 1) * tile)
            q, g = q_s[n, here, :], g_s[n, here, :]
            log = log_ref[0, pl.ds(n, 1), here]
            a_here = jnp.exp(jnp.where(keep, mm_nt(k_s[here, :], q), MASKED) - log)
            d_here = mm_nt(v_s[here, :], g)
            inner = jnp.sum(a_here * d_here, axis=0, keepdims=True)
            if t:
                a_before = jnp.exp(mm_nt(k_s[:before, :], q) - log)
                d_before = mm_nt(v_s[:before, :], g)
                inner = inner + jnp.sum(a_before * d_before, axis=0, keepdims=True)
            s_here = (a_here * (d_here - inner)).astype(BF)
            dq = mm(kt_s[:, here], s_here)
            dk_s[here, :] += mm(s_here, q)
            dv_s[here, :] += mm(a_here.astype(BF), g)
            if t:
                s_before = (a_before * (d_before - inner)).astype(BF)
                dq = dq + mm(kt_s[:, :before], s_before)
                dk_s[:before, :] += mm(s_before, q)
                dv_s[:before, :] += mm(a_before.astype(BF), g)
            dq_s[pl.ds(pl.multiple_of(n * HD, HD), HD), here] = dq * HD ** -0.5
        return carry

    lax.fori_loop(0, QPK, head, 0)
    cosine, sine = cos_ref[...], sin_ref[...]
    grad = jnp.transpose(dq_s[...])
    for b in range(QPK // 2):
        lanes = slice(b * LANES, (b + 1) * LANES)
        out_ref[:, lanes] = turn(grad[:, lanes], cosine, -sine).astype(BF)
    k_cos, k_sin = key_tables(cosine, sine)
    block = jnp.concatenate([dk_s[...], dv_s[...]], axis=1)
    out_ref[:, QPK * HD :] = turn(block, k_cos, -k_sin).astype(BF)

def attend_back(qkv, grad, log, cosine, sine, groups, group, earlier, tile=512):
    length, columns = qkv.shape[0], qkv.shape[1] // groups
    qw = QPK * HD
    table = pl.BlockSpec((length, LANES), lambda g: (0, 0))
    held = () if earlier is None else (earlier,)
    return pl.pallas_call(
        functools.partial(attend_back_kernel, tile),
        grid=(1,),
        in_specs=[
            pl.BlockSpec((length, columns), lambda g: (0, group)),
            pl.BlockSpec((length, qw), lambda g: (0, group)),
            pl.BlockSpec((1, QPK, length), lambda g: (group, 0, 0)),
            table,
            table,
        ]
        + [pl.BlockSpec(memory_space=pl.ANY)] * len(held),
        out_specs=pl.BlockSpec((length, columns), lambda g: (0, group)),
        out_shape=jax.ShapeDtypeStruct((length, groups * columns), BF),
        scratch_shapes=[
            pltpu.VMEM((QPK, length, HD), BF),
            pltpu.VMEM((length, HD), BF),
            pltpu.VMEM((length, HD), BF),
            pltpu.VMEM((HD, length), BF),
            pltpu.VMEM((QPK, length, HD), BF),
            pltpu.VMEM((length, HD), F32),
            pltpu.VMEM((length, HD), F32),
            pltpu.VMEM((qw, length), F32),
        ],
        input_output_aliases={5: 0} if held else {},
        compiler_params=pltpu.CompilerParams(vmem_limit_bytes=VMEM_LIMIT),
        cost_estimate=HEAVY,
        name="attend_back",
    )(qkv, grad, log, cosine, sine, *held)


def tables(length):
    half = HD // 2
    freq = ROPE_BASE ** (-(jnp.arange(half, dtype=F32) * 2.0 / HD))
    ang = jnp.arange(length).astype(F32)[:, None] * freq[None, :]
    c, s = jnp.cos(ang), jnp.sin(ang)
    return jnp.concatenate([c, c, c, c], 1), jnp.concatenate([-s, s, -s, s], 1)

def by_parts(at_ref, rows_ref, weights):
    depth = weights[0].shape[0]
    total = None
    for k, weight in enumerate(weights):
        rows = rows_ref[:, pl.ds(pl.multiple_of(at_ref[k] * depth, depth), depth)]
        part = mm(rows, weight[...])
        total = part if total is None else total + part
    return total


def gate_kernel(blocks, at_ref, *refs):
    rows_refs, weights, (gate_ref, rows_ref) = refs[:blocks], refs[blocks:-2], refs[-2:]

    @pl.when(pl.program_id(1) == 0)
    def _():
        for t in range(blocks):

            @pl.when(pl.program_id(0) == t)
            def _():
                rows_ref[...] = rows_refs[t][...]

    gate_ref[...] = by_parts(at_ref, rows_ref, weights)


def gate_rows(at, rows, gates, tf=1024):
    tm, k = rows[0].shape
    f = gates[0].shape[1]
    parts, blocks = len(gates), len(rows)
    return pl.pallas_call(
        functools.partial(gate_kernel, blocks),
        grid=(blocks, f // tf),
        in_specs=[pl.BlockSpec(memory_space=pltpu.SMEM)]
        + [pl.BlockSpec((tm, k), lambda i, j: (0, 0), pipeline_mode=pl.Buffered(1))] * blocks
        + [pl.BlockSpec((k // parts, tf), lambda i, j: (0, j))] * parts,
        out_specs=[
            pl.BlockSpec((tm, tf), lambda i, j: (i, j)),
            pl.BlockSpec((tm, k), lambda i, j: (i, 0)),
        ],
        out_shape=[
            jax.ShapeDtypeStruct((tm * blocks, f), F32),
            jax.ShapeDtypeStruct((tm * blocks, k), BF),
        ],
        compiler_params=pltpu.CompilerParams(vmem_limit_bytes=VMEM_LIMIT),
        cost_estimate=HEAVY,
        name="gate_rows",
    )(at, *rows, *gates)


def up_kernel(at_ref, rows_ref, gate_ref, *refs):
    weights, (hid_ref, a_ref, b_ref) = refs[:-3], refs[-3:]
    up = by_parts(at_ref, rows_ref, weights)
    gate = gate_ref[...]
    s = jax.nn.sigmoid(gate)
    act = gate * s
    hid_ref[...] = (act * up).astype(BF)
    a_ref[...] = act
    b_ref[...] = up * s * (1.0 + gate * (1.0 - s))


def up_rows(at, rows, gate, ups, tm=512, tf=1024):
    m, k = rows.shape
    f = gate.shape[1]
    parts = len(ups)
    o = pl.BlockSpec((tm, tf), lambda i, j: (i, j))
    return pl.pallas_call(
        up_kernel,
        grid=(m // tm, f // tf),
        in_specs=[
            pl.BlockSpec(memory_space=pltpu.SMEM),
            pl.BlockSpec((tm, k), lambda i, j: (i, 0)),
            o,
        ]
        + [pl.BlockSpec((k // parts, tf), lambda i, j: (0, j))] * parts,
        out_specs=[o, o, o],
        out_shape=[
            jax.ShapeDtypeStruct((m, f), BF),
            jax.ShapeDtypeStruct((m, f), F32),
            jax.ShapeDtypeStruct((m, f), F32),
        ],
        compiler_params=pltpu.CompilerParams(vmem_limit_bytes=VMEM_LIMIT),
        cost_estimate=HEAVY,
        name="up_rows",
    )(at, rows, gate, *ups)


def ffn_back_kernel(tf, downs, parts, at_ref, dy_ref, a_ref, b_ref, *refs):
    d_refs, weights, (dg_ref, du_ref, dn_ref) = refs[:downs], refs[downs : downs + 2 * parts], refs[-3:]
    dy = dy_ref[...]
    each = d_refs[0].shape[0]
    for j in range(downs * each // tf):
        c = slice(j * tf, (j + 1) * tf)
        row = j * tf % each
        dh = mm_nt(dy, d_refs[j * tf // each][row : row + tf, :])
        dg_ref[:, c] = (dh * b_ref[:, c]).astype(BF)
        du_ref[:, c] = (dh * a_ref[:, c]).astype(BF)
    depth = weights[0].shape[0]
    for k in range(parts):
        part = mm_nt(dg_ref[...], weights[k][...]) + mm_nt(du_ref[...], weights[parts + k][...])
        dn_ref[:, pl.ds(pl.multiple_of(at_ref[k] * depth, depth), depth)] = part.astype(BF)


def ffn_back(at, dy, a, b, downs, gates, ups, part, earlier, tm=256, tf=256):
    m, k = dy.shape
    f = gates[0].shape[1]
    parts = len(gates)
    steps = m // 2 // tm
    inner = pl.BlockSpec((tm, f), lambda i: (i + part * steps, 0))
    rows = pl.BlockSpec((tm, k), lambda i: (i + part * steps, 0))

    def whole(shape):
        return pl.BlockSpec(shape, lambda i: (0, 0), pipeline_mode=pl.Buffered(1))

    held = () if earlier is None else earlier
    return pl.pallas_call(
        functools.partial(ffn_back_kernel, tf, len(downs), parts),
        grid=(steps,),
        in_specs=[pl.BlockSpec(memory_space=pltpu.SMEM), rows, inner, inner]
        + [whole((f // len(downs), k))] * len(downs)
        + [whole((k // parts, f))] * (2 * parts)
        + [pl.BlockSpec(memory_space=pl.ANY)] * len(held),
        out_specs=[inner, inner, pl.BlockSpec((tm, k), lambda i: (i, 0))],
        out_shape=[
            jax.ShapeDtypeStruct((m, f), BF),
            jax.ShapeDtypeStruct((m, f), BF),
            jax.ShapeDtypeStruct((m // 2, k), BF),
        ],
        input_output_aliases={4 + len(downs) + 2 * parts + i: i for i in range(len(held))},
        compiler_params=pltpu.CompilerParams(vmem_limit_bytes=VMEM_LIMIT),
        cost_estimate=HEAVY,
        name="ffn_back",
    )(at, dy, a, b, *downs, *gates, *ups, *held)


def project_kernel(pieces, at_ref, *refs):
    piece_refs, (gain_ref, w_ref, n_ref, p_ref, x_s) = refs[:pieces], refs[pieces:]
    rows = piece_refs[0].shape[1]
    for k in range(pieces):
        x_s[pl.ds(pl.multiple_of(at_ref[k] * rows, rows), rows), :] = piece_refs[k][0]
    x = x_s[...].astype(F32)
    inverse = lax.rsqrt(jnp.mean(x * x, axis=-1, keepdims=True) + NORM_EPSILON)
    n_ref[...] = (x * inverse * gain_ref[...]).astype(BF)
    p_ref[...] = mm(n_ref[...], w_ref[...])


def project(at, pieces, gain, weights):
    b, r, d = pieces[0].shape
    c = weights.shape[1]
    rows = r * len(pieces)
    return pl.pallas_call(
        functools.partial(project_kernel, len(pieces)),
        grid=(b,),
        in_specs=[pl.BlockSpec(memory_space=pltpu.SMEM)]
        + [pl.BlockSpec((1, r, d), lambda i: (i, 0, 0))] * len(pieces)
        + [
            pl.BlockSpec((1, d), lambda i: (0, 0)),
            pl.BlockSpec((d, c), lambda i: (0, 0), pipeline_mode=pl.Buffered(1)),
        ],
        out_specs=[pl.BlockSpec((rows, d), lambda i: (i, 0)), pl.BlockSpec((rows, c), lambda i: (i, 0))],
        out_shape=[jax.ShapeDtypeStruct((b * rows, d), BF), jax.ShapeDtypeStruct((b * rows, c), F32)],
        scratch_shapes=[pltpu.VMEM((rows, d), BF)],
        compiler_params=pltpu.CompilerParams(vmem_limit_bytes=VMEM_LIMIT),
        cost_estimate=LIGHT,
        name="project",
    )(at, *pieces, gain, weights)


def context_kernel(pieces, at_ref, *refs):
    piece_refs, (w_ref, rows_ref, c_ref) = refs[:pieces], refs[pieces:]
    rows = piece_refs[0].shape[1]
    for k in range(pieces):
        rows_ref[pl.ds(pl.multiple_of(at_ref[k] * rows, rows), rows), :] = piece_refs[k][0]
    c_ref[...] = mm_nt(rows_ref[...], w_ref[...]).astype(BF)


def context_grad(at, pieces, weights):
    b, r, d = pieces[0].shape
    c = weights.shape[0]
    rows = r * len(pieces)
    return pl.pallas_call(
        functools.partial(context_kernel, len(pieces)),
        grid=(b,),
        in_specs=[pl.BlockSpec(memory_space=pltpu.SMEM)]
        + [pl.BlockSpec((1, r, d), lambda i: (i, 0, 0))] * len(pieces)
        + [pl.BlockSpec((c, d), lambda i: (0, 0), pipeline_mode=pl.Buffered(1))],
        out_specs=[pl.BlockSpec((rows, d), lambda i: (i, 0)), pl.BlockSpec((rows, c), lambda i: (i, 0))],
        out_shape=[jax.ShapeDtypeStruct((b * rows, d), BF), jax.ShapeDtypeStruct((b * rows, c), BF)],
        compiler_params=pltpu.CompilerParams(vmem_limit_bytes=VMEM_LIMIT),
        cost_estimate=LIGHT,
        name="context_grad",
    )(at, *pieces, weights)


def out_kernel(hid_ref, *refs):
    weights, out_ref = refs[:-1], refs[-1]
    each = weights[0].shape[0]
    total = None
    for k, weight in enumerate(weights):
        part = mm(hid_ref[:, k * each : (k + 1) * each], weight[...])
        total = part if total is None else total + part
    out_ref[...] = total.astype(BF)


def out_rows(hidden, weights, part, tm=256):
    m, f = hidden.shape
    steps = m // 2 // tm
    each, d = weights[0].shape
    return pl.pallas_call(
        out_kernel,
        grid=(steps,),
        in_specs=[pl.BlockSpec((tm, f), lambda i: (i + part * steps, 0))]
        + [pl.BlockSpec((each, d), lambda i: (0, 0), pipeline_mode=pl.Buffered(1))] * len(weights),
        out_specs=pl.BlockSpec((tm, d), lambda i: (i, 0)),
        out_shape=jax.ShapeDtypeStruct((m // 2, d), BF),
        compiler_params=pltpu.CompilerParams(vmem_limit_bytes=VMEM_LIMIT),
        cost_estimate=LIGHT,
        name="out_rows",
    )(hidden, *weights)


def join_kernel(count, *refs):
    rows = refs[0].shape[0]
    for k in range(count):
        refs[count][k * rows : (k + 1) * rows] = refs[k][...]


def join(pieces):
    rows, width = pieces[0].shape
    count = len(pieces)
    tile = width // 4
    return pl.pallas_call(
        functools.partial(join_kernel, count),
        grid=(width // tile,),
        in_specs=[pl.BlockSpec((rows, tile), lambda i: (0, i))] * count,
        out_specs=pl.BlockSpec((rows * count, tile), lambda i: (0, i)),
        out_shape=jax.ShapeDtypeStruct((rows * count, width), pieces[0].dtype),
        compiler_params=pltpu.CompilerParams(vmem_limit_bytes=VMEM_LIMIT),
        name="join",
    )(*pieces)


def collect_kernel(put, parts, at_ref, *refs):
    for k in range(parts):
        put(refs[k], refs[parts], at_ref[k])


def collect(at, pieces, shape, put):
    return pl.pallas_call(
        functools.partial(collect_kernel, put, len(pieces)),
        in_specs=[pl.BlockSpec(memory_space=pltpu.SMEM)]
        + [pl.BlockSpec(memory_space=pltpu.VMEM)] * len(pieces),
        out_specs=pl.BlockSpec(memory_space=pltpu.VMEM),
        out_shape=jax.ShapeDtypeStruct(shape, pieces[0].dtype),
        compiler_params=pltpu.CompilerParams(vmem_limit_bytes=VMEM_LIMIT),
        name="collect",
    )(at, *pieces)


def fence_kernel(x_ref, o_ref):
    o_ref[...] = x_ref[...]


def fence_call(value):
    return pl.pallas_call(
        fence_kernel,
        out_shape=jax.ShapeDtypeStruct(value.shape, value.dtype),
        cost_estimate=HEAVY,
        name="fence",
    )(value)


def adamw(param, grad, first, second, rate, decay):
    first_new = BETA_ONE * first + (1.0 - BETA_ONE) * grad
    second_new = BETA_TWO * second + (1.0 - BETA_TWO) * grad * grad
    first_hat = first_new / (1.0 - BETA_ONE**STEP)
    second_hat = second_new / (1.0 - BETA_TWO**STEP)
    param_new = param - rate * (first_hat / (jnp.sqrt(second_hat) + ADAM_EPSILON) + decay * param)
    return (param_new, first_new, second_new)


class Chain:
    def __init__(self):
        self.token = None
        self.fences = []
        self.begun = []

    def now(self, value):
        return value if self.token is None else after(value, self.token)

    def take(self, value):
        value = self.now(value)
        self.begun.append(value)
        return value

    def start(self, value, axis, mask, name):
        value = self.take(value)
        with jax.named_scope(name):
            return swap(value, axis, mask)

    def start_dp(self, value, name):
        return [self.start(value, "dp", k, name) for k in range(1, lax.axis_size("dp"))]

    def start_all(self, blocks, name):
        blocks = self.take(blocks)
        with jax.named_scope(name):
            return lax.all_to_all(blocks, SP, 0, 0, tiled=True)

    def fence(self, *values):
        self.passed(fence_call(after(jnp.zeros((8, LANES), F32), self.token, *self.fences, *self.begun, *values)
            if self.token is not None else after(jnp.zeros((8, LANES), F32), *self.begun, *values)))
        self.fences = [self.token]

    def passed(self, token):
        self.token = token
        self.begun = []

    def gate(self, value):
        return after(value, self.token, *self.begun)


def order_units(pieces, at, sp):
    _, outer, rows, width = pieces[0].shape
    if rows % 16:
        out = jnp.zeros((outer, len(pieces), sp * rows, width), BF)
        for k, piece in enumerate(pieces):
            piece = piece.transpose(1, 0, 2, 3).reshape(outer, 1, sp * rows, width)
            out = lax.dynamic_update_slice(out, piece, (0, at[k], 0, 0))
        return out.reshape(-1, width)

    def put(piece, out, x):
        for z in range(sp):
            out[:, x, z * rows : (z + 1) * rows] = piece[z]

    return collect(at, pieces, (outer, len(pieces), sp * rows, width), put).reshape(-1, width)


def place(pieces, index):
    out = jnp.zeros((len(pieces),) + pieces[0].shape, pieces[0].dtype)
    for mask, piece in pieces.items():
        out = lax.dynamic_update_index_in_dim(out, piece, index ^ mask, 0)
    return out


class Gather:
    def __init__(self, chain, rows, name):
        self.chain = chain
        self.name = name
        n = rows.shape[0] // 2
        self.a, self.b, self.n = rows[:n], rows[n:], n
        self.a_y = chain.start(self.a, "tp", 2, name)
        self.b_z = chain.start(self.b, SP, 1, name)

    def second(self):
        now, n = self.chain.now, self.n
        self.near = jnp.concatenate([self.a, now(self.a_y), self.b, now(self.b_z)], axis=0)
        self.far_z = self.chain.start(self.near[: 2 * n], SP, 1, self.name)
        self.far_y = self.chain.start(self.near[2 * n :], "tp", 2, self.name)

    def near_core(self):
        self.near_other = self.chain.start(self.near, "tp", 1, self.name)

    def far_core(self):
        now = self.chain.now
        self.far = jnp.concatenate([now(self.far_z), now(self.far_y)], axis=0)
        self.far_other = self.chain.start(self.far, "tp", 1, self.name)

    def result(self):
        now = self.chain.now
        return [self.near, self.far, now(self.near_other), now(self.far_other)]


class Reduce:
    def __init__(self, chain, other, name):
        self.chain = chain
        self.name = name
        self.got = chain.start(other, "tp", 1, name)

    def first(self, mine):
        total = (mine.astype(F32) + self.chain.now(self.got).astype(F32)).astype(BF)
        total = total.reshape(2, 2, 2, -1, total.shape[-1])
        self.a, self.b = (total[0, 0, 0], total[1, 0, 0]), (total[0, 1, 0], total[1, 1, 0])
        self.a_y = self.chain.start(total[:, 0, 1], "tp", 2, self.name)
        self.b_z = self.chain.start(total[:, 1, 1], SP, 1, self.name)

    def second(self):
        a_y, b_z = self.chain.now(self.a_y).astype(F32), self.chain.now(self.b_z).astype(F32)
        self.a_sum = self.a[0].astype(F32) + a_y[0]
        self.b_sum = self.b[0].astype(F32) + b_z[0]
        self.a_z = self.chain.start((self.a[1].astype(F32) + a_y[1]).astype(BF), SP, 1, self.name)
        self.b_y = self.chain.start((self.b[1].astype(F32) + b_z[1]).astype(BF), "tp", 2, self.name)

    def result(self):
        a = self.a_sum + self.chain.now(self.a_z).astype(F32)
        b = self.b_sum + self.chain.now(self.b_y).astype(F32)
        return jnp.concatenate([a, b], axis=0)


def local(
    block_in,
    cotangent,
    qkv_weight,
    proj_weight,
    feed_weight,
    down_weight,
    norm_gains,
    qkv_first,
    proj_first,
    feed_first,
    down_first,
    gains_first,
    qkv_second,
    proj_second,
    feed_second,
    down_second,
    gains_second,
):
    xi, zi, ti = lax.axis_index("dp"), lax.axis_index(SP), lax.axis_index("tp")
    nx, nz = lax.axis_size("dp"), lax.axis_size(SP)
    width = block_in.shape[2]
    span = block_in.shape[1]
    length = span * nz * 4
    groups, row_block, columns = qkv_weight.shape
    proj_rows = proj_weight.shape[1]
    units, unit_rows = down_weight.shape[0], down_weight.shape[1]
    feed_columns = feed_weight.shape[2] // 2

    y, c = ti // 2, ti % 2
    chain = Chain()
    now, start, fence = chain.now, chain.start, chain.fence

    at = jnp.stack([xi ^ k for k in range(nx)])

    at_tp = jnp.stack([ti ^ k for k in range(4)])

    x_rows = chain.start_all(block_in, "x_sp")
    qkv_mine = qkv_weight.transpose(1, 0, 2).reshape(row_block, groups * columns).astype(BF)
    qkv_all = lax.all_gather(qkv_mine, ("dp",) + SP, tiled=True)
    fence(qkv_mine)

    gains_low = now(norm_gains).astype(BF)
    gains_sent = {k: start(gains_low, SP, k, "gains_sp") for k in (1, 2, 3)}
    proj_blocks = now(proj_weight).astype(BF)
    proj_blocks = jnp.tile(proj_blocks[None], (nz, 1, 1, 1))
    fence(proj_blocks)

    gate_blocks = now(feed_weight[0]).astype(BF).reshape(row_block, 2, feed_columns)
    gate_blocks = jnp.tile(gate_blocks.transpose(1, 0, 2), (nz // 2, 1, 1))
    up_blocks = now(feed_weight[1]).astype(BF).reshape(row_block, 2, feed_columns)
    up_blocks = jnp.tile(up_blocks.transpose(1, 0, 2), (nz // 2, 1, 1))
    down_blocks = now(down_weight).astype(BF).reshape(2, units // 2, unit_rows, width)
    down_blocks = jnp.tile(down_blocks, (nz // 2, 1, 1, 1))

    x_rows = now(x_rows)
    x_y, x_c = start(x_rows, "tp", 2, "x_y"), start(x_rows, "tp", 1, "x_c")
    gains_sp = place({0: gains_low, **{k: now(v) for k, v in gains_sent.items()}}, zi)
    gains_dp = chain.start_dp(gains_sp, "gains_dp")
    fence()
    proj_own = chain.start_all(proj_blocks, "proj_sp")
    fence()
    x_y = now(x_y)
    x_yc = start(x_y, "tp", 1, "x_yc")
    fence(gate_blocks, up_blocks, down_blocks)

    gains_all = place({0: gains_sp, **{k + 1: now(v) for k, v in enumerate(gains_dp)}}, xi)
    gain_values = gains_all.transpose(2, 0, 1, 3).reshape(2, width).astype(F32)
    x_yc = now(x_yc)
    proj_own = now(proj_own)
    proj_got = chain.start_dp(proj_own, "proj_dp")
    gate_own = chain.start_all(after(gate_blocks, proj_own), "gate_sp")
    fence(x_yc, gain_values)

    def norm(rows, gain):
        inverse = lax.rsqrt(jnp.mean(rows * rows, axis=-1, keepdims=True) + NORM_EPSILON)
        unit = rows * inverse
        return unit, inverse, (unit * gain).astype(BF)

    normed_one, projected = project(at_tp, [x_rows, now(x_c), x_y, x_yc], gain_values[:1], qkv_all)
    cosine, sine = tables(length)
    qkv, context, logs = attend(chain.gate(projected), cosine, sine, groups)
    chain.passed(context)

    proj_all = order_units([proj_own] + [now(v) for v in proj_got], at, nz)
    attn_part = mm(context, proj_all).astype(BF).reshape(nz, 2, 2, span, width)
    attn_core = start(pick(attn_part, 1 - c, 2), "tp", 1, "attn_c")
    fence()
    attn_sum = (pick(attn_part, c, 2).astype(F32) + now(attn_core).astype(F32)).astype(BF)
    attn_y = start(pick(attn_sum, 1 - y, 1), "tp", 2, "attn_y")
    fence()
    gate_own = now(gate_own)
    gate_got = chain.start_dp(gate_own, "gate_dp")
    up_own = chain.start_all(after(up_blocks, gate_own), "up_sp")
    fence()

    attn_mine = (pick(attn_sum, y, 1).astype(F32) + now(attn_y).astype(F32)).reshape(-1, width)
    inputs = x_rows.astype(F32).reshape(-1, width)
    hidden_one = inputs + attn_mine
    unit_two, inverse_two, normed_two = norm(hidden_one, gain_values[1])
    gather = Gather(chain, normed_two, "normed")
    fence()
    gather.second()
    gather.near_core()
    fence()
    up_own = now(up_own)
    up_got = chain.start_dp(up_own, "up_dp")
    dy_rows = chain.start_all(after(cotangent, up_own), "dy_sp")
    fence()
    gather.far_core()
    gate_got = [chain.take(v) for v in gate_got]
    fence()

    def flat(arrays):
        return [v.reshape(-1, v.shape[-1]) for v in arrays]

    dy_rows = now(dy_rows)
    dy_gather = Gather(chain, dy_rows.reshape(-1, width), "dy")
    fence()
    cut = units // 4
    down_own = [chain.start_all(after(down_blocks[:, :cut], dy_rows), "down_sp")]
    gates = flat([gate_own] + gate_got)
    first, *others = gather.result()
    gate, normed_all = gate_rows(at, [chain.gate(first)] + others, gates)
    chain.passed(gate)

    ups = flat([up_own] + [chain.take(v) for v in up_got])
    down_own[0] = now(down_own[0])
    down_got = [chain.start_dp(down_own[0], "down_dp")]
    down_own.append(chain.start_all(after(down_blocks[:, cut:], down_own[0]), "down_sp"))
    dy_gather.second()
    dy_gather.near_core()
    hidden, activated, slope = up_rows(at, chain.gate(normed_all), gate, ups)
    chain.passed(hidden)

    down_own[1] = now(down_own[1])
    down_got.append(chain.start_dp(down_own[1], "down_dp"))
    dy_gather.far_core()
    fence()
    dy_all = join(dy_gather.result())
    down_part = mm_tn(hidden, dy_all).astype(BF)
    down_part = down_part.reshape(units // 2, nx, nz, unit_rows, width).transpose(1, 2, 0, 3, 4)

    def to_dp(parts, name):
        return [start(pick(parts, xi ^ k, 0), "dp", k, name) for k in range(1, nx)]

    def sum_dp(parts, got):
        total = pick(parts, xi, 0).astype(F32)
        for block in got:
            total = total + now(block).astype(F32)
        return total.astype(BF)

    down_dp = to_dp(down_part, "down_grad_dp")
    fence()
    downs = [
        order_units([own] + [now(v) for v in got], at, nz) for own, got in zip(down_own, down_got)
    ]

    grad_gate, grad_up, grad_other = ffn_back(
        at, chain.gate(dy_all), activated, slope, downs, gates, ups, 1, None
    )
    chain.passed(grad_other)
    reduce = Reduce(chain, grad_other, "normed_grad")
    grad_gate, grad_up, grad_mine = ffn_back(
        at, chain.gate(dy_all), activated, slope, downs, gates, ups, 0, (grad_gate, grad_up)
    )
    chain.passed(grad_mine)

    reduce.first(grad_mine)
    fence()
    down_moved = chain.start_all(sum_dp(down_part, down_dp), "down_grad_sp")
    gate_part = mm_tn(now(normed_all), grad_gate).astype(BF)
    gate_part = gate_part.reshape(nx, nz, row_block, feed_columns)
    gate_dp = to_dp(gate_part, "gate_grad_dp")
    fence()
    reduce.second()
    fence()
    up_part = mm_tn(now(normed_all), grad_up).astype(BF).reshape(nx, nz, row_block, feed_columns)
    up_dp = to_dp(up_part, "up_grad_dp")
    fence()

    grad_normed_two = reduce.result()
    grad_unit = grad_normed_two * gain_values[1]
    row_inner = jnp.mean(grad_unit * unit_two, axis=-1, keepdims=True)
    dy_own = dy_rows.astype(F32).reshape(-1, width)
    back_two = inverse_two * (grad_unit - unit_two * row_inner)
    gain_two_part = jnp.sum(grad_normed_two * unit_two, axis=0)
    grad_hidden_one = dy_own + back_two
    rows_mine = grad_hidden_one.astype(BF).reshape(nz, span, width)
    rows_y, rows_c = start(rows_mine, "tp", 2, "rows_y"), start(rows_mine, "tp", 1, "rows_c")
    fence()
    down_moved = chain.take(down_moved)
    gate_sum = sum_dp(gate_part, gate_dp)
    gate_moved = chain.start_all(after(gate_sum, down_moved), "gate_grad_sp")
    fence()
    out_other = out_rows(now(hidden), downs, 1)
    out_mine = out_rows(now(hidden), downs, 0)
    fence(out_other, out_mine)
    rows_y = now(rows_y)
    rows_yc = start(rows_y, "tp", 1, "rows_yc")
    fence()

    grad_rows, grad_context = context_grad(
        at_tp, [rows_mine, now(rows_c), rows_y, now(rows_yc)], proj_all
    )
    out_reduce = Reduce(chain, out_other, "out")
    fence(grad_context)
    out_reduce.first(out_mine)
    grad_projected = None
    for group in range(groups):
        grad_projected = attend_back(
            qkv, chain.gate(grad_context), logs, cosine, sine, groups, group, grad_projected
        )
        chain.passed(grad_projected)
        if group == 0:
            gate_moved = chain.take(gate_moved)
            up_sum = sum_dp(up_part, up_dp)
            up_moved = chain.start_all(after(up_sum, gate_moved), "up_grad_sp")
            proj_part = mm_tn(context, now(grad_rows)).astype(BF)
            proj_part = proj_part.reshape(groups, nx, nz, proj_rows, width).transpose(1, 2, 0, 3, 4)
            proj_dp = to_dp(proj_part, "proj_grad_dp")

    dn_part = mm_nt(now(grad_projected), qkv_all).astype(BF).reshape(nz, 2, 2, span, width)
    dn_core = start(pick(dn_part, 1 - c, 2), "tp", 1, "dn_c")
    fence()
    dn_sum = (pick(dn_part, c, 2).astype(F32) + now(dn_core).astype(F32)).astype(BF)
    dn_y = start(pick(dn_sum, 1 - y, 1), "tp", 2, "dn_y")
    qkv_part = mm_tn(normed_one, now(grad_projected)).astype(BF)
    qkv_grad = lax.psum_scatter(qkv_part, ("dp",) + SP, tiled=True)
    out_reduce.second()
    proj_sum = sum_dp(proj_part, proj_dp)
    proj_moved = chain.start_all(after(proj_sum, chain.take(up_moved)), "proj_grad_sp")

    grad_normed_one = (pick(dn_sum, y, 1).astype(F32) + now(dn_y).astype(F32)).reshape(-1, width)
    inverse_one = lax.rsqrt(jnp.mean(inputs * inputs, axis=-1, keepdims=True) + NORM_EPSILON)
    unit_one = inputs * inverse_one
    grad_unit = grad_normed_one * gain_values[0]
    row_inner = jnp.mean(grad_unit * unit_one, axis=-1, keepdims=True)
    back_one = inverse_one * (grad_unit - unit_one * row_inner)
    gain_one_part = jnp.sum(grad_normed_one * unit_one, axis=0)
    input_delta = (back_two + back_one).astype(BF).reshape(nz, span, width)
    gains_part = jnp.stack([gain_one_part, gain_two_part])
    gains_c = start(gains_part, "tp", 1, "gains_c")
    fence(input_delta, qkv_part)
    proj_moved = chain.take(proj_moved)
    input_moved = chain.start_all(after(input_delta, proj_moved), "input_sp")
    fence()

    def halves(blocks, axis):
        blocks = [blocks[i].astype(F32) for i in range(nz)]
        parity = [sum(blocks[i] for i in range(p, nz, 2)) for p in range(2)]
        return jnp.concatenate(parity, axis=axis)

    block_delta = (attn_mine + out_reduce.result()).astype(BF).reshape(nz, span, width)
    gains_part = gains_part + now(gains_c)
    gains_y = start(gains_part, "tp", 2, "gains_y")
    down_grad = halves(now(down_moved), 0)
    down_new, down_first_new, down_second_new = adamw(
        now(down_weight), down_grad, down_first, down_second, DOWN_RATE, WEIGHT_DECAY
    )
    fence(down_new, block_delta)

    input_moved = chain.take(input_moved)
    block_moved = chain.start_all(after(block_delta, input_moved), "block_sp")
    fence()

    gains_part = (gains_part + now(gains_y)).reshape(2, nx, nz, row_block).transpose(1, 2, 0, 3)
    gains_dp = to_dp(gains_part, "gains_dp")
    feed_grad = jnp.stack([halves(now(gate_moved), 1), halves(now(up_moved), 1)])
    feed_new, feed_first_new, feed_second_new = adamw(
        now(feed_weight), feed_grad, feed_first, feed_second, FEED_RATE, WEIGHT_DECAY
    )
    input_grad = now(cotangent).astype(F32) + input_moved.astype(F32)
    fence(feed_new, input_grad)

    gains_sum = pick(gains_part, xi, 0)
    for block in gains_dp:
        gains_sum = gains_sum + now(block)
    gains_moved = {k: start(pick(gains_sum, zi ^ k, 0), SP, k, "gains_sp") for k in (1, 2, 3)}
    fence()

    proj_grad = sum(now(proj_moved)[i].astype(F32) for i in range(nz))
    qkv_grad = now(qkv_grad).reshape(row_block, groups, columns).transpose(1, 0, 2)
    qkv_grad = after(qkv_grad).astype(F32)
    gains_grad = pick(gains_sum, zi, 0)
    for block in gains_moved.values():
        gains_grad = gains_grad + now(block)
    block_out = block_in.astype(F32) + now(block_moved).astype(F32)

    qkv_new, qkv_first_new, qkv_second_new = adamw(
        qkv_weight, qkv_grad, qkv_first, qkv_second, QKV_RATE, WEIGHT_DECAY
    )
    proj_new, proj_first_new, proj_second_new = adamw(
        proj_weight, proj_grad, proj_first, proj_second, PROJ_RATE, WEIGHT_DECAY
    )
    gains_new, gains_first_new, gains_second_new = adamw(
        norm_gains, gains_grad, gains_first, gains_second, GAIN_RATE, 0.0
    )
    return (
        block_out,
        input_grad,
        qkv_grad,
        proj_grad,
        feed_grad,
        down_grad,
        gains_grad,
        qkv_new,
        proj_new,
        feed_new,
        down_new,
        gains_new,
        qkv_first_new,
        proj_first_new,
        feed_first_new,
        down_first_new,
        gains_first_new,
        qkv_second_new,
        proj_second_new,
        feed_second_new,
        down_second_new,
        gains_second_new,
    )


def solution(mesh):
    sizes = mesh.shape
    mesh = Mesh(
        mesh.devices.reshape(sizes["dp"], sizes["sp"] // 2, 2, sizes["tp"]), ("dp",) + SP + ("tp",)
    )
    rows = P("dp", SP + ("tp",), None)
    heads = P("tp", ("dp",) + SP, None)
    feed = P(None, ("dp",) + SP, "tp")
    gains = P(None, ("dp",) + SP)
    params = (heads, heads, feed, heads, gains)
    return jax.shard_map(
        local,
        mesh=mesh,
        in_specs=(rows, rows) + params * 3,
        out_specs=(rows, rows) + params * 4,
        check_vma=False,
    )
```
